32 devices in a mesh: rep: 4 (over x, core), fsdp: 8 (over z, y).
Axes of the slice: x: 2, y: 2, z: 4, core: 2. Of those that a mesh axis runs over, the one named last changes fastest.
Arguments:
- tokens: bfloat16 [4096, 2048], P(('rep', 'fsdp')), may hold values from -6 to 6
- w_query: bfloat16 [2048, 2048], P('fsdp'), may hold values from -0.125 to 0.125
- w_key: bfloat16 [2048, 2048], P('fsdp'), may hold values from -0.125 to 0.125
- w_value: bfloat16 [2048, 4096], P('fsdp'), may hold values from -0.125 to 0.125
- w_gate: bfloat16 [2048, 4096], P('fsdp'), may hold values from -0.125 to 0.125
- w_out: bfloat16 [4096, 2048], P('fsdp'), may hold values from -0.09375 to 0.09375
- norm1_gain: bfloat16 [2048], P('fsdp'), may hold values from 0.5 to 1.5
- norm1_bias: bfloat16 [2048], P('fsdp'), may hold values from -3 to 3
- w_ffn_gate: bfloat16 [2048, 4096], P('fsdp'), may hold values from -0.125 to 0.125
- w_ffn_up: bfloat16 [2048, 4096], P('fsdp'), may hold values from -0.125 to 0.125
- w_ffn_down: bfloat16 [4096, 2048], P('fsdp'), may hold values from -0.09375 to 0.09375
- norm2_gain: bfloat16 [2048], P('fsdp'), may hold values from 0.5 to 1.5
- norm2_bias: bfloat16 [2048], P('fsdp'), may hold values from -3 to 3
- cotangent: bfloat16 [4096, 2048], P(('rep', 'fsdp')), may hold values from -6 to 6
Outputs:
- output: bfloat16 [4096, 2048], P(('rep', 'fsdp'))
- grad_tokens: float32 [4096, 2048], P(('rep', 'fsdp'))
- grad_w_query: float32 [2048, 2048], P('fsdp')
- grad_w_key: float32 [2048, 2048], P('fsdp')
- grad_w_value: float32 [2048, 4096], P('fsdp')
- grad_w_gate: float32 [2048, 4096], P('fsdp')
- grad_w_out: float32 [4096, 2048], P('fsdp')
- grad_norm1_gain: float32 [2048], P('fsdp')
- grad_norm1_bias: float32 [2048], P('fsdp')
- grad_w_ffn_gate: float32 [2048, 4096], P('fsdp')
- grad_w_ffn_up: float32 [2048, 4096], P('fsdp')
- grad_w_ffn_down: float32 [4096, 2048], P('fsdp')
- grad_norm2_gain: float32 [2048], P('fsdp')
- grad_norm2_bias: float32 [2048], P('fsdp')
The draws below stay inside these ranges and needn't reach their ends.
All inputs are finite; a program needn't handle non-finite values.
Results may differ from the reference program's by a relative error of at most 0.02.
Values may be sent and summed in bfloat16 or wider, within the bound.
No kernel may reach another device: no remote copies, remote signals or barrier semaphores. Data moves between devices by JAX's collectives and lax.ppermute only.
A program may use at most 576 MiB of HBM per device.

```python
import math
import jax
import jax.numpy as jnp
from jax import lax

D = 2048
HEADS = 8
FF = 4096
DK = 256
VD = 4096
DV = 512
SEQ = 1024
TOKENS = 4096


def level_of(rng, dims, shards, low, largest):
    def one(dim, blocks):
        heights = jax.random.uniform(jax.random.fold_in(jax.random.fold_in(rng, 6), dim), (blocks,), jnp.float32, low / len(shards), largest / len(shards))
        return jnp.repeat(jnp.exp(heights), dims[dim] // blocks).reshape((-1,) + (1,) * (len(dims) - dim - 1))

    level = one(*shards[0])
    for cut in shards[1:]:
        level = level * one(*cut)
    return level


def bell_draw(key, extent, width, most, cuts=(), kind=jnp.bfloat16):
    values = width * jax.random.normal(key, extent, jnp.float32)
    if cuts:
        values = values * level_of(key, extent, cuts, -0.22, 0.18)
    return jnp.clip(values, -most, most).astype(kind)


def setup_inputs(seed: int = 0) -> dict:
    arg_keys = jax.random.split(jax.random.key(seed), 15)
    return {
        "tokens": bell_draw(arg_keys[0], (TOKENS, D), 1.0, 6.0, ((0, 32),)),
        "w_query": bell_draw(arg_keys[1], (D, D), D ** -0.5, 0.125, ((0, 8),)),
        "w_key": bell_draw(arg_keys[2], (D, D), D ** -0.5, 0.125, ((0, 8),)),
        "w_value": bell_draw(arg_keys[3], (D, VD), D ** -0.5, 0.125, ((0, 8),)),
        "w_gate": bell_draw(arg_keys[4], (D, VD), D ** -0.5, 0.125, ((0, 8),)),
        "w_out": bell_draw(arg_keys[5], (VD, D), VD ** -0.5, 0.09375, ((0, 8),)),
        "norm1_gain": jnp.clip(1.0 + 0.1 * jax.random.normal(arg_keys[6], (D,), jnp.float32), 0.5, 1.5).astype(jnp.bfloat16),
        "norm1_bias": bell_draw(arg_keys[7], (D,), 0.5, 3.0, ((0, 8),)),
        "w_ffn_gate": bell_draw(arg_keys[8], (D, FF), D ** -0.5, 0.125, ((0, 8),)),
        "w_ffn_up": bell_draw(arg_keys[9], (D, FF), D ** -0.5, 0.125, ((0, 8),)),
        "w_ffn_down": bell_draw(arg_keys[10], (FF, D), FF ** -0.5, 0.09375, ((0, 8),)),
        "norm2_gain": jnp.clip(1.0 + 0.1 * jax.random.normal(arg_keys[11], (D,), jnp.float32), 0.5, 1.5).astype(jnp.bfloat16),
        "norm2_bias": bell_draw(arg_keys[12], (D,), 0.5, 3.0, ((0, 8),)),
        "cotangent": bell_draw(arg_keys[13], (TOKENS, D), 1.0, 6.0, ((0, 32),)),
    }


@jax.custom_vjp
def low(v):
    return lax.optimization_barrier(v.astype(jnp.bfloat16)).astype(jnp.float32)

@jax.custom_vjp
def low_back(v):
    return v

def low_keep(v):
    return (low(v), None)

def low_pass(kept, grad):
    return (grad,)

def back_keep(v):
    return (v, None)

def back_low(kept, grad):
    return (low(grad),)
low.defvjp(low_keep, low_pass)
low_back.defvjp(back_keep, back_low)
epsilon = 1e-05
head_epsilon = 1.0
highest = lax.Precision.HIGHEST

def normalize(values):
    center = values - lax.optimization_barrier(jnp.mean(values, axis=-1, keepdims=True))
    spread = lax.optimization_barrier(jnp.mean(center * center, axis=-1, keepdims=True))
    return center * lax.rsqrt(spread + epsilon)

def head_norm(values):
    center = values - lax.optimization_barrier(jnp.mean(values, axis=-1, keepdims=True))
    spread = lax.optimization_barrier(jnp.mean(center * center, axis=-1, keepdims=True))
    return center * lax.rsqrt(spread + head_epsilon)

def layer_norm(values, gain, shift):
    return normalize(values) * gain + shift

def rotate(tensor, positions):
    half = tensor.shape[-1] // 2
    kind = tensor.dtype
    freqs = jnp.exp(-jnp.arange(half).astype(kind) * (math.log(10000.0) / half))
    angles = positions.astype(kind)[:, None] * freqs[None, :]
    cosine = jnp.cos(angles)[:, None, :]
    sine = jnp.sin(angles)[:, None, :]
    first = tensor[..., :half]
    second = tensor[..., half:]
    return jnp.concatenate([first * cosine - second * sine, second * cosine + first * sine], axis=-1)

def decay_tables(heads, length, kind):
    logs = jnp.log(1.0 - 2.0 ** (-5.0 - jnp.arange(heads).astype(kind)))
    index = jnp.arange(length).astype(kind)
    differ = index[:, None] - index[None, :]
    mask = jnp.where(differ[None] >= 0, jnp.exp(jnp.maximum(differ, 0.0)[None] * logs[:, None, None]), jnp.zeros((), kind))
    query_decay = jnp.exp((index[None, :] + 1.0) * logs[:, None])
    key_decay = jnp.exp((length - 1.0 - index[None, :]) * logs[:, None])
    block_decay = jnp.exp(length * logs)
    return (mask, query_decay, key_decay, block_decay)

def retention(queries, key_rows, value_rows):
    seq_count = TOKENS // SEQ
    block_len = math.gcd(SEQ, 256)
    block_count = SEQ // block_len
    kind = queries.dtype
    mask, query_decay, key_decay, block_decay = decay_tables(HEADS, block_len, kind)

    def arrange(tensor):
        shaped = tensor.reshape(seq_count, block_count, block_len, HEADS, tensor.shape[-1])
        return jnp.moveaxis(shaped, 1, 0)

    def advance(state_now, inputs_now):
        query_blk, key_blk, value_blk = inputs_now
        scores = jnp.einsum('sihd,sjhd->shij', query_blk, key_blk, precision=highest) * mask[None]
        intra = jnp.einsum('shij,sjhe->sihe', scores, value_blk, precision=highest)
        decayed = query_blk * query_decay.T[None, :, :, None]
        inter = jnp.einsum('sihd,shde->sihe', decayed, state_now, precision=highest)
        weighted = key_blk * key_decay.T[None, :, :, None]
        state_next = state_now * block_decay[None, :, None, None] + jnp.einsum('sjhd,sjhe->shde', weighted, value_blk, precision=highest)
        return (state_next.astype(kind), (intra + inter).astype(kind))
    initial = jnp.zeros((seq_count, HEADS, DK, DV), kind)
    _, outputs = lax.scan(jax.checkpoint(advance), initial, (arrange(queries), arrange(key_rows), arrange(value_rows)))
    return jnp.moveaxis(outputs, 0, 1).reshape(TOKENS, HEADS, DV)

def forward(inputs, w_query, w_key, w_value, w_gate, w_out, gain_first, bias_first, w_ffn_gate, w_ffn_up, w_ffn_down, gain_second, bias_second):
    z_first = low(layer_norm(inputs, gain_first, bias_first))
    query_pre = low_back(jnp.dot(z_first, w_query, precision=highest, preferred_element_type=jnp.float32))
    key_pre = low_back(jnp.dot(z_first, w_key, precision=highest, preferred_element_type=jnp.float32))
    value_low = low_back(low(jnp.dot(z_first, w_value, precision=highest, preferred_element_type=jnp.float32)))
    gate_pre = low_back(jnp.dot(z_first, w_gate, precision=highest, preferred_element_type=jnp.float32))
    positions = (jnp.arange(TOKENS, dtype=jnp.int32) % SEQ).astype(inputs.dtype)
    query_low = low(rotate(query_pre.reshape(TOKENS, HEADS, DK), positions))
    key_low = low(rotate(key_pre.reshape(TOKENS, HEADS, DK), positions) * DK ** (-0.5))
    retained = retention(query_low, key_low, value_low.reshape(TOKENS, HEADS, DV))
    mixed = low_back(low(head_norm(retained).reshape(TOKENS, VD) * jax.nn.silu(gate_pre)))
    resid = inputs + low_back(jnp.dot(mixed, w_out, precision=highest, preferred_element_type=jnp.float32))
    z_second = low(layer_norm(resid, gain_second, bias_second))
    gate_ffn = low_back(jnp.dot(z_second, w_ffn_gate, precision=highest, preferred_element_type=jnp.float32))
    up_ffn = low_back(jnp.dot(z_second, w_ffn_up, precision=highest, preferred_element_type=jnp.float32))
    hidden = low_back(low(jax.nn.gelu(gate_ffn, approximate=False) * up_ffn))
    return resid + low_back(jnp.dot(hidden, w_ffn_down, precision=highest, preferred_element_type=jnp.float32))

def reference(tokens, w_query, w_key, w_value, w_gate, w_out, norm1_gain, norm1_bias, w_ffn_gate, w_ffn_up, w_ffn_down, norm2_gain, norm2_bias, cotangent):
    params = (w_query, w_key, w_value, w_gate, w_out, norm1_gain, norm1_bias, w_ffn_gate, w_ffn_up, w_ffn_down, norm2_gain, norm2_bias)
    params = tuple((param.astype(jnp.float32) for param in params))
    result, pull = jax.vjp(forward, tokens.astype(jnp.float32), *params)
    grads = pull(cotangent.astype(jnp.float32))
    return (result.astype(jnp.bfloat16), grads[0], grads[1], grads[2], grads[3], grads[4], grads[5], grads[6], grads[7], grads[8], grads[9], grads[10], grads[11], grads[12])
```

```python
import math

import jax
import jax.numpy as jnp
from jax import lax
from jax.sharding import PartitionSpec as P

HEADS = 8
epsilon = 1e-05
head_epsilon = 1.0
f32 = jnp.float32
bf16 = jnp.bfloat16


def dot(a, b, ca=1, cb=0, kind=f32):
    return lax.dot_general(a, b, (((ca,), (cb,)), ((), ())), preferred_element_type=kind)


class Ring:
    def __init__(self, axis):
        self.axis = axis
        self.n = n = lax.axis_size(axis)
        self.order = list(range(0, n, 2)) + list(range(n - 1, 0, -2))
        place = [0] * n
        for i, device in enumerate(self.order):
            place[device] = i
        self.place = jnp.array(place, jnp.int32)[lax.axis_index(axis)]
        self.forward = [(self.order[i], self.order[(i + 1) % n]) for i in range(n)]
        self.backward = [(b, a) for a, b in self.forward]
        self.half = n // 2
        self.offsets = [0]
        for s in range(1, self.half):
            self.offsets += [-s, s]
        self.offsets.append(self.half)

    def send(self, value, forward):
        return lax.ppermute(value, self.axis, self.forward if forward else self.backward)

    def owners(self):
        places = (self.place + jnp.array(self.offsets, jnp.int32)) % self.n
        return jnp.array(self.order, jnp.int32)[places]

    def gather(self, block):
        rows = block.shape[0] // 2
        blocks = [block]
        ahead = behind = block
        for _ in range(1, self.half):
            ahead = self.send(ahead, True)
            behind = self.send(behind, False)
            blocks += [ahead, behind]
        blocks.append(
            jnp.concatenate([self.send(ahead[:rows], True), self.send(behind[rows:], False)])
        )
        return blocks

    def scatter(self, parts):
        term = dict(zip(self.offsets, parts))
        rows = parts[0].shape[0] // 2
        far = term[self.half]
        ahead = self.send(far[:rows].astype(bf16), True).astype(f32)
        behind = self.send(far[rows:].astype(bf16), False).astype(f32)
        nothing = jnp.zeros_like(ahead)
        ahead = jnp.concatenate([ahead, nothing])
        behind = jnp.concatenate([nothing, behind])
        for s in range(self.half - 1, 0, -1):
            ahead = self.send((term[s] + ahead).astype(bf16), True).astype(f32)
            behind = self.send((term[-s] + behind).astype(bf16), False).astype(f32)
        return term[0] + ahead + behind


class Cube:
    def __init__(self, axis):
        self.axis = axis
        self.n = lax.axis_size(axis)
        self.bits = self.n.bit_length() - 1
        self.index = lax.axis_index(axis)

    def swap(self, value, bit):
        return lax.ppermute(value, self.axis, [(i, i ^ (1 << bit)) for i in range(self.n)])

    def mine(self, bit):
        return (self.index >> bit) & 1

    def gather(self, value, dim):
        for bit in reversed(range(self.bits)):
            other = self.swap(value, bit)
            low = self.mine(bit) == 0
            shape = list(value.shape)
            first = jnp.where(low, value, other)
            second = jnp.where(low, other, value)
            value = jnp.stack([first, second], dim + 1)
            shape[dim] *= 2
            value = value.reshape(shape)
        return value

    def scatter(self, value, dim):
        for bit in range(self.bits):
            shape = list(value.shape)
            value = value.reshape(shape[:dim] + [shape[dim] // 2, 2] + shape[dim + 1 :])
            mine = self.mine(bit)
            given = lax.dynamic_index_in_dim(value, 1 - mine, dim + 1, False).astype(bf16)
            kept = lax.dynamic_index_in_dim(value, mine, dim + 1, False)
            value = kept + self.swap(given, bit).astype(f32)
        return value


def normalize(values):
    center = values - jnp.mean(values, axis=-1, keepdims=True)
    spread = jnp.mean(center * center, axis=-1, keepdims=True)
    return center * lax.rsqrt(spread + epsilon)


def layer_norm(values, gain, shift):
    return normalize(values) * gain + shift


def head_norm(values):
    center = values - jnp.mean(values, axis=-1, keepdims=True)
    spread = jnp.mean(center * center, axis=-1, keepdims=True)
    return center * lax.rsqrt(spread + head_epsilon)


def turn(values, cosine, sine):
    half = values.shape[-1] // 2
    first, second = values[:, :half], values[:, half:]
    return jnp.concatenate([first * cosine - second * sine, second * cosine + first * sine], -1)


def turn_back(values, cosine, sine):
    return turn(values, cosine, -sine)


def on_device(
    tokens,
    w_query,
    w_key,
    w_value,
    w_gate,
    w_out,
    norm1_gain,
    norm1_bias,
    w_ffn_gate,
    w_ffn_up,
    w_ffn_down,
    norm2_gain,
    norm2_bias,
    cotangent,
):
    ring = Ring("fsdp")
    cube = Cube("rep")
    n = ring.n
    assert n == HEADS
    rows, width = tokens.shape
    depth = w_query.shape[0]
    part = depth // cube.n

    def columns_of(*weights):
        mine = [
            lax.dynamic_slice_in_dim(w, cube.index * part, part, 0)
            .reshape(part, n, w.shape[1] // n)
            .transpose(1, 0, 2)
            for w in weights
        ]
        sent = jnp.concatenate(mine, -1)
        got = lax.all_to_all(sent, "fsdp", 0, 0, tiled=True)
        whole = cube.gather(got[:, None], 1)
        return whole.reshape(n * depth, whole.shape[-1])

    def rows_of(grad):
        value = grad.reshape(n, cube.n, part, grad.shape[-1])
        value = cube.scatter(value, 1)[:, 0].astype(bf16)
        value = lax.all_to_all(value, "fsdp", 0, 0, tiled=True)
        value = cube.gather(value[:, None], 1)
        return value.reshape(n, depth, grad.shape[-1]).transpose(1, 0, 2).astype(f32)

    def own_rows(grad):
        value = grad.reshape(cube.n, grad.shape[0] // cube.n, grad.shape[1])
        value = cube.gather(cube.scatter(value, 0).astype(bf16), 0)
        return value.reshape(grad.shape).astype(f32)

    gains = jnp.stack([norm1_gain, norm1_bias, norm2_gain, norm2_bias])
    gains = lax.all_gather(gains, "fsdp", axis=1, tiled=True).astype(f32)
    x_all = jnp.concatenate(ring.gather(tokens))
    w_mix = columns_of(w_query, w_key, w_value, w_gate)
    dk = w_query.shape[1] // n
    dv = w_value.shape[1] // n
    ff = w_ffn_gate.shape[1] // n
    cot_all = jnp.concatenate(ring.gather(cotangent))
    w_ffn = columns_of(w_ffn_gate, w_ffn_up)

    head = lax.axis_index("fsdp")
    gamma_log = jnp.log(1.0 - 2.0 ** (-5.0 - head.astype(f32)))
    positions = (
        (ring.owners() * rows)[:, None] + jnp.arange(rows, dtype=jnp.int32)[None, :]
    ).reshape(-1).astype(f32)
    half = dk // 2
    freqs = jnp.exp(-jnp.arange(half, dtype=f32) * (math.log(10000.0) / half))
    angles = positions[:, None] * freqs[None, :]
    cosine, sine = jnp.cos(angles), jnp.sin(angles)
    differ = positions[:, None] - positions[None, :]
    decay = jnp.where(differ >= 0, jnp.exp(jnp.maximum(differ, 0.0) * gamma_log), 0.0)
    key_scale = dk ** (-0.5)

    z_first = layer_norm(x_all.astype(f32), gains[0], gains[1]).astype(bf16)
    pre = dot(z_first, w_mix)
    query = turn(pre[:, :dk], cosine, sine).astype(bf16)
    key = (turn(pre[:, dk : 2 * dk], cosine, sine) * key_scale).astype(bf16)
    value = pre[:, 2 * dk : 2 * dk + dv].astype(bf16)
    gate = pre[:, 2 * dk + dv :]
    scores = (dot(query, key, 1, 1) * decay).astype(bf16)
    retained = dot(scores, value)

    def mix(retained_in, gate_in):
        return head_norm(retained_in) * jax.nn.silu(gate_in)

    mixed, mix_pull = jax.vjp(mix, retained, gate)
    mixed = mixed.astype(bf16)
    out = dot(mixed, w_out)
    x_own = tokens.astype(f32)
    resid = x_own + ring.scatter(jnp.split(out, n))

    z_second_own, second_pull = jax.vjp(layer_norm, resid, gains[2], gains[3])
    z_second = jnp.concatenate(ring.gather(z_second_own.astype(bf16)))
    ab = dot(z_second, w_ffn)

    def unit(gate_in, up_in):
        return jax.nn.gelu(gate_in, approximate=False) * up_in

    hidden, unit_pull = jax.vjp(unit, ab[:, :ff], ab[:, ff:])
    hidden = hidden.astype(bf16)
    grad_hidden = dot(cot_all, w_ffn_down, 1, 1).astype(bf16).astype(f32)
    grad_ab = jnp.concatenate(unit_pull(grad_hidden), -1).astype(bf16)
    grad_z_second = ring.scatter(jnp.split(dot(grad_ab, w_ffn, 1, 1), n))
    grad_resid_norm, grad_gain_second, grad_bias_second = second_pull(grad_z_second)
    grad_resid = cotangent.astype(f32) + grad_resid_norm
    output = (resid + ring.scatter(jnp.split(dot(hidden, w_ffn_down), n))).astype(bf16)
    grad_down = own_rows(dot(hidden, cot_all, 0, 0))
    grad_ffn = rows_of(dot(z_second, grad_ab, 0, 0))

    grad_out = jnp.concatenate(ring.gather(grad_resid.astype(bf16)))
    grad_mixed = dot(grad_out, w_out, 1, 1).astype(bf16).astype(f32)
    grad_retained, grad_gate = mix_pull(grad_mixed)
    grad_retained = grad_retained.astype(bf16)
    grad_scores = (dot(grad_retained, value, 1, 1) * decay).astype(bf16)
    grad_query = turn_back(dot(grad_scores, key), cosine, sine)
    grad_key = turn_back(dot(grad_scores, query, 0, 0), cosine, sine) * key_scale
    grad_value = dot(scores, grad_retained, 0, 0)
    grad_pre = jnp.concatenate([grad_query, grad_key, grad_value, grad_gate], -1).astype(bf16)
    grad_z_first = ring.scatter(jnp.split(dot(grad_pre, w_mix, 1, 1), n))
    _, first_pull = jax.vjp(layer_norm, x_own, gains[0], gains[1])
    grad_input_norm, grad_gain_first, grad_bias_first = first_pull(grad_z_first)
    grad_tokens = grad_resid + grad_input_norm
    grad_w_out = own_rows(dot(mixed, grad_out, 0, 0))
    grad_mix = rows_of(dot(z_first, grad_pre, 0, 0))

    stack = jnp.stack([grad_gain_first, grad_bias_first, grad_gain_second, grad_bias_second])
    for bit in range(n.bit_length() - 1):
        stack = stack + lax.ppermute(stack, "fsdp", [(i, i ^ (1 << bit)) for i in range(n)])
    for bit in range(cube.bits):
        stack = stack + cube.swap(stack, bit)
    stack = lax.dynamic_slice_in_dim(stack, head * depth, depth, 1)

    def flat(grad, start, size):
        return grad[:, :, start : start + size].reshape(depth, n * size)

    return (
        output,
        grad_tokens,
        flat(grad_mix, 0, dk),
        flat(grad_mix, dk, dk),
        flat(grad_mix, 2 * dk, dv),
        flat(grad_mix, 2 * dk + dv, dv),
        grad_w_out,
        stack[0],
        stack[1],
        flat(grad_ffn, 0, ff),
        flat(grad_ffn, ff, ff),
        grad_down,
        stack[2],
        stack[3],
    )


def solution(mesh):
    tokens = P(("rep", "fsdp"), None)
    matrix = P("fsdp", None)
    vector = P("fsdp")
    in_specs = (tokens,) + (matrix,) * 5 + (vector,) * 2 + (matrix,) * 3 + (vector,) * 2 + (tokens,)
    out_specs = (
        (tokens,) * 2 + (matrix,) * 5 + (vector,) * 2 + (matrix,) * 3 + (vector,) * 2
    )
    return jax.shard_map(
        on_device, mesh=mesh, in_specs=in_specs, out_specs=out_specs, check_vma=False
    )
```

```python
import math

import jax
import jax.numpy as jnp
from jax import lax
from jax.experimental import pallas as pl
from jax.experimental.pallas import tpu as pltpu
from jax.sharding import PartitionSpec as P

HEADS = 8
epsilon = 1e-05
head_epsilon = 1.0
f32 = jnp.float32
bf16 = jnp.bfloat16
BOTH = ("rep", "fsdp")
CORE, X = 3, 4


def dot(a, b, ca=1, cb=0, kind=f32):
    return lax.dot_general(a, b, (((ca,), (cb,)), ((), ())), preferred_element_type=kind)


def after(*values):
    return lax.optimization_barrier(values)


def shape(dims, kind):
    return jax.ShapeDtypeStruct(tuple(dims), kind)


def block(dims, *index):
    return pl.BlockSpec(dims, lambda *_: index)


def kernel(body, outs, *ins, scalars=None, scratch=(), limit=48):
    whole = pl.BlockSpec(memory_space=pltpu.VMEM)
    grid = (1,) if any(isinstance(i, tuple) for i in ins) else ()
    specs = [i[1] if isinstance(i, tuple) else whole for i in ins]
    ins = [i[0] if isinstance(i, tuple) else i for i in ins]
    if scalars is not None:
        specs = [pl.BlockSpec(memory_space=pltpu.SMEM)] + specs
        ins = [scalars] + ins
    return pl.pallas_call(
        body,
        out_shape=list(outs),
        grid=grid,
        in_specs=specs,
        out_specs=[whole] * len(outs),
        scratch_shapes=list(scratch),
        compiler_params=pltpu.CompilerParams(vmem_limit_bytes=limit << 20),
        cost_estimate=pl.CostEstimate(flops=0, bytes_accessed=0, transcendentals=0),
    )(*ins)


def number():
    return lax.axis_index("rep") * lax.axis_size("fsdp") + lax.axis_index("fsdp")


def bit(place):
    return (number() >> place) & 1


def bits():
    return (lax.axis_size("rep") * lax.axis_size("fsdp")).bit_length() - 1


def swap(value, place):
    count = 1 << bits()
    return lax.ppermute(value, BOTH, [(i, i ^ (1 << place)) for i in range(count)])


def spread(value):
    for place in range(CORE):
        other = swap(value, place)
        first = bit(place) == 0
        value = jnp.concatenate(
            [jnp.where(first, value, other), jnp.where(first, other, value)], 1
        )
    return value


RING = (0, 2, 4, 6, 7, 5, 3, 1)
OFFSETS = (0, -1, -2, -3, 1, 2, 3, 4)


def owners():
    place = jnp.array([RING.index(i) for i in range(HEADS)], jnp.int32)[lax.axis_index("fsdp")]
    return jnp.array(RING, jnp.int32)[(place + jnp.array(OFFSETS, jnp.int32)) % HEADS]


def send(value, ahead):
    pairs = [(RING[i], RING[(i + 1) % HEADS]) for i in range(HEADS)]
    return lax.ppermute(value, "fsdp", pairs if ahead else [(b, a) for a, b in pairs])


class Gather:
    def __init__(self, own):
        self.own, self.ahead, self.behind = own, [own], [own]

    def step(self, *others):
        a, b = self.ahead[-1], self.behind[-1]
        if len(self.ahead) == 4:
            rows = a.shape[0] // 2
            a, b = a[:rows], b[rows:]
        a, b, *others = after(send(a, True), send(b, False), *others)
        self.ahead.append(a)
        self.behind.append(b)
        return others

    def hold(self, *others):
        self.ahead[-1], self.behind[-1], *others = after(self.ahead[-1], self.behind[-1], *others)
        return others

    def pieces(self):
        return (self.own, *self.ahead[1:4], *self.behind[1:4], self.ahead[4], self.behind[4])


def tile(refs, i):
    names = ((0, 1), (2, 3), (4, 5), (6, 7, 8))[i]
    return jnp.concatenate([refs[j][...] for j in names], 0)


def term_shapes(rows, width):
    return [shape((7 * rows, width), bf16)] + [shape((rows // 2, width), bf16)] * 2


def put_tile(refs, i, values):
    both = values.shape[0]
    rows = both // 2
    values = values.astype(bf16)
    if i < 3:
        refs[0][i * both : (i + 1) * both] = values
    else:
        refs[0][3 * both : 3 * both + rows] = values[:rows]
        refs[1][...] = values[rows : rows + rows // 2]
        refs[2][...] = values[rows + rows // 2 :]


class Scatter:
    def __init__(self, terms):
        self.terms, self.a, self.b = terms
        self.steps = 0

    def term(self, offset):
        rows, width = self.terms.shape[0] // 7, self.terms.shape[1]
        return self.terms, block((rows, width), OFFSETS.index(offset), 0)

    def step(self, *others):
        if self.steps:
            self.fold(4 - self.steps)
        self.a, self.b, *others = after(send(self.a, True), send(self.b, False), *others)
        self.steps += 1
        return others

    def hold(self, *others):
        self.a, self.b, *others = after(self.a, self.b, *others)
        return others

    def fold(self, offset):
        rows, width = self.terms.shape[0] // 7, self.terms.shape[1]
        half = rows // 2

        def body(term_a, term_b, a, b, out_a, out_b):
            if a.shape[0] == rows:
                out_a[...] = (term_a[...].astype(f32) + a[...].astype(f32)).astype(bf16)
                out_b[...] = (term_b[...].astype(f32) + b[...].astype(f32)).astype(bf16)
            else:
                out_a[:half] = (term_a[:half].astype(f32) + a[...].astype(f32)).astype(bf16)
                out_a[half:] = term_a[half:]
                out_b[:half] = term_b[:half]
                out_b[half:] = (term_b[half:].astype(f32) + b[...].astype(f32)).astype(bf16)

        self.a, self.b = kernel(
            body,
            [shape((rows, width), bf16)] * 2,
            self.term(offset), self.term(-offset), self.a, self.b,
            limit=16,
        )

    def pieces(self):
        return self.term(0), self.a, self.b


def total(refs):
    return refs[0][...].astype(f32) + refs[1][...].astype(f32) + refs[2][...].astype(f32)


def normalize(values):
    center = values - jnp.mean(values, axis=-1, keepdims=True)
    scale = lax.rsqrt(jnp.mean(center * center, axis=-1, keepdims=True) + epsilon)
    return center * scale, scale


def normalize_back(normed, scale, grad):
    return scale * (
        grad
        - jnp.mean(grad, axis=-1, keepdims=True)
        - normed * jnp.mean(grad * normed, axis=-1, keepdims=True)
    )


def head_norm(values):
    center = values - jnp.mean(values, axis=-1, keepdims=True)
    scale = lax.rsqrt(jnp.mean(center * center, axis=-1, keepdims=True) + head_epsilon)
    return center * scale, scale


def on_device(
    tokens,
    w_query,
    w_key,
    w_value,
    w_gate,
    w_out,
    norm1_gain,
    norm1_bias,
    w_ffn_gate,
    w_ffn_up,
    w_ffn_down,
    norm2_gain,
    norm2_bias,
    cotangent,
):
    n = lax.axis_size("fsdp")
    assert n == HEADS
    rows, width = tokens.shape
    depth = w_query.shape[0]
    half_depth = depth // 2
    dk = w_query.shape[1] // n
    dv = w_value.shape[1] // n
    ff = w_ffn_gate.shape[1] // n
    every = n * rows
    half_width = width // 2
    where = jnp.stack([bit(CORE), bit(X)])


    def fetch(*weights):
        sizes = [w.shape[1] // n // 2 for w in weights]
        whole = sum(sizes)

        def body(s, *refs):
            start = 0
            for ref, size in zip(refs, sizes):
                refs[-1][0, :, start : start + size] = ref[...]
                start += size

        packed = pl.pallas_call(
            body,
            out_shape=shape((n, half_depth, whole), bf16),
            grid_spec=pltpu.PrefetchScalarGridSpec(
                num_scalar_prefetch=1,
                grid=(n,),
                in_specs=[
                    pl.BlockSpec((half_depth, size), lambda k, s: (s[0], 2 * k + s[1]))
                    for size in sizes
                ],
                out_specs=pl.BlockSpec((1, half_depth, whole), lambda k, s: (k, 0, 0)),
            ),
            cost_estimate=pl.CostEstimate(flops=0, bytes_accessed=0, transcendentals=0),
        )(where, *weights)
        return packed

    def trade(packed):
        got = lax.all_to_all(packed, "fsdp", 0, 0, tiled=True)
        return got.reshape(n * half_depth, got.shape[-1])

    def more(value):
        for place in range(X + 1, bits()):
            value = value + swap(value.astype(bf16), place).astype(f32)
        return value

    def sum_cores(kept, given):
        size = n * half_depth
        kept = kept[:size].astype(f32) + swap(kept[size:], CORE).astype(f32)
        given = given[:size].astype(f32) + swap(given[size:], CORE).astype(f32)
        return kept, given.astype(bf16)

    def give(kept, got):
        grad = more(kept + got.astype(f32)).astype(bf16)
        grad = grad.reshape(n, half_depth, grad.shape[-1])
        return lax.all_to_all(grad, "fsdp", 0, 0, tiled=True)

    def everywhere(own):
        other = swap(own, X)
        return own, swap(own, CORE), other, swap(other, CORE)

    def flat(pieces, sizes):
        whole = sum(sizes) // 2

        def body(s, own, own_c, other, other_c, *outs):
            here = pl.ds(s[0] * half_depth, half_depth)
            there = pl.ds((1 - s[0]) * half_depth, half_depth)
            start = 0
            for out, size in zip(outs, sizes):
                half = size // 2
                columns = slice(start, start + half)
                for x, a, b in ((s[1], own, own_c), (1 - s[1], other, other_c)):
                    place = pl.ds(pl.multiple_of(x * half, half), half)
                    out[here, place] = a[0, :, columns].astype(f32)
                    out[there, place] = b[0, :, columns].astype(f32)
                start += half

        return pl.pallas_call(
            body,
            out_shape=[shape((depth, n * size), f32) for size in sizes],
            grid_spec=pltpu.PrefetchScalarGridSpec(
                num_scalar_prefetch=1,
                grid=(n,),
                in_specs=[pl.BlockSpec((1, half_depth, whole), lambda k, s: (k, 0, 0))] * 4,
                out_specs=[pl.BlockSpec((depth, size), lambda k, s: (0, k)) for size in sizes],
            ),
            cost_estimate=pl.CostEstimate(flops=0, bytes_accessed=0, transcendentals=0),
        )(where, *pieces)


    def sum_cores_rows(grad):
        size = grad.shape[0] // 4
        grad = grad.reshape(2, 2, size, grad.shape[1])
        core = bit(CORE)
        given = lax.dynamic_index_in_dim(grad, 1 - core, 1, False)
        kept = lax.dynamic_index_in_dim(grad, core, 1, False)
        grad = kept.astype(f32) + swap(given, CORE).astype(f32)
        return grad[0], grad[1].astype(bf16)

    def give_rows(kept, got):
        return more(kept + got.astype(f32)).astype(bf16)

    def flat_rows(pieces):
        size = pieces[0].shape[0]

        def body(s, own, own_c, other, other_c, out):
            for x, a, b in ((s[1], own, own_c), (1 - s[1], other, other_c)):
                out[pl.ds((2 * x + s[0]) * size, size), :] = a[...].astype(f32)
                out[pl.ds((2 * x + 1 - s[0]) * size, size), :] = b[...].astype(f32)

        (out,) = kernel(
            body, [shape((4 * size, pieces[0].shape[1]), f32)], *pieces, scalars=where, limit=24
        )
        return out


    def arranged(s):
        for i in range(2 * n):
            column = ((i % n) * 2 + (s[0] ^ (i // n))) * half_depth
            yield i * half_depth, pl.ds(pl.multiple_of(column, half_depth), half_depth)

    block_f32 = shape((rows, width), f32)
    block_bf16 = shape((rows, width), bf16)
    pair_f32 = shape((2, width), f32)
    room_of_block = [pltpu.VMEM((rows, width), f32)]

    def first_norm(s, *refs):
        parts, gains, z, room = refs[:-3], refs[-3], refs[-2], refs[-1]
        values = jnp.concatenate([part[...] for part in parts], 0).astype(f32)
        normed, _ = normalize(values)
        room[...] = normed * gains[0:1] + gains[1:2]
        for start, columns in arranged(s):
            z[:, start : start + half_depth] = room[:, columns].astype(bf16)

    def second_norm(s, *refs):
        sums, (tokens, gains, resid, z, room) = refs[:3], refs[3:]
        value = tokens[...].astype(f32) + total(sums)
        resid[...] = value
        normed, _ = normalize(value)
        room[...] = normed * gains[2:3] + gains[3:4]
        for start, columns in arranged(s):
            z[:, start : start + half_depth] = room[:, columns].astype(bf16)

    def norm_back(s, refs, inputs, gain, room, sums):
        grad = total(refs)
        for start, columns in arranged(s):
            room[:, columns] = grad[:, start : start + half_depth]
        grad = room[...]
        normed, scale = normalize(inputs)
        sums[0:1] = jnp.sum(grad * normed, axis=0, keepdims=True)
        sums[1:2] = jnp.sum(grad, axis=0, keepdims=True)
        return normalize_back(normed, scale, grad * gain)

    def second_back(s, *refs):
        parts, (resid, cot, gains, grad_resid, sums, out, room) = refs[:3], refs[3:]
        grad = norm_back(s, parts, resid[...], gains[2:3], room, sums)
        grad = grad + cot[...].astype(f32)
        grad_resid[...] = grad
        out[...] = grad.astype(bf16)

    def first_back(s, *refs):
        parts, (tokens, grad_resid, gains, out, sums, room) = refs[:3], refs[3:]
        grad = norm_back(s, parts, tokens[...].astype(f32), gains[0:1], room, sums)
        out[...] = grad_resid[...] + grad

    def last_sum(*refs):
        parts, resid, out = refs[:3], refs[3], refs[4]
        out[...] = (resid[...] + total(parts)).astype(bf16)


    tiles = range(4)
    halves = (slice(0, half_width), slice(half_width, width))

    def rows_of(i):
        return slice(2 * i * rows, 2 * (i + 1) * rows)

    def in_order(x, own, other):
        first = jnp.where(x == 0, own, other)
        second = jnp.where(x == 0, other, own)
        return first, second

    def project(s, *refs):
        zs, w, (cosine, sine, q, k, v, g) = refs[:4], refs[4:8], refs[8:]
        x = s[1]
        one = dk // 2
        for i in tiles:
            here = rows_of(i)
            own, other = (
                dot(zs[i][:, halves[0]], w[j][...]) + dot(zs[i][:, halves[1]], w[2 + j][...])
                for j in (0, 1)
            )
            c, sn = cosine[here], sine[here]
            a, b = in_order(x, own[:, :one], other[:, :one])
            q[here, :one] = (a * c - b * sn).astype(bf16)
            q[here, one:] = (b * c + a * sn).astype(bf16)
            a, b = in_order(x, own[:, one:dk], other[:, one:dk])
            k[here, :one] = ((a * c - b * sn) * dk**-0.5).astype(bf16)
            k[here, one:] = ((b * c + a * sn) * dk**-0.5).astype(bf16)
            middle = dk + dv // 2
            v[here, : dv // 2] = own[:, dk:middle].astype(bf16)
            v[here, dv // 2 :] = other[:, dk:middle].astype(bf16)
            g[here, : dv // 2] = own[:, middle:]
            g[here, dv // 2 :] = other[:, middle:]

    def of_x(ref, x, size):
        return [ref[pl.ds(pl.multiple_of(i * size, size), size), :] for i in (x, 1 - x)]

    def mix(s, q, k, v, decay, g, w, p, retained, mixed, *outs):
        for i in tiles:
            here = rows_of(i)
            scores = (dot(q[here], k[...], 1, 1) * decay[here]).astype(bf16)
            p[here] = scores
            value = dot(scores, v[...])
            retained[here] = value
            normed, _ = head_norm(value)
            gate = g[here]
            part = (normed * gate / (1.0 + jnp.exp(-gate))).astype(bf16)
            mixed[here] = part
            half = dv // 2
            own, other = of_x(w, s[1], half)
            put_tile(outs, i, dot(part[:, :half], own) + dot(part[:, half:], other))

    def hidden_back(s, *refs):
        pieces, (w, cot, d_hidden) = refs[:9], refs[9:]
        half = ff // 2
        for i in tiles:
            here = rows_of(i)
            part = tile(pieces, i)
            cot[here] = part
            own, other = of_x(w, s[1], half)
            d_hidden[here, :half] = dot(part, own, 1, 1).astype(bf16)
            d_hidden[here, half:] = dot(part, other, 1, 1).astype(bf16)

    def feed(*refs):
        pieces, d_hidden, w, (z, hidden, grad) = refs[:9], refs[9], refs[10:14], refs[14:17]
        outs = refs[17:]
        half = ff // 2
        for i in tiles:
            here = rows_of(i)
            part = tile(pieces, i)
            z[here] = part
            back = 0.0
            for j in (0, 1):
                ab = dot(part[:, halves[0]], w[j][...]) + dot(part[:, halves[1]], w[2 + j][...])
                a, b = ab[:, :half], ab[:, half:]
                below = 0.5 * (1.0 + lax.erf(a * math.sqrt(0.5)))
                gelu = a * below
                slope = below + a * jnp.exp(-0.5 * a * a) * (1.0 / math.sqrt(2.0 * math.pi))
                columns = slice(j * half, (j + 1) * half)
                hidden[here, columns] = (gelu * b).astype(bf16)
                d = d_hidden[here, columns].astype(f32)
                both = jnp.concatenate([d * b * slope, d * gelu], -1).astype(bf16)
                grad[j, here] = both
                back = back + jnp.concatenate(
                    [dot(both, w[j][...], 1, 1), dot(both, w[2 + j][...], 1, 1)], -1
                )
            put_tile(outs, i, back)

    def down(s, h, w, *outs):
        half = ff // 2
        for i in tiles:
            here = rows_of(i)
            own, other = of_x(w, s[1], half)
            put_tile(outs, i, dot(h[here, :half], own) + dot(h[here, half:], other))

    def mix_back(s, *refs):
        pieces, (w, r, g, d_out, d_retained, d_gate) = refs[:9], refs[9:]
        half = dv // 2
        for i in tiles:
            here = rows_of(i)
            part = tile(pieces, i)
            d_out[here] = part
            own, other = of_x(w, s[1], half)
            d_mixed = jnp.concatenate([dot(part, own, 1, 1), dot(part, other, 1, 1)], -1)
            d_mixed = d_mixed.astype(bf16).astype(f32)
            normed, scale = head_norm(r[here])
            gate = g[here]
            sigmoid = 1.0 / (1.0 + jnp.exp(-gate))
            d_gate[here] = (d_mixed * normed * sigmoid * (1.0 + gate * (1.0 - sigmoid))).astype(bf16)
            d_retained[here] = normalize_back(normed, scale, d_mixed * gate * sigmoid).astype(bf16)

    def within_back(s, d_r, d_g, q, k, v, p, decay, cosine, sine, *refs):
        w, wg, d_pre, outs, (d_k, d_v) = refs[:4], refs[4:8], refs[8], refs[9:12], refs[12:]
        one, half = dk // 2, dv // 2
        x = s[1]
        for i in tiles:
            here = rows_of(i)
            scores = (dot(d_r[here], v[...], 1, 1) * decay[here]).astype(bf16)
            c, sn = cosine[here], sine[here]
            grad = dot(scores, k[...])
            a, b = grad[:, :one], grad[:, one:]
            own, other = in_order(x, a * c + b * sn, b * c - a * sn)
            d_pre[0, here, :one] = own.astype(bf16)
            d_pre[1, here, :one] = other.astype(bf16)
            more_k, more_v = dot(scores, q[here], 0, 0), dot(p[here], d_r[here], 0, 0)
            if i == 0:
                d_k[...], d_v[...] = more_k, more_v
            else:
                d_k[...] += more_k
                d_v[...] += more_v
        for i in tiles:
            here = rows_of(i)
            c, sn = cosine[here] * dk**-0.5, sine[here] * dk**-0.5
            a, b = d_k[here, :one], d_k[here, one:]
            own, other = in_order(x, a * c + b * sn, b * c - a * sn)
            d_pre[0, here, one:dk] = own.astype(bf16)
            d_pre[1, here, one:dk] = other.astype(bf16)
            d_pre[0, here, dk:] = d_v[here, :half].astype(bf16)
            d_pre[1, here, dk:] = d_v[here, half:].astype(bf16)
            back = []
            for t in (0, 1):
                part = dot(d_g[here, :half], wg[2 * t][...], 1, 1)
                part = part + dot(d_g[here, half:], wg[2 * t + 1][...], 1, 1)
                for j in (0, 1):
                    part = part + dot(d_pre[j, here], w[2 * t + j][...], 1, 1)
                back.append(part)
            put_tile(outs, i, jnp.concatenate(back, -1))

    terms = term_shapes(rows, width)


    gains = jnp.stack([norm1_gain, norm1_bias, norm2_gain, norm2_bias])
    gains = spread(gains).astype(f32)
    packed, tokens_late = after(fetch(w_query, w_key, w_value, w_gate), tokens)
    mix_own = trade(packed)
    ring = Gather(tokens_late)

    head = lax.axis_index("fsdp")
    gamma_log = jnp.log(1.0 - 2.0 ** (-5.0 - head.astype(f32)))
    positions = (owners() * rows)[:, None] + jnp.arange(rows, dtype=jnp.int32)[None, :]
    positions = positions.reshape(-1).astype(f32)
    half = dk // 2
    freqs = jnp.exp(-jnp.arange(half, dtype=f32) * (math.log(10000.0) / half))
    angles = positions[:, None] * freqs[None, :]
    cosine, sine = jnp.cos(angles), jnp.sin(angles)
    differ = positions[:, None] - positions[None, :]
    decay = jnp.where(differ >= 0, jnp.exp(jnp.maximum(differ, 0.0) * gamma_log), 0.0)

    (mix_own,) = ring.step(mix_own)
    mix_other = swap(mix_own, X)
    mix_own_c = swap(mix_own, CORE)
    ring.step()
    ring.step()
    cosine, sine, decay = ring.step(cosine, sine, decay)
    pieces = ring.pieces()
    zs = []
    for i in tiles:
        names = ((0, 1), (2, 3), (4, 5), (6, 7, 8))[i]
        zs += kernel(
            first_norm,
            [shape((2 * rows, width), bf16)],
            *(pieces[j] for j in names), gains,
            scalars=where, scratch=[pltpu.VMEM((2 * rows, width), f32)], limit=16,
        )
    mix_other_c = swap(mix_other, CORE)
    w_mix = (mix_own, mix_other, mix_own_c, mix_other_c)
    *w_mix, z0, z1, z2, z3, ffn_gate_late, ffn_up_late = after(*w_mix, *zs, w_ffn_gate, w_ffn_up)
    zs = (z0, z1, z2, z3)
    ffn_own = trade(fetch(ffn_gate_late, ffn_up_late))
    query, key, value, gate = kernel(
        project,
        [shape((every, dk), bf16)] * 2 + [shape((every, dv), bf16), shape((every, dv), f32)],
        *zs, *w_mix, cosine, sine,
        scalars=where,
    )
    scores, retained, mixed, *parts = kernel(
        mix,
        [shape((every, every), bf16), shape((every, dv), f32), shape((every, dv), bf16)] + terms,
        query, key, value, decay, gate, w_out,
        scalars=where,
    )
    ring = Scatter(parts)
    cot_late, ffn_own = ring.hold(cotangent, ffn_own)
    ffn_other = swap(ffn_own, X)
    ffn_own_c = swap(ffn_own, CORE)
    cot_ring = Gather(cot_late)
    ring.step()
    cot_ring.step()
    ring.step()
    cot_ring.step()
    ring.step()
    cot_ring.step()
    ring.step()
    resid, second = kernel(
        second_norm, [block_f32, block_bf16], *ring.pieces(), tokens, gains,
        scalars=where, scratch=room_of_block, limit=16,
    )

    ring = Gather(second)
    (ffn_other,) = ring.step(ffn_other)
    ffn_other_c = swap(ffn_other, CORE)
    cot_ring.step()
    cot_all, d_hidden = kernel(
        hidden_back,
        [shape((every, width), bf16), shape((every, ff), bf16)],
        *cot_ring.pieces(), w_ffn_down,
        scalars=where,
    )
    ring.step()
    ring.step()
    w_ffn = (ffn_own, ffn_other, ffn_own_c, ffn_other_c)
    *w_ffn, d_hidden = ring.step(*w_ffn, d_hidden)
    z_second, hidden, d_ab, *parts = kernel(
        feed,
        [shape((every, width), bf16), shape((every, ff), bf16), shape((2, every, ff), bf16)]
        + terms,
        *ring.pieces(), d_hidden, *w_ffn,
    )
    ring = Scatter(parts)
    ring.step()
    grad_ffn = [dot(z_second, d_ab[j], 0, 0, bf16) for j in (0, 1)]
    grad_down = dot(hidden, cot_all, 0, 0, bf16)
    (grad_down, *grad_ffn) = ring.step(grad_down, *grad_ffn)
    down_kept, down_given = sum_cores_rows(grad_down)
    ffn_kept, ffn_given = sum_cores(*grad_ffn)
    ring.step()
    ring.step()
    grad_resid, second_sums, part = kernel(
        second_back, [block_f32, pair_f32, block_bf16],
        *ring.pieces(), resid, cotangent, gains,
        scalars=where, scratch=room_of_block, limit=16,
    )
    ring = Gather(part)
    ffn_given, ffn_kept, down_given, down_kept = ring.step(
        ffn_given, ffn_kept, down_given, down_kept
    )
    ffn_sent = swap(ffn_given, X)
    down_sent = swap(down_given, X)
    ring.step()
    ring.step()
    ffn_sent, down_sent, w_down_late = ring.step(ffn_sent, down_sent, w_ffn_down)

    ffn_owned = give(ffn_kept, ffn_sent)
    down_owned = give_rows(down_kept, down_sent)
    d_out, d_retained, d_gate = kernel(
        mix_back,
        [shape((every, width), bf16)] + [shape((every, dv), bf16)] * 2,
        *ring.pieces(), w_out, retained, gate,
        scalars=where,
    )
    z_first = jnp.concatenate(zs)
    w_qkv = [w[:, : dk + dv // 2] for w in w_mix]
    w_g = [w[:, dk + dv // 2 :] for w in w_mix]
    d_pre, *parts = kernel(
        within_back,
        [shape((2, every, dk + dv // 2), bf16)] + terms,
        d_retained, d_gate, query, key, value, scores, decay, cosine, sine, *w_qkv, *w_g,
        scalars=where, scratch=[pltpu.VMEM((every, dk), f32), pltpu.VMEM((every, dv), f32)],
    )
    grad_gate = [
        dot(z_first, d_gate[:, j * (dv // 2) : (j + 1) * (dv // 2)], 0, 0, bf16) for j in (0, 1)
    ]
    gate_kept, gate_given = sum_cores(*grad_gate)
    gate_owned = give(gate_kept, swap(gate_given, X))
    ring = Scatter(parts)
    grad_qkv = [dot(z_first, d_pre[j], 0, 0, bf16) for j in (0, 1)]
    qkv_kept, qkv_given = sum_cores(*grad_qkv)
    qkv_owned = give(qkv_kept, swap(qkv_given, X))
    out_kept, out_given = sum_cores_rows(dot(mixed, d_out, 0, 0, bf16))
    out_owned = give_rows(out_kept, swap(out_given, X))
    ring.step()
    ring.step()
    ring.step()
    ring.step()
    grad_tokens, first_sums = kernel(
        first_back, [block_f32, pair_f32], *ring.pieces(), tokens, grad_resid, gains,
        scalars=where, scratch=room_of_block, limit=16,
    )
    last = Scatter(
        kernel(down, terms, hidden, w_down_late, scalars=where)
    )
    last.hold(d_pre)
    for _ in range(4):
        last.step()
    (output,) = kernel(last_sum, [block_bf16], *last.pieces(), resid, limit=16)
    stack = jnp.concatenate([first_sums, second_sums])
    for place in range(bits()):
        stack = stack + swap(stack, place)
    stack = lax.dynamic_slice_in_dim(stack, lax.axis_index("fsdp") * depth, depth, 1)
    grad_ffn_gate, grad_ffn_up = flat(everywhere(ffn_owned), [ff, ff])
    grad_down = flat_rows(everywhere(down_owned))
    (grad_gate,) = flat(everywhere(gate_owned), [dv])
    grad_query, grad_key, grad_value = flat(everywhere(qkv_owned), [dk, dk, dv])
    grad_out = flat_rows(everywhere(out_owned))

    return (
        output,
        grad_tokens,
        grad_query,
        grad_key,
        grad_value,
        grad_gate,
        grad_out,
        stack[0],
        stack[1],
        grad_ffn_gate,
        grad_ffn_up,
        grad_down,
        stack[2],
        stack[3],
    )


def solution(mesh):
    tokens = P(("rep", "fsdp"), None)
    matrix = P("fsdp", None)
    vector = P("fsdp")
    in_specs = (tokens,) + (matrix,) * 5 + (vector,) * 2 + (matrix,) * 3 + (vector,) * 2 + (tokens,)
    out_specs = (tokens,) * 2 + (matrix,) * 5 + (vector,) * 2 + (matrix,) * 3 + (vector,) * 2
    return jax.shard_map(
        on_device, mesh=mesh, in_specs=in_specs, out_specs=out_specs, check_vma=False
    )
```

```python
import math

import jax
import jax.numpy as jnp
from jax import lax
from jax.experimental import pallas as pl
from jax.experimental.pallas import tpu as pltpu
from jax.sharding import PartitionSpec as P

HEADS = 8
epsilon = 1e-05
head_epsilon = 1.0
f32 = jnp.float32
bf16 = jnp.bfloat16
BOTH = ("rep", "fsdp")
CORE, X = 3, 4
LIMITS = (26, 30, 38, 30, 38, 24)


def dot(a, b, ca=1, cb=0, kind=f32):
    return lax.dot_general(a, b, (((ca,), (cb,)), ((), ())), preferred_element_type=kind)


def after(*values):
    return lax.optimization_barrier(values)


def shape(dims, kind):
    return jax.ShapeDtypeStruct(tuple(dims), kind)


def block(dims, *index):
    return pl.BlockSpec(dims, lambda *_: index)


def kernel(body, outs, *ins, scalars=None, scratch=(), limit=8):
    whole = pl.BlockSpec(memory_space=pltpu.VMEM)
    grid = (1,) if any(isinstance(i, tuple) for i in ins) else ()
    specs = [i[1] if isinstance(i, tuple) else whole for i in ins]
    ins = [i[0] if isinstance(i, tuple) else i for i in ins]
    if scalars is not None:
        specs = [pl.BlockSpec(memory_space=pltpu.SMEM)] + specs
        ins = [scalars] + ins
    return pl.pallas_call(
        body,
        out_shape=list(outs),
        grid=grid,
        in_specs=specs,
        out_specs=[whole] * len(outs),
        scratch_shapes=list(scratch),
        compiler_params=pltpu.CompilerParams(vmem_limit_bytes=limit << 20),
        cost_estimate=pl.CostEstimate(flops=0, bytes_accessed=0, transcendentals=0),
    )(*ins)


def number():
    return lax.axis_index("rep") * lax.axis_size("fsdp") + lax.axis_index("fsdp")


def bit(place):
    return (number() >> place) & 1


def bits():
    return (lax.axis_size("rep") * lax.axis_size("fsdp")).bit_length() - 1


def swap(value, place):
    count = 1 << bits()
    return lax.ppermute(value, BOTH, [(i, i ^ (1 << place)) for i in range(count)])


RING = (0, 2, 4, 6, 7, 5, 3, 1)
OFFSETS = (0, -1, -2, -3, 1, 2, 3, 4)


def owners():
    place = jnp.array([RING.index(i) for i in range(HEADS)], jnp.int32)[lax.axis_index("fsdp")]
    return jnp.array(RING, jnp.int32)[(place + jnp.array(OFFSETS, jnp.int32)) % HEADS]


def send(value, ahead):
    pairs = [(RING[i], RING[(i + 1) % HEADS]) for i in range(HEADS)]
    return lax.ppermute(value, "fsdp", pairs if ahead else [(b, a) for a, b in pairs])


class Gather:
    def __init__(self, own):
        self.own, self.ahead, self.behind = own, [own], [own]

    def peek(self):
        a, b = self.ahead[-1], self.behind[-1]
        if len(self.ahead) == 4:
            rows = a.shape[0] // 2
            a, b = a[:rows], b[rows:]
        return send(a, True), send(b, False)

    def put(self, a, b):
        self.ahead.append(a)
        self.behind.append(b)

    def step(self, *others):
        a, b, *others = after(*self.peek(), *others)
        self.put(a, b)
        return others

    def hold(self, *others):
        self.ahead[-1], self.behind[-1], *others = after(self.ahead[-1], self.behind[-1], *others)
        return others

    def pieces(self):
        return (self.own, *self.ahead[1:4], *self.behind[1:4], self.ahead[4], self.behind[4])


def tile(refs, i):
    names = ((0, 1), (2, 3), (4, 5), (6, 7, 8))[i]
    return jnp.concatenate([refs[j][...] for j in names], 0)


def term_shapes(rows, width):
    return [shape((7 * rows, width), bf16)] + [shape((rows // 2, width), bf16)] * 2


def put_tile(refs, i, values):
    both = values.shape[0]
    rows = both // 2
    values = values.astype(bf16)
    if i < 3:
        refs[0][i * both : (i + 1) * both] = values
    else:
        refs[0][3 * both : 3 * both + rows] = values[:rows]
        refs[1][...] = values[rows : rows + rows // 2]
        refs[2][...] = values[rows + rows // 2 :]


class Scatter:
    def __init__(self, terms):
        self.terms, self.a, self.b = terms
        self.steps = 0

    def term(self, offset):
        rows, width = self.terms.shape[0] // 7, self.terms.shape[1]
        return self.terms, block((rows, width), OFFSETS.index(offset), 0)

    def peek(self):
        if self.steps:
            self.fold(4 - self.steps)
        self.steps += 1
        return send(self.a, True), send(self.b, False)

    def put(self, a, b):
        self.a, self.b = a, b

    def step(self, *others):
        a, b, *others = after(*self.peek(), *others)
        self.put(a, b)
        return others

    def hold(self, *others):
        self.a, self.b, *others = after(self.a, self.b, *others)
        return others

    def fold(self, offset):
        rows, width = self.terms.shape[0] // 7, self.terms.shape[1]
        half = rows // 2

        def body(term_a, term_b, a, b, out_a, out_b):
            if a.shape[0] == rows:
                out_a[...] = (term_a[...].astype(f32) + a[...].astype(f32)).astype(bf16)
                out_b[...] = (term_b[...].astype(f32) + b[...].astype(f32)).astype(bf16)
            else:
                out_a[:half] = (term_a[:half].astype(f32) + a[...].astype(f32)).astype(bf16)
                out_a[half:] = term_a[half:]
                out_b[:half] = term_b[:half]
                out_b[half:] = (term_b[half:].astype(f32) + b[...].astype(f32)).astype(bf16)

        self.a, self.b = kernel(
            body,
            [shape((rows, width), bf16)] * 2,
            self.term(offset), self.term(-offset), self.a, self.b,
            limit=8,
        )

    def pieces(self):
        return self.term(0), self.a, self.b


def total(refs):
    return refs[0][...].astype(f32) + refs[1][...].astype(f32) + refs[2][...].astype(f32)


def normalize(values):
    center = values - jnp.mean(values, axis=-1, keepdims=True)
    scale = lax.rsqrt(jnp.mean(center * center, axis=-1, keepdims=True) + epsilon)
    return center * scale, scale


def normalize_back(normed, scale, grad):
    return scale * (
        grad
        - jnp.mean(grad, axis=-1, keepdims=True)
        - normed * jnp.mean(grad * normed, axis=-1, keepdims=True)
    )


def head_norm(values):
    center = values - jnp.mean(values, axis=-1, keepdims=True)
    scale = lax.rsqrt(jnp.mean(center * center, axis=-1, keepdims=True) + head_epsilon)
    return center * scale, scale


def on_device(
    tokens,
    w_query,
    w_key,
    w_value,
    w_gate,
    w_out,
    norm1_gain,
    norm1_bias,
    w_ffn_gate,
    w_ffn_up,
    w_ffn_down,
    norm2_gain,
    norm2_bias,
    cotangent,
):
    n = lax.axis_size("fsdp")
    assert n == HEADS
    rows, width = tokens.shape
    depth = w_query.shape[0]
    half_depth = depth // 2
    dk = w_query.shape[1] // n
    dv = w_value.shape[1] // n
    ff = w_ffn_gate.shape[1] // n
    every = n * rows
    half_width = width // 2
    where = jnp.stack([bit(CORE), bit(X)])


    def fetch(*weights):
        sizes = [w.shape[1] // n // 2 for w in weights]
        whole = sum(sizes)

        def body(s, *refs):
            for h in range(4):
                start = 0
                for ref, size in zip(refs, sizes):
                    place = pl.multiple_of((2 * h + s[1]) * size, size)
                    refs[-1][h, :, start : start + size] = ref[:, pl.ds(place, size)]
                    start += size

        packed = pl.pallas_call(
            body,
            out_shape=shape((n, half_depth, whole), bf16),
            grid_spec=pltpu.PrefetchScalarGridSpec(
                num_scalar_prefetch=1,
                grid=(n // 4,),
                in_specs=[
                    pl.BlockSpec((half_depth, 8 * size), lambda k, s: (s[0], k)) for size in sizes
                ],
                out_specs=pl.BlockSpec((4, half_depth, whole), lambda k, s: (k, 0, 0)),
            ),
            compiler_params=pltpu.CompilerParams(vmem_limit_bytes=60 << 20),
            cost_estimate=pl.CostEstimate(flops=0, bytes_accessed=0, transcendentals=0),
        )(where, *weights)
        return packed

    def trade(packed):
        got = lax.all_to_all(packed, "fsdp", 0, 0, tiled=True)
        return got.reshape(n * half_depth, got.shape[-1])

    def more(value):
        for place in range(X + 1, bits()):
            value = value + swap(value.astype(bf16), place).astype(f32)
        return value

    def columns_grad(z, own, other):
        size = own.shape[-1]

        def body(z, own, other, *outs):
            for t in (0, 1):
                rows_t = z[:, t * half_width : (t + 1) * half_width]
                for out, part in ((outs[t], own), (outs[2 + t], other)):
                    out[...] = dot(rows_t, part[...], 0, 0).astype(bf16)

        return kernel(body, [shape((half_width, size), bf16)] * 4, z, own, other, limit=LIMITS[5])

    def sum_cores(own, own_t, other, other_t):
        kept = own.astype(f32) + swap(own_t, CORE).astype(f32)
        given = other.astype(f32) + swap(other_t, CORE).astype(f32)
        return kept, given.astype(bf16)

    def give(kept, got):
        grad = more(kept + got.astype(f32)).astype(bf16)
        grad = grad.reshape(n, half_depth, grad.shape[-1])
        return lax.all_to_all(grad, "fsdp", 0, 0, tiled=True)

    def everywhere(own):
        other = swap(own, X)
        return own, swap(own, CORE), other, swap(other, CORE)

    def flat(pieces, sizes):
        whole = sum(sizes) // 2

        def body(s, own, own_c, other, other_c, *outs):
            here = pl.ds(s[0] * half_depth, half_depth)
            there = pl.ds((1 - s[0]) * half_depth, half_depth)
            for h in (0, 1):
                start = 0
                for out, size in zip(outs, sizes):
                    half = size // 2
                    columns = slice(start, start + half)
                    for x, a, b in ((s[1], own, own_c), (1 - s[1], other, other_c)):
                        place = pl.ds(pl.multiple_of(x * half, half) + h * size, half)
                        out[here, place] = a[h, :, columns].astype(f32)
                        out[there, place] = b[h, :, columns].astype(f32)
                    start += half

        return pl.pallas_call(
            body,
            out_shape=[shape((depth, n * size), f32) for size in sizes],
            grid_spec=pltpu.PrefetchScalarGridSpec(
                num_scalar_prefetch=1,
                grid=(n // 2,),
                in_specs=[pl.BlockSpec((2, half_depth, whole), lambda k, s: (k, 0, 0))] * 4,
                out_specs=[pl.BlockSpec((depth, 2 * size), lambda k, s: (0, k)) for size in sizes],
            ),
            compiler_params=pltpu.CompilerParams(vmem_limit_bytes=24 << 20),
            cost_estimate=pl.CostEstimate(flops=0, bytes_accessed=0, transcendentals=0),
        )(where, *pieces)


    def rows_products(s, left, right, kept, given):
        size = left.shape[1] // 4
        for out, c in ((kept, s[0]), (given, 1 - s[0])):
            for i in (0, 1):
                columns = pl.ds(pl.multiple_of((2 * i + c) * size, size), size)
                out[i] = dot(left[:, columns], right[...], 0, 0).astype(bf16)

    def rows_grad(left, right):
        return kernel(
            rows_products, [shape((2, left.shape[1] // 4, right.shape[1]), bf16)] * 2, left, right,
            scalars=where, limit=14,
        )

    def sum_cores_rows(kept, given):
        grad = kept.astype(f32) + swap(given, CORE).astype(f32)
        return grad[0], grad[1].astype(bf16)

    def give_rows(kept, got):
        return more(kept + got.astype(f32)).astype(bf16)

    def flat_rows(pieces):
        size = pieces[0].shape[0]

        def body(s, own, own_c, other, other_c, out):
            for x, a, b in ((s[1], own, own_c), (1 - s[1], other, other_c)):
                out[pl.ds((2 * x + s[0]) * size, size), :] = a[...].astype(f32)
                out[pl.ds((2 * x + 1 - s[0]) * size, size), :] = b[...].astype(f32)

        (out,) = kernel(
            body, [shape((4 * size, pieces[0].shape[1]), f32)], *pieces, scalars=where, limit=8
        )
        return out


    def arranged(s):
        for i in range(2 * n):
            column = ((i % n) * 2 + (s[0] ^ (i // n))) * half_depth
            yield i * half_depth, pl.ds(pl.multiple_of(column, half_depth), half_depth)

    block_f32 = shape((rows, width), f32)
    block_bf16 = shape((rows, width), bf16)
    pair_f32 = shape((2, width), f32)
    room_of_block = [pltpu.VMEM((rows, width), f32)]

    def first_norm(s, *refs):
        parts, gains, z, room = refs[:-3], refs[-3], refs[-2], refs[-1]
        values = jnp.concatenate([part[...] for part in parts], 0).astype(f32)
        normed, _ = normalize(values)
        room[...] = normed * gains[0:1] + gains[1:2]
        for start, columns in arranged(s):
            z[:, start : start + half_depth] = room[:, columns].astype(bf16)

    def second_norm(s, *refs):
        sums, (tokens, gains, resid, z, room) = refs[:3], refs[3:]
        value = tokens[...].astype(f32) + total(sums)
        resid[...] = value
        normed, _ = normalize(value)
        room[...] = normed * gains[2:3] + gains[3:4]
        for start, columns in arranged(s):
            z[:, start : start + half_depth] = room[:, columns].astype(bf16)

    def norm_back(s, refs, inputs, gain, room, sums=None):
        grad = total(refs)
        for start, columns in arranged(s):
            room[:, columns] = grad[:, start : start + half_depth]
        grad = room[...]
        normed, scale = normalize(inputs)
        if sums is not None:
            sums[0:1] = jnp.sum(grad * normed, axis=0, keepdims=True)
            sums[1:2] = jnp.sum(grad, axis=0, keepdims=True)
        return normalize_back(normed, scale, grad * gain)

    def second_back(s, *refs):
        parts, (resid, cot, gains, grad_resid, sums, out, room) = refs[:3], refs[3:]
        grad = norm_back(s, parts, resid[...], gains[2:3], room, sums)
        grad = grad + cot[...].astype(f32)
        grad_resid[...] = grad
        out[...] = grad.astype(bf16)

    def first_back(s, *refs):
        parts, (tokens, grad_resid, gains, out, room) = refs[:3], refs[3:]
        grad = norm_back(s, parts, tokens[...].astype(f32), gains[0:1], room)
        out[...] = grad_resid[...] + grad

    def last_sum(*refs):
        parts, resid, out = refs[:3], refs[3], refs[4]
        out[...] = (resid[...] + total(parts)).astype(bf16)


    tiles = range(4)
    halves = (slice(0, half_width), slice(half_width, width))

    def rows_of(i):
        return slice(2 * i * rows, 2 * (i + 1) * rows)

    def in_order(x, own, other):
        first = jnp.where(x == 0, own, other)
        second = jnp.where(x == 0, other, own)
        return first, second

    def project(s, *refs):
        zs, w, (cosine, sine, q, k, v, g) = refs[:4], refs[4:8], refs[8:]
        x = s[1]
        one = dk // 2
        for i in tiles:
            here = rows_of(i)
            own, other = (
                dot(zs[i][:, halves[0]], w[j][...]) + dot(zs[i][:, halves[1]], w[2 + j][...])
                for j in (0, 1)
            )
            c, sn = cosine[here], sine[here]
            a, b = in_order(x, own[:, :one], other[:, :one])
            q[here, :one] = (a * c - b * sn).astype(bf16)
            q[here, one:] = (b * c + a * sn).astype(bf16)
            a, b = in_order(x, own[:, one:dk], other[:, one:dk])
            k[here, :one] = ((a * c - b * sn) * dk**-0.5).astype(bf16)
            k[here, one:] = ((b * c + a * sn) * dk**-0.5).astype(bf16)
            middle = dk + dv // 2
            v[here, : dv // 2] = own[:, dk:middle].astype(bf16)
            v[here, dv // 2 :] = other[:, dk:middle].astype(bf16)
            g[here, : dv // 2] = own[:, middle:]
            g[here, dv // 2 :] = other[:, middle:]

    def of_x(ref, x, size):
        return [ref[pl.ds(pl.multiple_of(i * size, size), size), :] for i in (x, 1 - x)]

    def mix(s, q, k, v, decay, g, w, p, retained, mixed, *outs):
        for i in tiles:
            here = rows_of(i)
            scores = (dot(q[here], k[...], 1, 1) * decay[here]).astype(bf16)
            p[here] = scores
            value = dot(scores, v[...])
            retained[here] = value
            normed, _ = head_norm(value)
            gate = g[here]
            part = (normed * gate / (1.0 + jnp.exp(-gate))).astype(bf16)
            mixed[here] = part
            half = dv // 2
            own, other = of_x(w, s[1], half)
            put_tile(outs, i, dot(part[:, :half], own) + dot(part[:, half:], other))

    def join_tiles(*refs):
        for i in tiles:
            refs[9][rows_of(i)] = tile(refs, i)

    def feed(s, *refs):
        pieces, cots, w_down, w = refs[:9], refs[9:18], refs[18], refs[19:23]
        (z, hidden, grad), outs = refs[23:26], refs[26:]
        half = ff // 2
        for i in tiles:
            here = rows_of(i)
            part = tile(pieces, i)
            z[here] = part
            cot = tile(cots, i)
            downs = of_x(w_down, s[1], half)
            back = 0.0
            for j in (0, 1):
                ab = dot(part[:, halves[0]], w[j][...]) + dot(part[:, halves[1]], w[2 + j][...])
                a, b = ab[:, :half], ab[:, half:]
                below = 0.5 * (1.0 + lax.erf(a * math.sqrt(0.5)))
                gelu = a * below
                slope = below + a * jnp.exp(-0.5 * a * a) * (1.0 / math.sqrt(2.0 * math.pi))
                columns = slice(j * half, (j + 1) * half)
                hidden[here, columns] = (gelu * b).astype(bf16)
                d = dot(cot, downs[j], 1, 1).astype(bf16).astype(f32)
                both = jnp.concatenate([d * b * slope, d * gelu], -1).astype(bf16)
                grad[j, here] = both
                back = back + jnp.concatenate(
                    [dot(both, w[j][...], 1, 1), dot(both, w[2 + j][...], 1, 1)], -1
                )
            put_tile(outs, i, back)

    def down(s, h, w, *outs):
        half = ff // 2
        for i in tiles:
            here = rows_of(i)
            own, other = of_x(w, s[1], half)
            put_tile(outs, i, dot(h[here, :half], own) + dot(h[here, half:], other))

    def mix_back(s, *refs):
        pieces, (w, r, g, mixed, kept, given, d_retained, d_gate, d_out) = refs[:9], refs[9:]
        half = dv // 2
        for i in tiles:
            here = rows_of(i)
            part = tile(pieces, i)
            d_out[here] = part
            own, other = of_x(w, s[1], half)
            d_mixed = jnp.concatenate([dot(part, own, 1, 1), dot(part, other, 1, 1)], -1)
            d_mixed = d_mixed.astype(bf16).astype(f32)
            normed, scale = head_norm(r[here])
            gate = g[here]
            sigmoid = 1.0 / (1.0 + jnp.exp(-gate))
            both = (d_mixed * normed * sigmoid * (1.0 + gate * (1.0 - sigmoid))).astype(bf16)
            d_gate[0, here], d_gate[1, here] = both[:, :half], both[:, half:]
            d_retained[here] = normalize_back(normed, scale, d_mixed * gate * sigmoid).astype(bf16)
        rows_products(s, mixed, d_out, kept, given)

    def within_back(s, d_r, d_g, q, k, v, p, decay, cosine, sine, *refs):
        w, zs, (d_pre, sums), outs = refs[:4], refs[4:8], refs[8:10], refs[10:13]
        d_k, d_v, room = refs[13:]
        cut = dk + dv // 2
        one, half = dk // 2, dv // 2
        x = s[1]
        for i in tiles:
            here = rows_of(i)
            scores = (dot(d_r[here], v[...], 1, 1) * decay[here]).astype(bf16)
            c, sn = cosine[here], sine[here]
            grad = dot(scores, k[...])
            a, b = grad[:, :one], grad[:, one:]
            own, other = in_order(x, a * c + b * sn, b * c - a * sn)
            d_pre[0, here, :one] = own.astype(bf16)
            d_pre[1, here, :one] = other.astype(bf16)
            more_k, more_v = dot(scores, q[here], 0, 0), dot(p[here], d_r[here], 0, 0)
            if i == 0:
                d_k[...], d_v[...] = more_k, more_v
            else:
                d_k[...] += more_k
                d_v[...] += more_v
        for i in tiles:
            here = rows_of(i)
            c, sn = cosine[here] * dk**-0.5, sine[here] * dk**-0.5
            a, b = d_k[here, :one], d_k[here, one:]
            own, other = in_order(x, a * c + b * sn, b * c - a * sn)
            d_pre[0, here, one:dk] = own.astype(bf16)
            d_pre[1, here, one:dk] = other.astype(bf16)
            d_pre[0, here, dk:] = d_v[here, :half].astype(bf16)
            d_pre[1, here, dk:] = d_v[here, half:].astype(bf16)
            back = []
            for t in (0, 1):
                part = dot(d_g[0, here], w[2 * t][:, cut:], 1, 1)
                part = part + dot(d_g[1, here], w[2 * t + 1][:, cut:], 1, 1)
                for j in (0, 1):
                    part = part + dot(d_pre[j, here], w[2 * t + j][:, :cut], 1, 1)
                back.append(part)
            back = jnp.concatenate(back, -1)
            put_tile(outs, i, back)
            parts = jnp.concatenate(
                [
                    jnp.sum(back * zs[i][...].astype(f32), axis=0, keepdims=True),
                    jnp.sum(back, axis=0, keepdims=True),
                ],
                0,
            )
            if i == 0:
                room[...] = parts
            else:
                room[...] += parts
        for start, columns in arranged(s):
            sums[:, columns] = room[:, start : start + half_depth]

    terms = term_shapes(rows, width)


    gains = jnp.stack([norm1_gain, norm1_bias, norm2_gain, norm2_bias])
    packed, tokens_late, gains_late, ffn_gate_late, ffn_up_late = after(
        fetch(w_query, w_key, w_value, w_gate), tokens, gains, w_ffn_gate, w_ffn_up
    )
    mix_own = trade(packed)
    ring = Gather(tokens_late)

    head = lax.axis_index("fsdp")
    gamma_log = jnp.log(1.0 - 2.0 ** (-5.0 - head.astype(f32)))
    positions = (owners() * rows)[:, None] + jnp.arange(rows, dtype=jnp.int32)[None, :]
    positions = positions.reshape(-1).astype(f32)
    half = dk // 2
    freqs = jnp.exp(-jnp.arange(half, dtype=f32) * (math.log(10000.0) / half))
    angles = positions[:, None] * freqs[None, :]
    cosine, sine = jnp.cos(angles), jnp.sin(angles)
    differ = positions[:, None] - positions[None, :]
    decay = jnp.where(differ >= 0, jnp.exp(jnp.maximum(differ, 0.0) * gamma_log), 0.0)

    def widen(value, place):
        other = swap(value, place)
        first = bit(place) == 0
        return jnp.concatenate([jnp.where(first, value, other), jnp.where(first, other, value)], 1)

    cosine, sine, decay, ffn_packed, mix_own, gains = ring.step(
        cosine, sine, decay, fetch(ffn_gate_late, ffn_up_late), mix_own, widen(gains_late, 0)
    )
    mix_other = swap(mix_own, X)
    mix_own_c = swap(mix_own, CORE)
    (gains,) = ring.step(widen(gains, 1))
    (gains,) = ring.step(widen(gains, 2))
    gains = gains.astype(f32)

    def norm_tile(*parts):
        return kernel(
            first_norm,
            [shape((2 * rows, width), bf16)],
            *parts, gains,
            scalars=where, scratch=[pltpu.VMEM((2 * rows, width), f32)],
        )[0]

    z0 = norm_tile(ring.own, ring.ahead[1])
    z2 = norm_tile(*ring.behind[1:3])
    z1 = norm_tile(*ring.ahead[2:4])
    z0, z1, z2, mix_other, mix_own_c = ring.step(z0, z1, z2, mix_other, mix_own_c)
    mix_other_c = swap(mix_other, CORE)
    z3 = norm_tile(ring.behind[3], ring.ahead[4], ring.behind[4])
    w_mix = (mix_own, mix_other, mix_own_c, mix_other_c)
    *w_mix, z0, z1, z2, z3, ffn_packed = after(*w_mix, z0, z1, z2, z3, ffn_packed)
    zs = (z0, z1, z2, z3)
    ffn_own = trade(ffn_packed)
    query, key, value, gate = kernel(
        project,
        [shape((every, dk), bf16)] * 2 + [shape((every, dv), bf16), shape((every, dv), f32)],
        *zs, *w_mix, cosine, sine,
        scalars=where, limit=LIMITS[0],
    )
    scores, retained, mixed, *parts = kernel(
        mix,
        [shape((every, every), bf16), shape((every, dv), f32), shape((every, dv), bf16)] + terms,
        query, key, value, decay, gate, w_out,
        scalars=where, limit=LIMITS[1],
    )
    ring = Scatter(parts)
    cot_late, ffn_own = ring.hold(cotangent, ffn_own)
    ffn_other = swap(ffn_own, X)
    ffn_own_c = swap(ffn_own, CORE)
    cot_ring = Gather(cot_late)
    ring.step()
    cot_ring.step()
    ring.step()
    cot_ring.step()
    ring.step()
    cot_ring.step()
    ring.step()
    resid, second = kernel(
        second_norm, [block_f32, block_bf16], *ring.pieces(), tokens, gains,
        scalars=where, scratch=room_of_block, limit=8,
    )

    ring = Gather(second)
    (ffn_other,) = ring.step(ffn_other)
    ffn_other_c = swap(ffn_other, CORE)
    ring.step()
    ring.step()
    cot_ring.step()
    w_ffn = ring.step(ffn_own, ffn_other, ffn_own_c, ffn_other_c)
    z_second, hidden, d_ab, *parts = kernel(
        feed,
        [shape((every, width), bf16), shape((every, ff), bf16), shape((2, every, ff), bf16)]
        + terms,
        *ring.pieces(), *cot_ring.pieces(), w_ffn_down, *w_ffn,
        scalars=where, limit=LIMITS[2],
    )
    ring = Scatter(parts)
    (cot_all,) = ring.step(
        *kernel(join_tiles, [shape((every, width), bf16)], *cot_ring.pieces(), limit=12)
    )
    grad_ffn = ring.step(*columns_grad(z_second, d_ab[0], d_ab[1]))
    ffn_kept, ffn_given = sum_cores(*grad_ffn)
    ffn_kept, ffn_given, down_kept, down_given = ring.step(
        ffn_kept, ffn_given, *rows_grad(hidden, cot_all)
    )
    ffn_sent = swap(ffn_given, X)
    down_kept, down_given = ring.step(*sum_cores_rows(down_kept, down_given))
    grad_resid, second_sums, part = kernel(
        second_back, [block_f32, pair_f32, block_bf16],
        *ring.pieces(), resid, cotangent, gains,
        scalars=where, scratch=room_of_block,
    )
    ring = Gather(part)
    ffn_kept, down_given = ring.step(ffn_kept, down_given)
    ffn_kept, ffn_sent, hidden_late = ring.step(ffn_kept, ffn_sent, hidden)
    down_sent = swap(down_given, X)
    last = Scatter(kernel(down, terms, hidden_late, w_ffn_down, scalars=where, limit=20))
    ffn_sum = more(ffn_kept + ffn_sent.astype(f32)).astype(bf16)
    (ffn_sum,) = ring.step(ffn_sum)
    a, b, down_sent, z_first = ring.step(*last.peek(), down_sent, jnp.concatenate(zs))
    last.put(a, b)

    ffn_owned = lax.all_to_all(
        ffn_sum.reshape(n, half_depth, ffn_sum.shape[-1]), "fsdp", 0, 0, tiled=True
    )
    out_kept, out_given, d_retained, d_gate = kernel(
        mix_back,
        [shape((2, dv // 4, width), bf16)] * 2
        + [shape((every, dv), bf16), shape((2, every, dv // 2), bf16)],
        *ring.pieces(), w_out, retained, gate, mixed,
        scalars=where, limit=LIMITS[3], scratch=[pltpu.VMEM((every, width), bf16)],
    )
    d_pre, first_sums, *parts = kernel(
        within_back,
        [shape((2, every, dk + dv // 2), bf16), pair_f32] + terms,
        d_retained, d_gate, query, key, value, scores, decay, cosine, sine, *w_mix, *zs,
        scalars=where, limit=LIMITS[4],
        scratch=[
            pltpu.VMEM((every, dk), f32),
            pltpu.VMEM((every, dv), f32),
            pltpu.VMEM((2, width), f32),
        ],
    )
    ring = Scatter(parts)
    stack = jnp.concatenate([first_sums, second_sums])
    *grad_gate, out_kept, out_given, stack_c, ffn_owned = ring.step(
        *columns_grad(z_first, d_gate[0], d_gate[1]), out_kept, out_given,
        swap(stack, CORE), ffn_owned,
    )
    stack = stack + stack_c
    gate_kept, gate_given = sum_cores(*grad_gate)
    grad_qkv = columns_grad(z_first, d_pre[0], d_pre[1])
    gate_sent = swap(gate_given, X)
    out_kept, out_given = sum_cores_rows(out_kept, out_given)
    down_owned = give_rows(down_kept, down_sent)
    a, b, gate_sent, *grad_qkv, out_given, stack_c = ring.step(
        *last.peek(), gate_sent, *grad_qkv, out_given, swap(stack, X)
    )
    last.put(a, b)
    stack = stack + stack_c
    for place in range(X + 1, bits()):
        stack = stack + swap(stack, place)
    qkv_kept, qkv_given = sum_cores(*grad_qkv)
    qkv_sent = swap(qkv_given, X)
    gate_owned = give(gate_kept, gate_sent)
    gate_owned, qkv_sent, stack_c = ring.step(gate_owned, qkv_sent, swap(stack, 0))
    stack = stack + stack_c
    qkv_owned = give(qkv_kept, qkv_sent)
    out_sent = swap(out_given, X)
    a, b, qkv_owned, out_sent, stack_c = ring.step(
        *last.peek(), qkv_owned, out_sent, swap(stack, 1)
    )
    last.put(a, b)
    stack = stack + stack_c
    qkv_all = everywhere(qkv_owned)
    grad_tokens = kernel(
        first_back, [block_f32], *ring.pieces(), tokens, grad_resid, gains,
        scalars=where, scratch=room_of_block,
    )[0]
    out_owned = give_rows(out_kept, out_sent)
    gate_all = everywhere(gate_owned)
    ffn_all = everywhere(ffn_owned)
    down_all = everywhere(down_owned)
    out_all = everywhere(out_owned)
    (stack_c,) = last.step(swap(stack, 2))
    stack = lax.dynamic_slice_in_dim(stack + stack_c, head * depth, depth, 1)
    first_gain = (stack[0] - norm1_bias.astype(f32) * stack[1]) / norm1_gain.astype(f32)
    (output,) = kernel(last_sum, [block_bf16], *last.pieces(), resid)
    grad_ffn_gate, grad_ffn_up = flat(ffn_all, [ff, ff])
    grad_down = flat_rows(down_all)
    (grad_gate,) = flat(gate_all, [dv])
    grad_query, grad_key, grad_value = flat(qkv_all, [dk, dk, dv])
    grad_out = flat_rows(out_all)

    return (
        output,
        grad_tokens,
        grad_query,
        grad_key,
        grad_value,
        grad_gate,
        grad_out,
        first_gain,
        stack[1],
        grad_ffn_gate,
        grad_ffn_up,
        grad_down,
        stack[2],
        stack[3],
    )


def solution(mesh):
    tokens = P(("rep", "fsdp"), None)
    matrix = P("fsdp", None)
    vector = P("fsdp")
    in_specs = (tokens,) + (matrix,) * 5 + (vector,) * 2 + (matrix,) * 3 + (vector,) * 2 + (tokens,)
    out_specs = (tokens,) * 2 + (matrix,) * 5 + (vector,) * 2 + (matrix,) * 3 + (vector,) * 2
    return jax.shard_map(
        on_device, mesh=mesh, in_specs=in_specs, out_specs=out_specs, check_vma=False
    )
```

```python
import math

import jax
import jax.numpy as jnp
from jax import lax
from jax.experimental import pallas as pl
from jax.experimental.pallas import tpu as pltpu
from jax.sharding import PartitionSpec as P

HEADS = 8
epsilon = 1e-05
head_epsilon = 1.0
f32 = jnp.float32
bf16 = jnp.bfloat16
BOTH = ("rep", "fsdp")
CORE, X = 3, 4
LIMITS = (52, 30, 38, 30, 56, 24)


def dot(a, b, ca=1, cb=0, kind=f32):
    return lax.dot_general(a, b, (((ca,), (cb,)), ((), ())), preferred_element_type=kind)


def after(*values):
    return lax.optimization_barrier(values)


def shape(dims, kind):
    return jax.ShapeDtypeStruct(tuple(dims), kind)


def block(dims, *index):
    return pl.BlockSpec(dims, lambda *_: index)


def kernel(body, outs, *ins, scalars=None, scratch=(), limit=8):
    whole = pl.BlockSpec(memory_space=pltpu.VMEM)
    grid = (1,) if any(isinstance(i, tuple) for i in ins) else ()
    specs = [i[1] if isinstance(i, tuple) else whole for i in ins]
    ins = [i[0] if isinstance(i, tuple) else i for i in ins]
    if scalars is not None:
        specs = [pl.BlockSpec(memory_space=pltpu.SMEM)] + specs
        ins = [scalars] + ins
    return pl.pallas_call(
        body,
        out_shape=list(outs),
        grid=grid,
        in_specs=specs,
        out_specs=[whole] * len(outs),
        scratch_shapes=list(scratch),
        compiler_params=pltpu.CompilerParams(vmem_limit_bytes=limit << 20),
        cost_estimate=pl.CostEstimate(flops=0, bytes_accessed=0, transcendentals=0),
    )(*ins)


def streamed(body, outs, *ins, scalars=None, scratch=(), limit=8, late=(), stream=()):
    whole = pl.BlockSpec(memory_space=pltpu.VMEM)
    away = pl.BlockSpec(memory_space=pltpu.HBM)
    first = 0 if scalars is None else 1
    n_in, n_out, n_own = len(ins), len(outs), len(scratch)
    late, stream = list(late), list(stream)
    pushes = len(stream)

    def run(*refs):
        given, refs = refs[:first], refs[first:]
        ins, refs = list(refs[:n_in]), refs[n_in:]
        outs, refs = list(refs[:n_out]), refs[n_out:]
        own, refs = refs[:n_own], refs[n_own:]
        rooms, refs = refs[: len(late)], refs[len(late) :]
        stages, refs = refs[: len(stream)], refs[len(stream) :]
        comes, goes = refs
        arrivals, departures = {}, []
        for k, (i, room) in enumerate(zip(late, rooms)):
            arrivals[i] = pltpu.make_async_copy(ins[i], room, comes.at[k])
            arrivals[i].start()
            ins[i] = room
        targets = {}
        for i, stage in zip(stream, stages):
            targets[i], outs[i] = outs[i], stage

        def ready(*numbers):
            for i in numbers:
                arrivals.pop(i).wait()

        def push(i, *index):
            source, target = outs[i], targets[i]
            if index:
                source, target = source.at[index], target.at[index]
            copy = pltpu.make_async_copy(source, target, goes.at[len(departures)])
            copy.start()
            departures.append(copy)

        more = {}
        if late:
            more["ready"] = ready
        if stream:
            more["push"] = push
        body(*given, *ins, *outs, *own, **more)
        for copy in departures:
            copy.wait()

    specs = [away if i in late else whole for i in range(n_in)]
    if scalars is not None:
        specs = [pl.BlockSpec(memory_space=pltpu.SMEM)] + specs
    rooms = [pltpu.VMEM(ins[i].shape, ins[i].dtype) for i in late]
    stages = [pltpu.VMEM(outs[i].shape, outs[i].dtype) for i in stream]
    sems = [pltpu.SemaphoreType.DMA((max(len(late), 1),)), pltpu.SemaphoreType.DMA((pushes,))]
    return pl.pallas_call(
        run,
        out_shape=list(outs),
        in_specs=specs,
        out_specs=[away if i in stream else whole for i in range(n_out)],
        scratch_shapes=[*scratch, *rooms, *stages, *sems],
        compiler_params=pltpu.CompilerParams(vmem_limit_bytes=limit << 20),
        cost_estimate=pl.CostEstimate(flops=0, bytes_accessed=0, transcendentals=0),
    )(*(() if scalars is None else (scalars,)), *ins)


def number():
    return lax.axis_index("rep") * lax.axis_size("fsdp") + lax.axis_index("fsdp")


def bit(place):
    return (number() >> place) & 1


def bits():
    return (lax.axis_size("rep") * lax.axis_size("fsdp")).bit_length() - 1


def swap(value, place):
    count = 1 << bits()
    return lax.ppermute(value, BOTH, [(i, i ^ (1 << place)) for i in range(count)])


RING = (0, 2, 4, 6, 7, 5, 3, 1)
OFFSETS = (0, -1, -2, -3, 1, 2, 3, 4)


def owners():
    place = jnp.array([RING.index(i) for i in range(HEADS)], jnp.int32)[lax.axis_index("fsdp")]
    return jnp.array(RING, jnp.int32)[(place + jnp.array(OFFSETS, jnp.int32)) % HEADS]


def send(value, ahead):
    pairs = [(RING[i], RING[(i + 1) % HEADS]) for i in range(HEADS)]
    return lax.ppermute(value, "fsdp", pairs if ahead else [(b, a) for a, b in pairs])


class Gather:
    def __init__(self, own):
        self.own, self.ahead, self.behind = own, [own], [own]

    def peek(self):
        a, b = self.ahead[-1], self.behind[-1]
        if len(self.ahead) == 4:
            rows = a.shape[0] // 2
            a, b = a[:rows], b[rows:]
        return send(a, True), send(b, False)

    def put(self, a, b):
        self.ahead.append(a)
        self.behind.append(b)

    def step(self, *others):
        a, b, *others = after(*self.peek(), *others)
        self.put(a, b)
        return others

    def hold(self, *others):
        self.ahead[-1], self.behind[-1], *others = after(self.ahead[-1], self.behind[-1], *others)
        return others

    def pieces(self):
        return (self.own, *self.ahead[1:4], *self.behind[1:4], self.ahead[4], self.behind[4])


def tile(refs, i):
    names = ((0, 1), (2, 3), (4, 5), (6, 7, 8))[i]
    return jnp.concatenate([refs[j][...] for j in names], 0)


def term_shapes(rows, width):
    return [shape((7 * rows, width), bf16)] + [shape((rows // 2, width), bf16)] * 2


def put_tile(refs, i, values):
    both = values.shape[0]
    rows = both // 2
    values = values.astype(bf16)
    if i < 3:
        refs[0][i * both : (i + 1) * both] = values
    else:
        refs[0][3 * both : 3 * both + rows] = values[:rows]
        refs[1][...] = values[rows : rows + rows // 2]
        refs[2][...] = values[rows + rows // 2 :]


class Scatter:
    def __init__(self, terms):
        self.terms, self.a, self.b = terms
        self.steps = 0

    def term(self, offset):
        rows, width = self.terms.shape[0] // 7, self.terms.shape[1]
        return self.terms, block((rows, width), OFFSETS.index(offset), 0)

    def peek(self):
        if self.steps:
            self.fold(4 - self.steps)
        self.steps += 1
        return send(self.a, True), send(self.b, False)

    def put(self, a, b):
        self.a, self.b = a, b

    def step(self, *others):
        a, b, *others = after(*self.peek(), *others)
        self.put(a, b)
        return others

    def hold(self, *others):
        self.a, self.b, *others = after(self.a, self.b, *others)
        return others

    def fold(self, offset):
        rows, width = self.terms.shape[0] // 7, self.terms.shape[1]
        half = rows // 2

        def body(term_a, term_b, a, b, out_a, out_b):
            if a.shape[0] == rows:
                out_a[...] = (term_a[...].astype(f32) + a[...].astype(f32)).astype(bf16)
                out_b[...] = (term_b[...].astype(f32) + b[...].astype(f32)).astype(bf16)
            else:
                out_a[:half] = (term_a[:half].astype(f32) + a[...].astype(f32)).astype(bf16)
                out_a[half:] = term_a[half:]
                out_b[:half] = term_b[:half]
                out_b[half:] = (term_b[half:].astype(f32) + b[...].astype(f32)).astype(bf16)

        self.a, self.b = kernel(
            body,
            [shape((rows, width), bf16)] * 2,
            self.term(offset), self.term(-offset), self.a, self.b,
            limit=8,
        )

    def pieces(self):
        return self.term(0), self.a, self.b


def total(refs):
    return refs[0][...].astype(f32) + refs[1][...].astype(f32) + refs[2][...].astype(f32)


def normalize(values):
    center = values - jnp.mean(values, axis=-1, keepdims=True)
    scale = lax.rsqrt(jnp.mean(center * center, axis=-1, keepdims=True) + epsilon)
    return center * scale, scale


def normalize_back(normed, scale, grad):
    return scale * (
        grad
        - jnp.mean(grad, axis=-1, keepdims=True)
        - normed * jnp.mean(grad * normed, axis=-1, keepdims=True)
    )


def head_norm(values):
    center = values - jnp.mean(values, axis=-1, keepdims=True)
    scale = lax.rsqrt(jnp.mean(center * center, axis=-1, keepdims=True) + head_epsilon)
    return center * scale, scale


def on_device(
    tokens,
    w_query,
    w_key,
    w_value,
    w_gate,
    w_out,
    norm1_gain,
    norm1_bias,
    w_ffn_gate,
    w_ffn_up,
    w_ffn_down,
    norm2_gain,
    norm2_bias,
    cotangent,
):
    n = lax.axis_size("fsdp")
    assert n == HEADS
    rows, width = tokens.shape
    depth = w_query.shape[0]
    half_depth = depth // 2
    dk = w_query.shape[1] // n
    dv = w_value.shape[1] // n
    ff = w_ffn_gate.shape[1] // n
    every = n * rows
    half_width = width // 2
    where = jnp.stack([bit(CORE), bit(X)])


    def fetch(*weights):
        sizes = [w.shape[1] // n // 2 for w in weights]
        whole = sum(sizes)

        def body(s, *refs):
            for h in range(4):
                start = 0
                for ref, size in zip(refs, sizes):
                    place = pl.multiple_of((2 * h + s[1]) * size, size)
                    refs[-1][h, :, start : start + size] = ref[:, pl.ds(place, size)]
                    start += size

        packed = pl.pallas_call(
            body,
            out_shape=shape((n, half_depth, whole), bf16),
            grid_spec=pltpu.PrefetchScalarGridSpec(
                num_scalar_prefetch=1,
                grid=(n // 4,),
                in_specs=[
                    pl.BlockSpec((half_depth, 8 * size), lambda k, s: (s[0], k)) for size in sizes
                ],
                out_specs=pl.BlockSpec((4, half_depth, whole), lambda k, s: (k, 0, 0)),
            ),
            compiler_params=pltpu.CompilerParams(vmem_limit_bytes=60 << 20),
            cost_estimate=pl.CostEstimate(flops=0, bytes_accessed=0, transcendentals=0),
        )(where, *weights)
        return packed

    def trade(packed):
        got = lax.all_to_all(packed, "fsdp", 0, 0, tiled=True)
        return got.reshape(n * half_depth, got.shape[-1])

    def more(value):
        for place in range(X + 1, bits()):
            value = value + swap(value.astype(bf16), place).astype(f32)
        return value

    def columns_grad(z, halves_of):
        size = halves_of.shape[-1]

        def body(z, parts, *outs):
            for j in (1, 0):
                for t in (1, 0):
                    rows_t = z[:, t * half_width : (t + 1) * half_width]
                    outs[2 * j + t][...] = dot(rows_t, parts[j], 0, 0).astype(bf16)

        return kernel(body, [shape((half_width, size), bf16)] * 4, z, halves_of, limit=LIMITS[5])

    def sum_cores(own, own_t, other, other_t):
        given = other.astype(f32) + swap(other_t, CORE).astype(f32)
        return own, swap(own_t, CORE), given.astype(bf16)

    def sum_x(own, own_c, got):
        return more(own.astype(f32) + own_c.astype(f32) + got.astype(f32)).astype(bf16)

    def give(grad):
        grad = grad.reshape(n, half_depth, grad.shape[-1])
        return lax.all_to_all(grad, "fsdp", 0, 0, tiled=True)

    def everywhere(own, other):
        return own, swap(own, CORE), other, swap(other, CORE)

    def flat(pieces, sizes):
        whole = sum(sizes) // 2

        def body(s, own, own_c, other, other_c, *outs):
            here = pl.ds(s[0] * half_depth, half_depth)
            there = pl.ds((1 - s[0]) * half_depth, half_depth)
            for h in (0, 1):
                start = 0
                for out, size in zip(outs, sizes):
                    half = size // 2
                    columns = slice(start, start + half)
                    for x, a, b in ((s[1], own, own_c), (1 - s[1], other, other_c)):
                        place = pl.ds(pl.multiple_of(x * half, half) + h * size, half)
                        out[here, place] = a[h, :, columns].astype(f32)
                        out[there, place] = b[h, :, columns].astype(f32)
                    start += half

        return pl.pallas_call(
            body,
            out_shape=[shape((depth, n * size), f32) for size in sizes],
            grid_spec=pltpu.PrefetchScalarGridSpec(
                num_scalar_prefetch=1,
                grid=(n // 2,),
                in_specs=[pl.BlockSpec((2, half_depth, whole), lambda k, s: (k, 0, 0))] * 4,
                out_specs=[pl.BlockSpec((depth, 2 * size), lambda k, s: (0, k)) for size in sizes],
            ),
            compiler_params=pltpu.CompilerParams(vmem_limit_bytes=24 << 20),
            cost_estimate=pl.CostEstimate(flops=0, bytes_accessed=0, transcendentals=0),
        )(where, *pieces)


    def rows_products(s, left, right, kept, given):
        size = left.shape[1] // 4
        for out, c in ((kept, s[0]), (given, 1 - s[0])):
            for i in (0, 1):
                columns = pl.ds(pl.multiple_of((2 * i + c) * size, size), size)
                out[i] = dot(left[:, columns], right[...], 0, 0).astype(bf16)

    def rows_grad(left, right):
        return kernel(
            rows_products, [shape((2, left.shape[1] // 4, right.shape[1]), bf16)] * 2, left, right,
            scalars=where, limit=14,
        )

    def sum_cores_rows(kept, given):
        grad = kept.astype(f32) + swap(given, CORE).astype(f32)
        return grad[0], grad[1].astype(bf16)

    def give_rows(kept, got):
        return more(kept + got.astype(f32)).astype(bf16)

    def flat_rows(pieces):
        size = pieces[0].shape[0]

        def body(s, own, own_c, other, other_c, out):
            for x, a, b in ((s[1], own, own_c), (1 - s[1], other, other_c)):
                out[pl.ds((2 * x + s[0]) * size, size), :] = a[...].astype(f32)
                out[pl.ds((2 * x + 1 - s[0]) * size, size), :] = b[...].astype(f32)

        (out,) = kernel(
            body, [shape((4 * size, pieces[0].shape[1]), f32)], *pieces, scalars=where, limit=8
        )
        return out


    def arranged(s):
        for i in range(2 * n):
            column = ((i % n) * 2 + (s[0] ^ (i // n))) * half_depth
            yield i * half_depth, pl.ds(pl.multiple_of(column, half_depth), half_depth)

    block_f32 = shape((rows, width), f32)
    block_bf16 = shape((rows, width), bf16)
    pair_f32 = shape((2, width), f32)
    room_of_block = [pltpu.VMEM((rows, width), f32)]

    def second_norm(s, *refs):
        sums, (tokens, gains, resid, z, room) = refs[:3], refs[3:]
        value = tokens[...].astype(f32) + total(sums)
        resid[...] = value
        normed, _ = normalize(value)
        room[...] = normed * gains[2:3] + gains[3:4]
        for start, columns in arranged(s):
            z[:, start : start + half_depth] = room[:, columns].astype(bf16)

    def norm_back(s, refs, inputs, gain, room, sums=None):
        grad = total(refs)
        for start, columns in arranged(s):
            room[:, columns] = grad[:, start : start + half_depth]
        grad = room[...]
        normed, scale = normalize(inputs)
        if sums is not None:
            sums[0:1] = jnp.sum(grad * normed, axis=0, keepdims=True)
            sums[1:2] = jnp.sum(grad, axis=0, keepdims=True)
        return normalize_back(normed, scale, grad * gain)

    def second_back(s, *refs):
        parts, (resid, cot, gains, grad_resid, sums, out, room) = refs[:3], refs[3:]
        grad = norm_back(s, parts, resid[...], gains[2:3], room, sums)
        grad = grad + cot[...].astype(f32)
        grad_resid[...] = grad
        out[...] = grad.astype(bf16)

    def first_back(s, *refs):
        parts, (tokens, grad_resid, gains, out, room) = refs[:3], refs[3:]
        grad = norm_back(s, parts, tokens[...].astype(f32), gains[0:1], room)
        out[...] = grad_resid[...] + grad

    def last_sum(*refs):
        parts, resid, out = refs[:3], refs[3], refs[4]
        out[...] = (resid[...] + total(parts)).astype(bf16)


    tiles = range(4)
    halves = (slice(0, half_width), slice(half_width, width))

    def rows_of(i):
        return slice(2 * i * rows, 2 * (i + 1) * rows)

    def in_order(x, own, other):
        first = jnp.where(x == 0, own, other)
        second = jnp.where(x == 0, other, own)
        return first, second

    def of_x(ref, x, size):
        return [ref[pl.ds(pl.multiple_of(i * size, size), size), :] for i in (x, 1 - x)]

    def mixer(s, *refs, ready, push):
        pieces, gains, w, (cosine, sine, decay, w_out), refs = (
            refs[:9], refs[9], refs[10:14], refs[14:18], refs[18:]
        )
        z, q, k, v, g, p, retained, mixed, *outs, room = refs
        x = s[1]
        one, half, middle = dk // 2, dv // 2, dk + dv // 2
        for i in tiles:
            normed, _ = normalize(tile(pieces, i).astype(f32))
            room[...] = normed * gains[0:1] + gains[1:2]
            for start, columns in arranged(s):
                z[rows_of(i), start : start + half_depth] = room[:, columns].astype(bf16)
        push(0)
        ready(10, 11, 12, 13, 14, 15)
        for i in tiles:
            here = rows_of(i)
            own, other = (
                dot(z[here, halves[0]], w[j][...]) + dot(z[here, halves[1]], w[2 + j][...])
                for j in (0, 1)
            )
            c, sn = cosine[here], sine[here]
            a, b = in_order(x, own[:, :one], other[:, :one])
            q[here, :one] = (a * c - b * sn).astype(bf16)
            q[here, one:] = (b * c + a * sn).astype(bf16)
            a, b = in_order(x, own[:, one:dk], other[:, one:dk])
            k[here, :one] = ((a * c - b * sn) * dk**-0.5).astype(bf16)
            k[here, one:] = ((b * c + a * sn) * dk**-0.5).astype(bf16)
            v[here, :half] = own[:, dk:middle].astype(bf16)
            v[here, half:] = other[:, dk:middle].astype(bf16)
            g[here, :half] = own[:, middle:]
            g[here, half:] = other[:, middle:]
        for i in (1, 2, 3, 4):
            push(i)
        ready(16, 17)
        for i in tiles:
            here = rows_of(i)
            scores = (dot(q[here], k[...], 1, 1) * decay[here]).astype(bf16)
            p[here] = scores
            value = dot(scores, v[...])
            retained[here] = value
            normed, _ = head_norm(value)
            gate = g[here]
            part = (normed * gate / (1.0 + jnp.exp(-gate))).astype(bf16)
            mixed[here] = part
            own, other = of_x(w_out, x, half)
            put_tile(outs, i, dot(part[:, :half], own) + dot(part[:, half:], other))
        for i in (9, 10, 8, 5, 6, 7):
            push(i)

    def join_tiles(*refs):
        for i in tiles:
            refs[9][rows_of(i)] = tile(refs, i)

    def feed(s, *refs):
        pieces, cots, w_down, w = refs[:9], refs[9:18], refs[18], refs[19:23]
        (z, hidden, grad), outs = refs[23:26], refs[26:]
        half = ff // 2
        for i in tiles:
            here = rows_of(i)
            part = tile(pieces, i)
            z[here] = part
            cot = tile(cots, i)
            downs = of_x(w_down, s[1], half)
            back = 0.0
            for j in (0, 1):
                ab = dot(part[:, halves[0]], w[j][...]) + dot(part[:, halves[1]], w[2 + j][...])
                a, b = ab[:, :half], ab[:, half:]
                below = 0.5 * (1.0 + lax.erf(a * math.sqrt(0.5)))
                gelu = a * below
                slope = below + a * jnp.exp(-0.5 * a * a) * (1.0 / math.sqrt(2.0 * math.pi))
                columns = slice(j * half, (j + 1) * half)
                hidden[here, columns] = (gelu * b).astype(bf16)
                d = dot(cot, downs[j], 1, 1).astype(bf16).astype(f32)
                both = jnp.concatenate([d * b * slope, d * gelu], -1).astype(bf16)
                grad[j, here] = both
                back = back + jnp.concatenate(
                    [dot(both, w[j][...], 1, 1), dot(both, w[2 + j][...], 1, 1)], -1
                )
            put_tile(outs, i, back)

    def down(s, h, w, *outs):
        half = ff // 2
        for i in tiles:
            here = rows_of(i)
            own, other = of_x(w, s[1], half)
            put_tile(outs, i, dot(h[here, :half], own) + dot(h[here, half:], other))

    def mixer_back(s, *refs, ready, push):
        pieces, (w_out, r, g, mixed, q, k, v, p, decay, cosine, sine), w, z = (
            refs[:9], refs[9:20], refs[20:24], refs[24]
        )
        kept, given, sums, d_pre, *outs = refs[25:32]
        d_out, d_r, d_k, d_v, room = refs[32:]
        one, half = dk // 2, dv // 2
        cut = dk + half
        x = s[1]
        ready(9, 10, 11)
        for i in tiles:
            here = rows_of(i)
            part = tile(pieces, i)
            d_out[here] = part
            own, other = of_x(w_out, x, half)
            d_mixed = jnp.concatenate([dot(part, own, 1, 1), dot(part, other, 1, 1)], -1)
            d_mixed = d_mixed.astype(bf16).astype(f32)
            normed, scale = head_norm(r[here])
            gate = g[here]
            sigmoid = 1.0 / (1.0 + jnp.exp(-gate))
            both = (d_mixed * normed * sigmoid * (1.0 + gate * (1.0 - sigmoid))).astype(bf16)
            d_pre[0, here, cut:], d_pre[1, here, cut:] = both[:, :half], both[:, half:]
            d_r[here] = normalize_back(normed, scale, d_mixed * gate * sigmoid).astype(bf16)
        ready(12)
        rows_products(s, mixed, d_out, kept, given)
        push(0)
        push(1)
        ready(13, 14, 15, 16, 17, 18, 19)
        for i in tiles:
            here = rows_of(i)
            scores = (dot(d_r[here], v[...], 1, 1) * decay[here]).astype(bf16)
            c, sn = cosine[here], sine[here]
            grad = dot(scores, k[...])
            a, b = grad[:, :one], grad[:, one:]
            own, other = in_order(x, a * c + b * sn, b * c - a * sn)
            d_pre[0, here, :one] = own.astype(bf16)
            d_pre[1, here, :one] = other.astype(bf16)
            more_k, more_v = dot(scores, q[here], 0, 0), dot(p[here], d_r[here], 0, 0)
            if i == 0:
                d_k[...], d_v[...] = more_k, more_v
            else:
                d_k[...] += more_k
                d_v[...] += more_v
        for i in tiles:
            here = rows_of(i)
            c, sn = cosine[here] * dk**-0.5, sine[here] * dk**-0.5
            a, b = d_k[here, :one], d_k[here, one:]
            own, other = in_order(x, a * c + b * sn, b * c - a * sn)
            d_pre[0, here, one:dk] = own.astype(bf16)
            d_pre[1, here, one:dk] = other.astype(bf16)
            d_pre[0, here, dk:cut] = d_v[here, :half].astype(bf16)
            d_pre[1, here, dk:cut] = d_v[here, half:].astype(bf16)
        push(3)
        ready(20, 21, 22, 23, 24)
        for i in tiles:
            here = rows_of(i)
            back = [
                dot(d_pre[0, here], w[2 * t][...], 1, 1)
                + dot(d_pre[1, here], w[2 * t + 1][...], 1, 1)
                for t in (0, 1)
            ]
            back = jnp.concatenate(back, -1)
            put_tile(outs, i, back)
            parts = jnp.concatenate(
                [
                    jnp.sum(back * z[here].astype(f32), axis=0, keepdims=True),
                    jnp.sum(back, axis=0, keepdims=True),
                ],
                0,
            )
            if i == 0:
                room[...] = parts
            else:
                room[...] += parts
        for i in (5, 6, 4):
            push(i)
        for start, columns in arranged(s):
            sums[:, columns] = room[:, start : start + half_depth]

    terms = term_shapes(rows, width)


    packed, tokens_late, ffn_gate_late, ffn_up_late, *gains_late = after(
        fetch(w_query, w_key, w_value, w_gate), tokens, w_ffn_gate, w_ffn_up,
        norm1_gain, norm1_bias, norm2_gain, norm2_bias,
    )
    gains_late = jnp.stack(gains_late)
    mix_own = trade(packed)
    ring = Gather(tokens_late)

    head = lax.axis_index("fsdp")
    gamma_log = jnp.log(1.0 - 2.0 ** (-5.0 - head.astype(f32)))
    positions = (owners() * rows)[:, None] + jnp.arange(rows, dtype=jnp.int32)[None, :]
    positions = positions.reshape(-1).astype(f32)
    half = dk // 2
    freqs = jnp.exp(-jnp.arange(half, dtype=f32) * (math.log(10000.0) / half))
    angles = positions[:, None] * freqs[None, :]
    cosine, sine = jnp.cos(angles), jnp.sin(angles)
    differ = positions[:, None] - positions[None, :]
    decay = jnp.where(differ >= 0, jnp.exp(jnp.maximum(differ, 0.0) * gamma_log), 0.0)

    def widen(value, place):
        other = swap(value, place)
        first = bit(place) == 0
        return jnp.concatenate([jnp.where(first, value, other), jnp.where(first, other, value)], 1)

    cosine, sine, decay, ffn_packed, mix_own, gains = ring.step(
        cosine, sine, decay, fetch(ffn_gate_late, ffn_up_late), mix_own, widen(gains_late, 0)
    )
    mix_other = swap(mix_own, X)
    mix_own_c = swap(mix_own, CORE)
    (gains,) = ring.step(widen(gains, 1))
    (gains,) = ring.step(widen(gains, 2))
    gains = gains.astype(f32)

    mix_other, mix_own_c, ffn_packed = ring.step(mix_other, mix_own_c, ffn_packed)
    mix_other_c = swap(mix_other, CORE)
    w_mix = (mix_own, mix_other, mix_own_c, mix_other_c)
    ffn_own = trade(ffn_packed)
    z_first, query, key, value, gate, scores, retained, mixed, *parts = streamed(
        mixer,
        [shape((every, width), bf16)]
        + [shape((every, dk), bf16)] * 2
        + [shape((every, dv), bf16), shape((every, dv), f32), shape((every, every), bf16)]
        + [shape((every, dv), f32), shape((every, dv), bf16)]
        + terms,
        *ring.pieces(), gains, *w_mix, cosine, sine, decay, w_out,
        scalars=where, limit=LIMITS[0], late=range(10, 18), stream=range(11),
        scratch=[pltpu.VMEM((2 * rows, width), f32)],
    )
    ring = Scatter(parts)
    cot_late = ring.hold(cotangent)[0]
    cot_ring = Gather(cot_late)
    (ffn_own,) = ring.step(ffn_own)
    ffn_other = swap(ffn_own, X)
    ffn_own_c = swap(ffn_own, CORE)
    cot_ring.step()
    ring.step()
    cot_ring.step()
    ring.step()
    cot_ring.step()
    ring.step()
    resid, second = kernel(
        second_norm, [block_f32, block_bf16], *ring.pieces(), tokens, gains,
        scalars=where, scratch=room_of_block, limit=8,
    )

    ring = Gather(second)
    (ffn_other,) = ring.step(ffn_other)
    ffn_other_c = swap(ffn_other, CORE)
    ring.step()
    ring.step()
    cot_ring.step()
    w_ffn = ring.step(ffn_own, ffn_other, ffn_own_c, ffn_other_c)
    z_second, hidden, d_ab, *parts = kernel(
        feed,
        [shape((every, width), bf16), shape((every, ff), bf16), shape((2, every, ff), bf16)]
        + terms,
        *ring.pieces(), *cot_ring.pieces(), w_ffn_down, *w_ffn,
        scalars=where, limit=LIMITS[2],
    )
    ring = Scatter(parts)
    (cot_all,) = ring.step(
        *kernel(join_tiles, [shape((every, width), bf16)], *cot_ring.pieces(), limit=12)
    )
    grad_ffn = ring.step(*columns_grad(z_second, d_ab))
    ffn_own, ffn_own_c, ffn_given = sum_cores(*grad_ffn)
    ffn_own, ffn_own_c, ffn_given, down_kept, down_given = ring.step(
        ffn_own, ffn_own_c, ffn_given, *rows_grad(hidden, cot_all)
    )
    ffn_sent = swap(ffn_given, X)
    down_kept, down_given = ring.step(*sum_cores_rows(down_kept, down_given))
    grad_resid, second_sums, part = kernel(
        second_back, [block_f32, pair_f32, block_bf16],
        *ring.pieces(), resid, cotangent, gains,
        scalars=where, scratch=room_of_block,
    )
    ring = Gather(part)
    ffn_own, ffn_sent, down_given = ring.step(ffn_own, ffn_sent, down_given)
    down_sent = swap(down_given, X)
    ffn_sum = sum_x(ffn_own, ffn_own_c, ffn_sent)
    ring.step()
    last = Scatter(kernel(down, terms, hidden, w_ffn_down, scalars=where, limit=20))
    (down_sent,) = ring.step(down_sent)
    down_owned = give_rows(down_kept, down_sent)
    a, b, down_owned, ffn_sum = ring.step(*last.peek(), down_owned, ffn_sum)
    last.put(a, b)

    ffn_owned = give(ffn_sum)
    down_other = swap(down_owned, X)
    out_kept, out_given, first_sums, d_pre, *parts = streamed(
        mixer_back,
        [shape((2, dv // 4, width), bf16)] * 2
        + [pair_f32, shape((2, every, dk + dv), bf16)]
        + terms,
        *ring.pieces(), w_out, retained, gate, mixed,
        query, key, value, scores, decay, cosine, sine, *w_mix, z_first,
        scalars=where, limit=LIMITS[4], late=range(9, 25), stream=(0, 1, 3, 4, 5, 6),
        scratch=[
            pltpu.VMEM((every, width), bf16),
            pltpu.VMEM((every, dv), bf16),
            pltpu.VMEM((every, dk), f32),
            pltpu.VMEM((every, dv), f32),
            pltpu.VMEM((2, width), f32),
        ],
    )
    out_kept, out_given, first_sums, d_pre, ffn_owned, *parts = after(
        out_kept, out_given, first_sums, d_pre, ffn_owned, *parts
    )
    ring = Scatter(parts)
    stack = jnp.concatenate([first_sums, second_sums])
    mix_own, mix_own_c, mix_given = sum_cores(*columns_grad(z_first, d_pre))
    out_kept, out_given = sum_cores_rows(out_kept, out_given)
    mix_own, mix_own_c, mix_given, out_kept, out_given, stack_c = ring.step(
        mix_own, mix_own_c, mix_given, out_kept, out_given, swap(stack, X)
    )
    stack = stack + stack_c
    for place in range(X + 1, bits()):
        stack = stack + swap(stack, place)
    mix_sent = swap(mix_given, X)
    stack_c, down_other = ring.step(swap(stack, CORE), down_other)
    stack = stack + stack_c
    out_sent = swap(out_given, X)
    (stack_c,) = ring.step(swap(stack, 0))
    stack = stack + stack_c
    mix_sent, stack_c = ring.step(mix_sent, swap(stack, 1))
    stack = stack + stack_c
    mix_owned = give(sum_x(mix_own, mix_own_c, mix_sent))
    out_owned = give_rows(out_kept, out_sent)
    ffn_other, out_other = swap(ffn_owned, X), swap(out_owned, X)
    grad_tokens = kernel(
        first_back, [block_f32], *ring.pieces(), tokens, grad_resid, gains,
        scalars=where, scratch=room_of_block,
    )[0]
    grad_down = flat_rows(everywhere(down_owned, down_other))
    a, b, mix_owned, stack_c, ffn_other, out_other, grad_tokens, grad_down = after(
        *last.peek(), mix_owned, swap(stack, 2), ffn_other, out_other, grad_tokens, grad_down
    )
    last.put(a, b)
    stack = lax.dynamic_slice_in_dim(stack + stack_c, head * depth, depth, 1)
    first_gain = (stack[0] - norm1_bias.astype(f32) * stack[1]) / norm1_gain.astype(f32)
    mix_other = swap(mix_owned, X)
    grad_ffn_gate, grad_ffn_up = flat(everywhere(ffn_owned, ffn_other), [ff, ff])
    grad_out = flat_rows(everywhere(out_owned, out_other))
    last.put(*last.peek())
    a, b, mix_other, grad_ffn_gate, grad_ffn_up, grad_out = after(
        last.a, last.b, mix_other, grad_ffn_gate, grad_ffn_up, grad_out
    )
    last.put(a, b)
    mix_grads = last.step(*flat(everywhere(mix_owned, mix_other), [dk, dk, dv, dv]))
    grad_query, grad_key, grad_value, grad_gate = mix_grads
    (output,) = kernel(last_sum, [block_bf16], *last.pieces(), resid)

    return (
        output,
        grad_tokens,
        grad_query,
        grad_key,
        grad_value,
        grad_gate,
        grad_out,
        first_gain,
        stack[1],
        grad_ffn_gate,
        grad_ffn_up,
        grad_down,
        stack[2],
        stack[3],
    )


def solution(mesh):
    tokens = P(("rep", "fsdp"), None)
    matrix = P("fsdp", None)
    vector = P("fsdp")
    in_specs = (tokens,) + (matrix,) * 5 + (vector,) * 2 + (matrix,) * 3 + (vector,) * 2 + (tokens,)
    out_specs = (tokens,) * 2 + (matrix,) * 5 + (vector,) * 2 + (matrix,) * 3 + (vector,) * 2
    return jax.shard_map(
        on_device, mesh=mesh, in_specs=in_specs, out_specs=out_specs, check_vma=False
    )
```

```python
import math

import jax
import jax.numpy as jnp
from jax import lax
from jax.experimental import pallas as pl
from jax.experimental.pallas import tpu as pltpu
from jax.sharding import PartitionSpec as P

HEADS = 8
epsilon = 1e-05
head_epsilon = 1.0
f32 = jnp.float32
bf16 = jnp.bfloat16
BOTH = ("rep", "fsdp")
CORE, X = 3, 4
LIMITS = (52, 30, 38, 30, 56, 24)


def dot(a, b, ca=1, cb=0, kind=f32):
    return lax.dot_general(a, b, (((ca,), (cb,)), ((), ())), preferred_element_type=kind)


def after(*values):
    return lax.optimization_barrier(values)


def shape(dims, kind):
    return jax.ShapeDtypeStruct(tuple(dims), kind)


def block(dims, *index):
    return pl.BlockSpec(dims, lambda *_: index)


def kernel(body, outs, *ins, scalars=None, scratch=(), limit=8):
    whole = pl.BlockSpec(memory_space=pltpu.VMEM)
    grid = (1,) if any(isinstance(i, tuple) for i in ins) else ()
    specs = [i[1] if isinstance(i, tuple) else whole for i in ins]
    ins = [i[0] if isinstance(i, tuple) else i for i in ins]
    if scalars is not None:
        specs = [pl.BlockSpec(memory_space=pltpu.SMEM)] + specs
        ins = [scalars] + ins
    return pl.pallas_call(
        body,
        out_shape=list(outs),
        grid=grid,
        in_specs=specs,
        out_specs=[whole] * len(outs),
        scratch_shapes=list(scratch),
        compiler_params=pltpu.CompilerParams(vmem_limit_bytes=limit << 20),
        cost_estimate=pl.CostEstimate(flops=0, bytes_accessed=0, transcendentals=0),
    )(*ins)


def streamed(body, outs, *ins, scalars=None, scratch=(), limit=8, late=(), stream=()):
    whole = pl.BlockSpec(memory_space=pltpu.VMEM)
    away = pl.BlockSpec(memory_space=pltpu.HBM)
    first = 0 if scalars is None else 1
    n_in, n_out, n_own = len(ins), len(outs), len(scratch)
    late, stream = list(late), list(stream)
    pushes = len(stream)

    def run(*refs):
        given, refs = refs[:first], refs[first:]
        ins, refs = list(refs[:n_in]), refs[n_in:]
        outs, refs = list(refs[:n_out]), refs[n_out:]
        own, refs = refs[:n_own], refs[n_own:]
        rooms, refs = refs[: len(late)], refs[len(late) :]
        stages, refs = refs[: len(stream)], refs[len(stream) :]
        comes, goes = refs
        arrivals, departures = {}, []
        for k, (i, room) in enumerate(zip(late, rooms)):
            arrivals[i] = pltpu.make_async_copy(ins[i], room, comes.at[k])
            arrivals[i].start()
            ins[i] = room
        targets = {}
        for i, stage in zip(stream, stages):
            targets[i], outs[i] = outs[i], stage

        def ready(*numbers):
            for i in numbers:
                arrivals.pop(i).wait()

        def push(i, *index):
            source, target = outs[i], targets[i]
            if index:
                source, target = source.at[index], target.at[index]
            copy = pltpu.make_async_copy(source, target, goes.at[len(departures)])
            copy.start()
            departures.append(copy)

        more = {}
        if late:
            more["ready"] = ready
        if stream:
            more["push"] = push
        body(*given, *ins, *outs, *own, **more)
        for copy in departures:
            copy.wait()

    specs = [away if i in late else whole for i in range(n_in)]
    if scalars is not None:
        specs = [pl.BlockSpec(memory_space=pltpu.SMEM)] + specs
    rooms = [pltpu.VMEM(ins[i].shape, ins[i].dtype) for i in late]
    stages = [pltpu.VMEM(outs[i].shape, outs[i].dtype) for i in stream]
    sems = [pltpu.SemaphoreType.DMA((max(len(late), 1),)), pltpu.SemaphoreType.DMA((pushes,))]
    return pl.pallas_call(
        run,
        out_shape=list(outs),
        in_specs=specs,
        out_specs=[away if i in stream else whole for i in range(n_out)],
        scratch_shapes=[*scratch, *rooms, *stages, *sems],
        compiler_params=pltpu.CompilerParams(vmem_limit_bytes=limit << 20),
        cost_estimate=pl.CostEstimate(flops=0, bytes_accessed=0, transcendentals=0),
    )(*(() if scalars is None else (scalars,)), *ins)


def number():
    return lax.axis_index("rep") * lax.axis_size("fsdp") + lax.axis_index("fsdp")


def bit(place):
    return (number() >> place) & 1


def bits():
    return (lax.axis_size("rep") * lax.axis_size("fsdp")).bit_length() - 1


def swap(value, place):
    count = 1 << bits()
    return lax.ppermute(value, BOTH, [(i, i ^ (1 << place)) for i in range(count)])


RING = (0, 2, 4, 6, 7, 5, 3, 1)
OFFSETS = (0, -1, -2, -3, 1, 2, 3, 4)


def owners():
    place = jnp.array([RING.index(i) for i in range(HEADS)], jnp.int32)[lax.axis_index("fsdp")]
    return jnp.array(RING, jnp.int32)[(place + jnp.array(OFFSETS, jnp.int32)) % HEADS]


def send(value, ahead):
    pairs = [(RING[i], RING[(i + 1) % HEADS]) for i in range(HEADS)]
    return lax.ppermute(value, "fsdp", pairs if ahead else [(b, a) for a, b in pairs])


class Gather:
    def __init__(self, own):
        self.own, self.ahead, self.behind = own, [own], [own]

    def peek(self):
        a, b = self.ahead[-1], self.behind[-1]
        if len(self.ahead) == 4:
            rows = a.shape[0] // 2
            a, b = a[:rows], b[rows:]
        return send(a, True), send(b, False)

    def put(self, a, b):
        self.ahead.append(a)
        self.behind.append(b)

    def step(self, *others):
        a, b, *others = after(*self.peek(), *others)
        self.put(a, b)
        return others

    def hold(self, *others):
        self.ahead[-1], self.behind[-1], *others = after(self.ahead[-1], self.behind[-1], *others)
        return others

    def pieces(self):
        return (self.own, *self.ahead[1:4], *self.behind[1:4], self.ahead[4], self.behind[4])


def tile(refs, i):
    names = ((0, 1), (2, 3), (4, 5), (6, 7, 8))[i]
    return jnp.concatenate([refs[j][...] for j in names], 0)


def term_shapes(rows, width, tiles=(0, 1, 2, 3)):
    full = 2 * len(tiles) - (3 in tiles)
    return [shape((full * rows, width), bf16)] + [shape((rows // 2, width), bf16)] * 2 * (3 in tiles)


def put_tile(refs, i, values, first=0):
    both = values.shape[0]
    rows, start = both // 2, (i - first) * both
    values = values.astype(bf16)
    if i < 3:
        refs[0][start : start + both] = values
    else:
        refs[0][start : start + rows] = values[:rows]
        refs[1][...] = values[rows : rows + rows // 2]
        refs[2][...] = values[rows + rows // 2 :]


def fold(term_a, term_b, a, b):
    rows, width = term_a[1].block_shape
    half = rows // 2

    def body(term_a, term_b, a, b, out_a, out_b):
        if a.shape[0] == rows:
            out_a[...] = (term_a[...].astype(f32) + a[...].astype(f32)).astype(bf16)
            out_b[...] = (term_b[...].astype(f32) + b[...].astype(f32)).astype(bf16)
        else:
            out_a[:half] = (term_a[:half].astype(f32) + a[...].astype(f32)).astype(bf16)
            out_a[half:] = term_a[half:]
            out_b[:half] = term_b[:half]
            out_b[half:] = (term_b[half:].astype(f32) + b[...].astype(f32)).astype(bf16)

    return kernel(body, [shape((rows, width), bf16)] * 2, term_a, term_b, a, b)


class Scatter:
    def __init__(self, terms):
        *self.terms, self.a, self.b = terms
        self.rows = 2 * self.a.shape[0]
        self.steps = 0

    def term(self, offset):
        slot = OFFSETS.index(offset)
        rows, width = self.rows, self.terms[0].shape[1]
        for terms in self.terms:
            if slot < terms.shape[0] // rows:
                return terms, block((rows, width), slot, 0)
            slot -= terms.shape[0] // rows

    def peek(self):
        if self.steps:
            self.fold(4 - self.steps)
        self.steps += 1
        return send(self.a, True), send(self.b, False)

    def put(self, a, b):
        self.a, self.b = a, b

    def step(self, *others):
        a, b, *others = after(*self.peek(), *others)
        self.put(a, b)
        return others

    def hold(self, *others):
        self.a, self.b, *others = after(self.a, self.b, *others)
        return others

    def fold(self, offset):
        self.a, self.b = fold(self.term(offset), self.term(-offset), self.a, self.b)

    def pieces(self):
        return self.term(0), self.a, self.b


class Pair:
    def __init__(self, terms):
        *self.terms, a, b = terms
        self.rows, self.width = 2 * a.shape[0], a.shape[1] // 2
        self.a = [a[:, : self.width], a[:, self.width :]]
        self.b = [b[:, : self.width], b[:, self.width :]]
        self.steps = [0, 0]

    def term(self, offset, c):
        slot = OFFSETS.index(offset)
        for terms in self.terms:
            if slot < terms.shape[0] // self.rows:
                return terms, block((self.rows, self.width), slot, c)
            slot -= terms.shape[0] // self.rows

    def step(self, c):
        if self.steps[c]:
            offset = 4 - self.steps[c]
            self.a[c], self.b[c] = fold(
                self.term(offset, c), self.term(-offset, c), self.a[c], self.b[c]
            )
        self.steps[c] += 1
        self.a[c], self.b[c] = after(send(self.a[c], True), send(self.b[c], False))

    def run(self):
        for _ in range(4):
            for c in (0, 1):
                self.step(c)

    def pieces(self):
        whole = block((self.rows, 2 * self.width), 0, 0)
        return ((self.terms[0], whole), *self.a, *self.b)


def total(refs):
    if len(refs) == 5:
        a, b = (jnp.concatenate([refs[i][...], refs[i + 1][...]], -1) for i in (1, 3))
    else:
        a, b = refs[1][...], refs[2][...]
    return refs[0][...].astype(f32) + a.astype(f32) + b.astype(f32)


def normalize(values):
    center = values - jnp.mean(values, axis=-1, keepdims=True)
    scale = lax.rsqrt(jnp.mean(center * center, axis=-1, keepdims=True) + epsilon)
    return center * scale, scale


def normalize_back(normed, scale, grad):
    return scale * (
        grad
        - jnp.mean(grad, axis=-1, keepdims=True)
        - normed * jnp.mean(grad * normed, axis=-1, keepdims=True)
    )


def head_norm(values):
    center = values - jnp.mean(values, axis=-1, keepdims=True)
    scale = lax.rsqrt(jnp.mean(center * center, axis=-1, keepdims=True) + head_epsilon)
    return center * scale, scale


def on_device(
    tokens,
    w_query,
    w_key,
    w_value,
    w_gate,
    w_out,
    norm1_gain,
    norm1_bias,
    w_ffn_gate,
    w_ffn_up,
    w_ffn_down,
    norm2_gain,
    norm2_bias,
    cotangent,
):
    n = lax.axis_size("fsdp")
    assert n == HEADS
    rows, width = tokens.shape
    depth = w_query.shape[0]
    half_depth = depth // 2
    dk = w_query.shape[1] // n
    dv = w_value.shape[1] // n
    ff = w_ffn_gate.shape[1] // n
    every = n * rows
    half_width = width // 2
    where = jnp.stack([bit(CORE), bit(X)])


    def fetch(*weights):
        sizes = [w.shape[1] // n // 2 for w in weights]
        whole = sum(sizes)

        def body(s, *refs):
            for h in range(4):
                start = 0
                for ref, size in zip(refs, sizes):
                    place = pl.multiple_of((2 * h + s[1]) * size, size)
                    refs[-1][h, :, start : start + size] = ref[:, pl.ds(place, size)]
                    start += size

        packed = pl.pallas_call(
            body,
            out_shape=shape((n, half_depth, whole), bf16),
            grid_spec=pltpu.PrefetchScalarGridSpec(
                num_scalar_prefetch=1,
                grid=(n // 4,),
                in_specs=[
                    pl.BlockSpec((half_depth, 8 * size), lambda k, s: (s[0], k)) for size in sizes
                ],
                out_specs=pl.BlockSpec((4, half_depth, whole), lambda k, s: (k, 0, 0)),
            ),
            compiler_params=pltpu.CompilerParams(vmem_limit_bytes=60 << 20),
            cost_estimate=pl.CostEstimate(flops=0, bytes_accessed=0, transcendentals=0),
        )(where, *weights)
        return packed

    def trade(packed):
        got = lax.all_to_all(packed, "fsdp", 0, 0, tiled=True)
        return got.reshape(n * half_depth, got.shape[-1])

    def more(value):
        for place in range(X + 1, bits()):
            low = value.astype(bf16)
            value = low.astype(f32) + swap(low, place).astype(f32)
        return value

    def columns_grad(zs, parts):
        count, size = len(zs), parts[0].shape[-1]

        def body(*refs):
            zs, parts, outs = refs[:count], refs[count : 2 * count], refs[2 * count :]
            for j in (1, 0):
                for t in (1, 0):
                    columns = slice(t * half_width, (t + 1) * half_width)
                    value = sum(dot(z[:, columns], part[j], 0, 0) for z, part in zip(zs, parts))
                    outs[2 * j + t][...] = value.astype(bf16)

        return kernel(
            body, [shape((half_width, size), bf16)] * 4, *zs, *parts, limit=LIMITS[5]
        )

    def sum_cores(own, own_t, other, other_t):
        given = other.astype(f32) + swap(other_t, CORE).astype(f32)
        return own, swap(own_t, CORE), given.astype(bf16)

    def sum_x(own, own_c, got):
        return more(own.astype(f32) + own_c.astype(f32) + got.astype(f32)).astype(bf16)

    def give(grad):
        grad = grad.reshape(n, half_depth, grad.shape[-1])
        return lax.all_to_all(grad, "fsdp", 0, 0, tiled=True)

    def everywhere(own, other):
        return own, swap(own, CORE), other, swap(other, CORE)

    def flat(pieces, sizes):
        whole = sum(sizes) // 2

        def body(s, own, own_c, other, other_c, *outs):
            here = pl.ds(s[0] * half_depth, half_depth)
            there = pl.ds((1 - s[0]) * half_depth, half_depth)
            for h in (0, 1):
                start = 0
                for out, size in zip(outs, sizes):
                    half = size // 2
                    columns = slice(start, start + half)
                    for x, a, b in ((s[1], own, own_c), (1 - s[1], other, other_c)):
                        place = pl.ds(pl.multiple_of(x * half, half) + h * size, half)
                        out[here, place] = a[h, :, columns].astype(f32)
                        out[there, place] = b[h, :, columns].astype(f32)
                    start += half

        return pl.pallas_call(
            body,
            out_shape=[shape((depth, n * size), f32) for size in sizes],
            grid_spec=pltpu.PrefetchScalarGridSpec(
                num_scalar_prefetch=1,
                grid=(n // 2,),
                in_specs=[pl.BlockSpec((2, half_depth, whole), lambda k, s: (k, 0, 0))] * 4,
                out_specs=[pl.BlockSpec((depth, 2 * size), lambda k, s: (0, k)) for size in sizes],
            ),
            compiler_params=pltpu.CompilerParams(vmem_limit_bytes=24 << 20),
            cost_estimate=pl.CostEstimate(flops=0, bytes_accessed=0, transcendentals=0),
        )(where, *pieces)


    def rows_products(s, lefts, right, kept, given):
        size = lefts[0].shape[1] // 4
        for out, c in ((kept, s[0]), (given, 1 - s[0])):
            for i in (0, 1):
                columns = pl.ds(pl.multiple_of((2 * i + c) * size, size), size)
                total, start = 0.0, 0
                for left in lefts:
                    rows_here = slice(start, start + left.shape[0])
                    total = total + dot(left[:, columns], right[rows_here], 0, 0)
                    start += left.shape[0]
                out[i] = total.astype(bf16)

    def rows_grad(lefts, right):
        count = len(lefts)

        def body(s, *refs):
            rows_products(s, refs[:count], *refs[count:])

        return kernel(
            body, [shape((2, lefts[0].shape[1] // 4, right.shape[1]), bf16)] * 2, *lefts, right,
            scalars=where, limit=14,
        )

    def sum_cores_rows(kept, given):
        return (kept.astype(f32) + swap(given, CORE).astype(f32)).astype(bf16)

    def sum_x_rows(mine, got):
        return more(mine.astype(f32) + got[::-1].astype(f32)).astype(bf16)

    def flat_rows(grad):
        size = grad.shape[1]

        def body(s, own, own_c, out):
            for i, x in enumerate((s[1], 1 - s[1])):
                out[pl.ds((2 * x + s[0]) * size, size), :] = own[i].astype(f32)
                out[pl.ds((2 * x + 1 - s[0]) * size, size), :] = own_c[i].astype(f32)

        (out,) = kernel(
            body, [shape((4 * size, grad.shape[2]), f32)], grad, swap(grad, CORE), scalars=where
        )
        return out


    def arranged(s):
        for i in range(2 * n):
            column = ((i % n) * 2 + (s[0] ^ (i // n))) * half_depth
            yield i * half_depth, pl.ds(pl.multiple_of(column, half_depth), half_depth)

    block_f32 = shape((rows, width), f32)
    block_bf16 = shape((rows, width), bf16)
    pair_f32 = shape((2, width), f32)
    room_of_block = [pltpu.VMEM((rows, width), f32)]

    def second_norm(s, *refs):
        sums, (tokens, gains, resid, z, room) = refs[:-5], refs[-5:]
        value = tokens[...].astype(f32) + total(sums)
        resid[...] = value
        normed, _ = normalize(value)
        room[...] = normed * gains[2:3] + gains[3:4]
        for start, columns in arranged(s):
            z[:, start : start + half_depth] = room[:, columns].astype(bf16)

    def norm_back(s, refs, inputs, gain, room, sums=None):
        grad = total(refs)
        for start, columns in arranged(s):
            room[:, columns] = grad[:, start : start + half_depth]
        grad = room[...]
        normed, scale = normalize(inputs)
        if sums is not None:
            sums[0:1] = jnp.sum(grad * normed, axis=0, keepdims=True)
            sums[1:2] = jnp.sum(grad, axis=0, keepdims=True)
        return normalize_back(normed, scale, grad * gain)

    def second_back(s, *refs):
        parts, (resid, cot, gains, grad_resid, sums, out, room) = refs[:3], refs[3:]
        grad = norm_back(s, parts, resid[...], gains[2:3], room, sums)
        grad = grad + cot[...].astype(f32)
        grad_resid[...] = grad
        out[...] = grad.astype(bf16)

    def first_back(s, *refs):
        parts, (tokens, grad_resid, gains, out, room) = refs[:3], refs[3:]
        grad = norm_back(s, parts, tokens[...].astype(f32), gains[0:1], room)
        out[...] = grad_resid[...] + grad

    def last_sum(*refs):
        parts, resid, out = refs[:3], refs[3], refs[4]
        out[...] = (resid[...] + total(parts)).astype(bf16)


    tiles = range(4)
    halves = (slice(0, half_width), slice(half_width, width))

    def rows_of(i):
        return slice(2 * i * rows, 2 * (i + 1) * rows)

    def in_order(x, own, other):
        first = jnp.where(x == 0, own, other)
        second = jnp.where(x == 0, other, own)
        return first, second

    def of_x(ref, x, size):
        return [ref[pl.ds(pl.multiple_of(i * size, size), size), :] for i in (x, 1 - x)]

    def mixer(s, *refs, ready, push):
        pieces, gains, w, (cosine, sine, decay, w_out), refs = (
            refs[:9], refs[9], refs[10:14], refs[14:18], refs[18:]
        )
        z, q, k, v, g, p, retained, mixed, *outs, room = refs
        x = s[1]
        one, half, middle = dk // 2, dv // 2, dk + dv // 2
        for i in tiles:
            normed, _ = normalize(tile(pieces, i).astype(f32))
            room[...] = normed * gains[0:1] + gains[1:2]
            for start, columns in arranged(s):
                z[rows_of(i), start : start + half_depth] = room[:, columns].astype(bf16)
        push(0)
        ready(10, 11, 12, 13, 14, 15)
        for i in tiles:
            here = rows_of(i)
            own, other = (
                dot(z[here, halves[0]], w[j][...]) + dot(z[here, halves[1]], w[2 + j][...])
                for j in (0, 1)
            )
            c, sn = cosine[here], sine[here]
            a, b = in_order(x, own[:, :one], other[:, :one])
            q[here, :one] = (a * c - b * sn).astype(bf16)
            q[here, one:] = (b * c + a * sn).astype(bf16)
            a, b = in_order(x, own[:, one:dk], other[:, one:dk])
            k[here, :one] = ((a * c - b * sn) * dk**-0.5).astype(bf16)
            k[here, one:] = ((b * c + a * sn) * dk**-0.5).astype(bf16)
            v[here, :half] = own[:, dk:middle].astype(bf16)
            v[here, half:] = other[:, dk:middle].astype(bf16)
            g[here, :half] = own[:, middle:]
            g[here, half:] = other[:, middle:]
        for i in (1, 2, 3, 4):
            push(i)
        ready(16, 17)
        for i in tiles:
            here = rows_of(i)
            scores = (dot(q[here], k[...], 1, 1) * decay[here]).astype(bf16)
            p[here] = scores
            value = dot(scores, v[...])
            retained[here] = value
            normed, _ = head_norm(value)
            gate = g[here]
            part = (normed * gate / (1.0 + jnp.exp(-gate))).astype(bf16)
            mixed[here] = part
            own, other = of_x(w_out, x, half)
            put_tile(outs, i, dot(part[:, :half], own) + dot(part[:, half:], other))
        for i in (9, 10, 8, 5, 6, 7):
            push(i)

    def join_tiles(*refs):
        for i in tiles:
            refs[9][rows_of(i)] = tile(refs, i)

    def feed(which, count):
        def body(s, *refs):
            pieces, cots, w_down, w = (
                refs[:count], refs[count : 2 * count], refs[2 * count],
                refs[2 * count + 1 : 2 * count + 5],
            )
            (z, hidden, grad), outs = refs[2 * count + 5 : 2 * count + 8], refs[2 * count + 8 :]
            half = ff // 2
            for i in which:
                here = rows_of(i - which[0])
                part, cot = (
                    tile(p, i) if count > 3 else jnp.concatenate([r[...] for r in p], 0)
                    for p in (pieces, cots)
                )
                z[here] = part
                downs = of_x(w_down, s[1], half)
                back = 0.0
                for j in (0, 1):
                    ab = dot(part[:, halves[0]], w[j][...]) + dot(part[:, halves[1]], w[2 + j][...])
                    a, b = ab[:, :half], ab[:, half:]
                    below = 0.5 * (1.0 + lax.erf(a * math.sqrt(0.5)))
                    gelu = a * below
                    slope = below + a * jnp.exp(-0.5 * a * a) * (1.0 / math.sqrt(2.0 * math.pi))
                    columns = slice(j * half, (j + 1) * half)
                    hidden[here, columns] = (gelu * b).astype(bf16)
                    d = dot(cot, downs[j], 1, 1).astype(bf16).astype(f32)
                    both = jnp.concatenate([d * b * slope, d * gelu], -1).astype(bf16)
                    grad[j, here] = both
                    back = back + jnp.concatenate(
                        [dot(both, w[j][...], 1, 1), dot(both, w[2 + j][...], 1, 1)], -1
                    )
                put_tile(outs, i, back, which[0])

        return body

    def feed_shapes(which):
        count = 2 * rows * len(which)
        return [
            shape((count, width), bf16), shape((count, ff), bf16), shape((2, count, ff), bf16)
        ] + term_shapes(rows, width, which)

    def down(s, h, last_h, w, *outs):
        half = ff // 2
        for i in tiles:
            here = h[rows_of(i)] if i < 3 else last_h[...]
            own, other = of_x(w, s[1], half)
            put_tile(outs, i, dot(here[:, :half], own) + dot(here[:, half:], other))

    def mixer_back(s, *refs, ready, push):
        pieces, (w_out, r, g, mixed, q, k, v, p, decay, cosine, sine), w, z = (
            refs[:9], refs[9:20], refs[20:24], refs[24]
        )
        kept, given, sums, d_pre, *outs = refs[25:32]
        d_out, d_r, d_k, d_v, room = refs[32:]
        one, half = dk // 2, dv // 2
        cut = dk + half
        x = s[1]
        ready(9, 10, 11)
        for i in tiles:
            here = rows_of(i)
            part = tile(pieces, i)
            d_out[here] = part
            own, other = of_x(w_out, x, half)
            d_mixed = jnp.concatenate([dot(part, own, 1, 1), dot(part, other, 1, 1)], -1)
            d_mixed = d_mixed.astype(bf16).astype(f32)
            normed, scale = head_norm(r[here])
            gate = g[here]
            sigmoid = 1.0 / (1.0 + jnp.exp(-gate))
            both = (d_mixed * normed * sigmoid * (1.0 + gate * (1.0 - sigmoid))).astype(bf16)
            d_pre[0, here, cut:], d_pre[1, here, cut:] = both[:, :half], both[:, half:]
            d_r[here] = normalize_back(normed, scale, d_mixed * gate * sigmoid).astype(bf16)
        ready(12)
        rows_products(s, [mixed], d_out, kept, given)
        push(0)
        push(1)
        ready(13, 14, 15, 16, 17, 18, 19)
        for i in tiles:
            here = rows_of(i)
            scores = (dot(d_r[here], v[...], 1, 1) * decay[here]).astype(bf16)
            c, sn = cosine[here], sine[here]
            grad = dot(scores, k[...])
            a, b = grad[:, :one], grad[:, one:]
            own, other = in_order(x, a * c + b * sn, b * c - a * sn)
            d_pre[0, here, :one] = own.astype(bf16)
            d_pre[1, here, :one] = other.astype(bf16)
            more_k, more_v = dot(scores, q[here], 0, 0), dot(p[here], d_r[here], 0, 0)
            if i == 0:
                d_k[...], d_v[...] = more_k, more_v
            else:
                d_k[...] += more_k
                d_v[...] += more_v
        for i in tiles:
            here = rows_of(i)
            c, sn = cosine[here] * dk**-0.5, sine[here] * dk**-0.5
            a, b = d_k[here, :one], d_k[here, one:]
            own, other = in_order(x, a * c + b * sn, b * c - a * sn)
            d_pre[0, here, one:dk] = own.astype(bf16)
            d_pre[1, here, one:dk] = other.astype(bf16)
            d_pre[0, here, dk:cut] = d_v[here, :half].astype(bf16)
            d_pre[1, here, dk:cut] = d_v[here, half:].astype(bf16)
        push(3)
        ready(20, 21, 22, 23, 24)
        for i in tiles:
            here = rows_of(i)
            back = [
                dot(d_pre[0, here], w[2 * t][...], 1, 1)
                + dot(d_pre[1, here], w[2 * t + 1][...], 1, 1)
                for t in (0, 1)
            ]
            back = jnp.concatenate(back, -1)
            put_tile(outs, i, back)
            parts = jnp.concatenate(
                [
                    jnp.sum(back * z[here].astype(f32), axis=0, keepdims=True),
                    jnp.sum(back, axis=0, keepdims=True),
                ],
                0,
            )
            if i == 0:
                room[...] = parts
            else:
                room[...] += parts
        for i in (5, 6, 4):
            push(i)
        for start, columns in arranged(s):
            sums[:, columns] = room[:, start : start + half_depth]

    terms = term_shapes(rows, width)


    packed, tokens_late, ffn_gate_late, ffn_up_late, *gains_late = after(
        fetch(w_query, w_key, w_value, w_gate), tokens, w_ffn_gate, w_ffn_up,
        norm1_gain, norm1_bias, norm2_gain, norm2_bias,
    )
    gains_late = jnp.stack(gains_late)
    mix_own = trade(packed)
    ring = Gather(tokens_late)

    head = lax.axis_index("fsdp")
    gamma_log = jnp.log(1.0 - 2.0 ** (-5.0 - head.astype(f32)))
    positions = (owners() * rows)[:, None] + jnp.arange(rows, dtype=jnp.int32)[None, :]
    positions = positions.reshape(-1).astype(f32)
    half = dk // 2
    freqs = jnp.exp(-jnp.arange(half, dtype=f32) * (math.log(10000.0) / half))
    angles = positions[:, None] * freqs[None, :]
    cosine, sine = jnp.cos(angles), jnp.sin(angles)
    differ = positions[:, None] - positions[None, :]
    decay = jnp.where(differ >= 0, jnp.exp(jnp.maximum(differ, 0.0) * gamma_log), 0.0)

    def widen(value, place):
        other = swap(value, place)
        first = bit(place) == 0
        return jnp.concatenate([jnp.where(first, value, other), jnp.where(first, other, value)], 1)

    cosine, sine, decay, ffn_packed, mix_own, gains = ring.step(
        cosine, sine, decay, fetch(ffn_gate_late, ffn_up_late), mix_own, widen(gains_late, 0)
    )
    mix_other = swap(mix_own, X)
    mix_own_c = swap(mix_own, CORE)
    (gains,) = ring.step(widen(gains, 1))
    (gains,) = ring.step(widen(gains, 2))
    gains = gains.astype(f32)

    mix_other, mix_own_c, ffn_packed = ring.step(mix_other, mix_own_c, ffn_packed)
    mix_other_c = swap(mix_other, CORE)
    w_mix = (mix_own, mix_other, mix_own_c, mix_other_c)
    ffn_own = trade(ffn_packed)
    z_first, query, key, value, gate, scores, retained, mixed, *parts = streamed(
        mixer,
        [shape((every, width), bf16)]
        + [shape((every, dk), bf16)] * 2
        + [shape((every, dv), bf16), shape((every, dv), f32), shape((every, every), bf16)]
        + [shape((every, dv), f32), shape((every, dv), bf16)]
        + terms,
        *ring.pieces(), gains, *w_mix, cosine, sine, decay, w_out,
        scalars=where, limit=LIMITS[0], late=range(10, 18), stream=range(11),
        scratch=[pltpu.VMEM((2 * rows, width), f32)],
    )
    *parts, cot_late = after(*parts, cotangent)
    ring = Pair(parts)
    cot_ring = Gather(cot_late)
    ring.step(0)
    ring.a[0], ffn_own = after(ring.a[0], ffn_own)
    ffn_other = swap(ffn_own, X)
    ffn_own_c = swap(ffn_own, CORE)
    ring.step(1)
    for _ in range(3):
        ring.step(0)
        ring.step(1)
        cot_ring.step()
    resid, second = kernel(
        second_norm, [block_f32, block_bf16], *ring.pieces(), tokens, gains,
        scalars=where, scratch=room_of_block, limit=8,
    )

    ring = Gather(second)
    (ffn_other,) = ring.step(ffn_other)
    ffn_other_c = swap(ffn_other, CORE)
    ring.step()
    w_ffn = ring.step(ffn_own, ffn_other, ffn_own_c, ffn_other_c)
    early = (ring.own, *ring.ahead[1:4], *ring.behind[1:3])
    early_cots = (cot_ring.own, *cot_ring.ahead[1:4], *cot_ring.behind[1:3])
    done = kernel(
        feed((0, 1, 2), 6), feed_shapes((0, 1, 2)),
        *early, *early_cots, w_ffn_down, *w_ffn,
        scalars=where, limit=LIMITS[2],
    )
    a, b, *done = after(*cot_ring.peek(), *done)
    cot_ring.put(a, b)
    done = ring.step(*done)
    z_second, hidden, d_ab, terms_early = done
    z_last, hidden_last, d_ab_last, *parts = kernel(
        feed((3,), 3), feed_shapes((3,)),
        ring.behind[3], ring.ahead[4], ring.behind[4],
        cot_ring.behind[3], cot_ring.ahead[4], cot_ring.behind[4], w_ffn_down, *w_ffn,
        scalars=where, limit=18,
    )
    ring = Scatter([terms_early, *parts])
    (cot_all,) = ring.step(
        *kernel(join_tiles, [shape((every, width), bf16)], *cot_ring.pieces(), limit=24)
    )
    grad_ffn = ring.step(*columns_grad([z_second, z_last], [d_ab, d_ab_last]))
    ffn_own, ffn_own_c, ffn_given = sum_cores(*grad_ffn)
    ffn_own, ffn_own_c, ffn_given, down_kept, down_given = ring.step(
        ffn_own, ffn_own_c, ffn_given, *rows_grad([hidden, hidden_last], cot_all)
    )
    ffn_sent = swap(ffn_given, X)
    (down_sum,) = ring.step(sum_cores_rows(down_kept, down_given))
    grad_resid, second_sums, part = kernel(
        second_back, [block_f32, pair_f32, block_bf16],
        *ring.pieces(), resid, cotangent, gains,
        scalars=where, scratch=room_of_block,
    )
    ring = Gather(part)
    ffn_own, ffn_sent, down_sum = ring.step(ffn_own, ffn_sent, down_sum)
    down_got = swap(down_sum, X)
    ffn_sum = sum_x(ffn_own, ffn_own_c, ffn_sent)
    ring.step()
    last = Scatter(kernel(down, terms, hidden, hidden_last, w_ffn_down, scalars=where, limit=20))
    ring.step()
    a, b, down_got, ffn_sum = ring.step(*last.peek(), down_got, ffn_sum)
    last.put(a, b)

    ffn_owned = give(ffn_sum)
    out_kept, out_given, first_sums, d_pre, *parts = streamed(
        mixer_back,
        [shape((2, dv // 4, width), bf16)] * 2
        + [pair_f32, shape((2, every, dk + dv), bf16)]
        + terms,
        *ring.pieces(), w_out, retained, gate, mixed,
        query, key, value, scores, decay, cosine, sine, *w_mix, z_first,
        scalars=where, limit=LIMITS[4], late=range(9, 25), stream=(0, 1, 3, 4, 5, 6),
        scratch=[
            pltpu.VMEM((every, width), bf16),
            pltpu.VMEM((every, dv), bf16),
            pltpu.VMEM((every, dk), f32),
            pltpu.VMEM((every, dv), f32),
            pltpu.VMEM((2, width), f32),
        ],
    )
    out_kept, out_given, first_sums, d_pre, ffn_owned, *parts = after(
        out_kept, out_given, first_sums, d_pre, ffn_owned, *parts
    )
    ring = Scatter(parts)
    stack = jnp.concatenate([first_sums, second_sums])
    mix_own, mix_own_c, mix_given = sum_cores(*columns_grad([z_first], [d_pre]))
    out_sum = sum_cores_rows(out_kept, out_given)
    mix_own, mix_own_c, mix_given, out_sum, stack_c = ring.step(
        mix_own, mix_own_c, mix_given, out_sum, swap(stack, X)
    )
    stack = stack + stack_c
    for place in range(X + 1, bits()):
        stack = stack + swap(stack, place)
    mix_sent = swap(mix_given, X)
    (stack_c,) = ring.step(swap(stack, CORE))
    stack = stack + stack_c
    (stack_c,) = ring.step(swap(stack, 0))
    stack = stack + stack_c
    mix_sent, stack_c, out_sum = ring.step(mix_sent, swap(stack, 1), out_sum)
    stack = stack + stack_c
    mix_owned = give(sum_x(mix_own, mix_own_c, mix_sent))
    out_got, ffn_other = swap(out_sum, X), swap(ffn_owned, X)
    grad_tokens = kernel(
        first_back, [block_f32], *ring.pieces(), tokens, grad_resid, gains,
        scalars=where, scratch=room_of_block,
    )[0]
    grad_down = flat_rows(sum_x_rows(down_sum, down_got))
    a, b, mix_owned, ffn_other, out_got, grad_tokens, grad_down = after(
        *last.peek(), mix_owned, ffn_other, out_got, grad_tokens, grad_down
    )
    last.put(a, b)
    mix_other = swap(mix_owned, X)
    grad_ffn_gate, grad_ffn_up = flat(everywhere(ffn_owned, ffn_other), [ff, ff])
    grad_out = flat_rows(sum_x_rows(out_sum, out_got))
    grad_ffn_gate, grad_ffn_up, grad_out, stack_c = last.step(
        grad_ffn_gate, grad_ffn_up, grad_out, swap(stack, 2)
    )
    stack = lax.dynamic_slice_in_dim(stack + stack_c, head * depth, depth, 1)
    first_gain = (stack[0] - norm1_bias.astype(f32) * stack[1]) / norm1_gain.astype(f32)
    last.step()
    (output,) = kernel(last_sum, [block_bf16], *last.pieces(), resid)
    mix_other, output, first_gain = after(mix_other, output, first_gain)
    grad_query, grad_key, grad_value, grad_gate = flat(
        everywhere(mix_owned, mix_other), [dk, dk, dv, dv]
    )

    return (
        output,
        grad_tokens,
        grad_query,
        grad_key,
        grad_value,
        grad_gate,
        grad_out,
        first_gain,
        stack[1],
        grad_ffn_gate,
        grad_ffn_up,
        grad_down,
        stack[2],
        stack[3],
    )


def solution(mesh):
    tokens = P(("rep", "fsdp"), None)
    matrix = P("fsdp", None)
    vector = P("fsdp")
    in_specs = (tokens,) + (matrix,) * 5 + (vector,) * 2 + (matrix,) * 3 + (vector,) * 2 + (tokens,)
    out_specs = (tokens,) * 2 + (matrix,) * 5 + (vector,) * 2 + (matrix,) * 3 + (vector,) * 2
    return jax.shard_map(
        on_device, mesh=mesh, in_specs=in_specs, out_specs=out_specs, check_vma=False
    )
```

```python
import math

import jax
import jax.numpy as jnp
from jax import lax
from jax.experimental import pallas as pl
from jax.experimental.pallas import tpu as pltpu
from jax.sharding import PartitionSpec as P

HEADS = 8
epsilon = 1e-05
head_epsilon = 1.0
f32 = jnp.float32
bf16 = jnp.bfloat16
BOTH = ("rep", "fsdp")
CORE, X = 3, 4
LIMITS = (52, 30, 38, 30, 56, 24)


def dot(a, b, ca=1, cb=0, kind=f32):
    return lax.dot_general(a, b, (((ca,), (cb,)), ((), ())), preferred_element_type=kind)


def after(*values):
    return lax.optimization_barrier(values)


def shape(dims, kind):
    return jax.ShapeDtypeStruct(tuple(dims), kind)


def block(dims, *index):
    return pl.BlockSpec(dims, lambda *_: index)


def kernel(body, outs, *ins, scalars=None, scratch=(), limit=8):
    whole = pl.BlockSpec(memory_space=pltpu.VMEM)
    grid = (1,) if any(isinstance(i, tuple) for i in ins) else ()
    specs = [i[1] if isinstance(i, tuple) else whole for i in ins]
    ins = [i[0] if isinstance(i, tuple) else i for i in ins]
    if scalars is not None:
        specs = [pl.BlockSpec(memory_space=pltpu.SMEM)] + specs
        ins = [scalars] + ins
    return pl.pallas_call(
        body,
        out_shape=list(outs),
        grid=grid,
        in_specs=specs,
        out_specs=[whole] * len(outs),
        scratch_shapes=list(scratch),
        compiler_params=pltpu.CompilerParams(vmem_limit_bytes=limit << 20),
        cost_estimate=pl.CostEstimate(flops=0, bytes_accessed=0, transcendentals=0),
    )(*ins)


def streamed(body, outs, *ins, scalars=None, scratch=(), limit=8, late=(), stream=()):
    whole = pl.BlockSpec(memory_space=pltpu.VMEM)
    away = pl.BlockSpec(memory_space=pltpu.HBM)
    first = 0 if scalars is None else 1
    n_in, n_out, n_own = len(ins), len(outs), len(scratch)
    late, stream = list(late), list(stream)
    pushes = len(stream)

    def run(*refs):
        given, refs = refs[:first], refs[first:]
        ins, refs = list(refs[:n_in]), refs[n_in:]
        outs, refs = list(refs[:n_out]), refs[n_out:]
        own, refs = refs[:n_own], refs[n_own:]
        rooms, refs = refs[: len(late)], refs[len(late) :]
        stages, refs = refs[: len(stream)], refs[len(stream) :]
        comes, goes = refs
        arrivals, departures = {}, []
        for k, (i, room) in enumerate(zip(late, rooms)):
            arrivals[i] = pltpu.make_async_copy(ins[i], room, comes.at[k])
            arrivals[i].start()
            ins[i] = room
        targets = {}
        for i, stage in zip(stream, stages):
            targets[i], outs[i] = outs[i], stage

        def ready(*numbers):
            for i in numbers:
                arrivals.pop(i).wait()

        def push(i, *index):
            source, target = outs[i], targets[i]
            if index:
                source, target = source.at[index], target.at[index]
            copy = pltpu.make_async_copy(source, target, goes.at[len(departures)])
            copy.start()
            departures.append(copy)

        more = {}
        if late:
            more["ready"] = ready
        if stream:
            more["push"] = push
        body(*given, *ins, *outs, *own, **more)
        for copy in departures:
            copy.wait()

    specs = [away if i in late else whole for i in range(n_in)]
    if scalars is not None:
        specs = [pl.BlockSpec(memory_space=pltpu.SMEM)] + specs
    rooms = [pltpu.VMEM(ins[i].shape, ins[i].dtype) for i in late]
    stages = [pltpu.VMEM(outs[i].shape, outs[i].dtype) for i in stream]
    sems = [pltpu.SemaphoreType.DMA((max(len(late), 1),)), pltpu.SemaphoreType.DMA((pushes,))]
    return pl.pallas_call(
        run,
        out_shape=list(outs),
        in_specs=specs,
        out_specs=[away if i in stream else whole for i in range(n_out)],
        scratch_shapes=[*scratch, *rooms, *stages, *sems],
        compiler_params=pltpu.CompilerParams(vmem_limit_bytes=limit << 20),
        cost_estimate=pl.CostEstimate(flops=0, bytes_accessed=0, transcendentals=0),
    )(*(() if scalars is None else (scalars,)), *ins)


def number():
    return lax.axis_index("rep") * lax.axis_size("fsdp") + lax.axis_index("fsdp")


def bit(place):
    return (number() >> place) & 1


def bits():
    return (lax.axis_size("rep") * lax.axis_size("fsdp")).bit_length() - 1


def swap(value, place):
    count = 1 << bits()
    return lax.ppermute(value, BOTH, [(i, i ^ (1 << place)) for i in range(count)])


RING = (0, 2, 4, 6, 7, 5, 3, 1)
OFFSETS = (0, -1, -2, -3, 1, 2, 3, 4)


def owners():
    place = jnp.array([RING.index(i) for i in range(HEADS)], jnp.int32)[lax.axis_index("fsdp")]
    return jnp.array(RING, jnp.int32)[(place + jnp.array(OFFSETS, jnp.int32)) % HEADS]


def send(value, ahead):
    pairs = [(RING[i], RING[(i + 1) % HEADS]) for i in range(HEADS)]
    return lax.ppermute(value, "fsdp", pairs if ahead else [(b, a) for a, b in pairs])


class Gather:
    def __init__(self, own):
        self.own, self.ahead, self.behind = own, [own], [own]

    def peek(self):
        a, b = self.ahead[-1], self.behind[-1]
        if len(self.ahead) == 4:
            rows = a.shape[0] // 2
            a, b = a[:rows], b[rows:]
        return send(a, True), send(b, False)

    def put(self, a, b):
        self.ahead.append(a)
        self.behind.append(b)

    def step(self, *others):
        a, b, *others = after(*self.peek(), *others)
        self.put(a, b)
        return others

    def hold(self, *others):
        self.ahead[-1], self.behind[-1], *others = after(self.ahead[-1], self.behind[-1], *others)
        return others

    def pieces(self):
        return (self.own, *self.ahead[1:4], *self.behind[1:4], self.ahead[4], self.behind[4])


def tile(refs, i):
    names = ((0, 1), (2, 3), (4, 5), (6, 7, 8))[i]
    return jnp.concatenate([refs[j][...] for j in names], 0)


def term_shapes(rows, width, tiles=(0, 1, 2, 3)):
    full = 2 * len(tiles) - (3 in tiles)
    return [shape((full * rows, width), bf16)] + [shape((rows // 2, width), bf16)] * 2 * (3 in tiles)


def put_tile(refs, i, values, first=0, part=None):
    both, width = values.shape
    rows, start = both // 2, (i - first) * both
    values = values.astype(bf16)
    columns = slice(0, width) if part is None else slice(part * width, (part + 1) * width)
    if i < 3:
        refs[0][start : start + both, columns] = values
    else:
        refs[0][start : start + rows, columns] = values[:rows]
        refs[1][:, columns] = values[rows : rows + rows // 2]
        refs[2][:, columns] = values[rows + rows // 2 :]


def fold(term_a, term_b, a, b):
    rows, width = term_a[1].block_shape
    half = rows // 2

    def body(term_a, term_b, a, b, out_a, out_b):
        if a.shape[0] == rows:
            out_a[...] = (term_a[...].astype(f32) + a[...].astype(f32)).astype(bf16)
            out_b[...] = (term_b[...].astype(f32) + b[...].astype(f32)).astype(bf16)
        else:
            out_a[:half] = (term_a[:half].astype(f32) + a[...].astype(f32)).astype(bf16)
            out_a[half:] = term_a[half:]
            out_b[:half] = term_b[:half]
            out_b[half:] = (term_b[half:].astype(f32) + b[...].astype(f32)).astype(bf16)

    return kernel(body, [shape((rows, width), bf16)] * 2, term_a, term_b, a, b)


class Scatter:
    def __init__(self, terms):
        *self.terms, self.a, self.b = terms
        self.rows = 2 * self.a.shape[0]
        self.steps = 0

    def term(self, offset):
        slot = OFFSETS.index(offset)
        rows, width = self.rows, self.terms[0].shape[1]
        for terms in self.terms:
            if slot < terms.shape[0] // rows:
                return terms, block((rows, width), slot, 0)
            slot -= terms.shape[0] // rows

    def peek(self):
        if self.steps:
            self.fold(4 - self.steps)
        self.steps += 1
        return send(self.a, True), send(self.b, False)

    def put(self, a, b):
        self.a, self.b = a, b

    def step(self, *others):
        a, b, *others = after(*self.peek(), *others)
        self.put(a, b)
        return others

    def hold(self, *others):
        self.a, self.b, *others = after(self.a, self.b, *others)
        return others

    def fold(self, offset):
        self.a, self.b = fold(self.term(offset), self.term(-offset), self.a, self.b)

    def pieces(self):
        return self.term(0), self.a, self.b


class Pair:
    def __init__(self, terms):
        *self.terms, a, b = terms
        self.rows, self.width = 2 * a.shape[0], a.shape[1] // 2
        self.a = [a[:, : self.width], a[:, self.width :]]
        self.b = [b[:, : self.width], b[:, self.width :]]
        self.steps = [0, 0]

    def term(self, offset, c):
        slot = OFFSETS.index(offset)
        for terms in self.terms:
            if slot < terms.shape[0] // self.rows:
                return terms, block((self.rows, self.width), slot, c)
            slot -= terms.shape[0] // self.rows

    def step(self, c):
        if self.steps[c]:
            offset = 4 - self.steps[c]
            self.a[c], self.b[c] = fold(
                self.term(offset, c), self.term(-offset, c), self.a[c], self.b[c]
            )
        self.steps[c] += 1
        self.a[c], self.b[c] = after(send(self.a[c], True), send(self.b[c], False))

    def run(self):
        for _ in range(4):
            for c in (0, 1):
                self.step(c)

    def pieces(self):
        whole = block((self.rows, 2 * self.width), 0, 0)
        return ((self.terms[0], whole), *self.a, *self.b)


def total(refs):
    if len(refs) == 5:
        a, b = (jnp.concatenate([refs[i][...], refs[i + 1][...]], -1) for i in (1, 3))
    else:
        a, b = refs[1][...], refs[2][...]
    return refs[0][...].astype(f32) + a.astype(f32) + b.astype(f32)


def normalize(values):
    center = values - jnp.mean(values, axis=-1, keepdims=True)
    scale = lax.rsqrt(jnp.mean(center * center, axis=-1, keepdims=True) + epsilon)
    return center * scale, scale


def normalize_back(normed, scale, grad):
    return scale * (
        grad
        - jnp.mean(grad, axis=-1, keepdims=True)
        - normed * jnp.mean(grad * normed, axis=-1, keepdims=True)
    )


def head_norm(values):
    center = values - jnp.mean(values, axis=-1, keepdims=True)
    scale = lax.rsqrt(jnp.mean(center * center, axis=-1, keepdims=True) + head_epsilon)
    return center * scale, scale


def on_device(
    tokens,
    w_query,
    w_key,
    w_value,
    w_gate,
    w_out,
    norm1_gain,
    norm1_bias,
    w_ffn_gate,
    w_ffn_up,
    w_ffn_down,
    norm2_gain,
    norm2_bias,
    cotangent,
):
    n = lax.axis_size("fsdp")
    assert n == HEADS
    rows, width = tokens.shape
    depth = w_query.shape[0]
    half_depth = depth // 2
    dk = w_query.shape[1] // n
    dv = w_value.shape[1] // n
    ff = w_ffn_gate.shape[1] // n
    every = n * rows
    half_width = width // 2
    where = jnp.stack([bit(CORE), bit(X)])


    def fetch(*weights):
        sizes = [w.shape[1] // n // 2 for w in weights]
        whole = sum(sizes)

        def body(s, *refs):
            for h in range(4):
                start = 0
                for ref, size in zip(refs, sizes):
                    place = pl.multiple_of((2 * h + s[1]) * size, size)
                    refs[-1][h, :, start : start + size] = ref[:, pl.ds(place, size)]
                    start += size

        packed = pl.pallas_call(
            body,
            out_shape=shape((n, half_depth, whole), bf16),
            grid_spec=pltpu.PrefetchScalarGridSpec(
                num_scalar_prefetch=1,
                grid=(n // 4,),
                in_specs=[
                    pl.BlockSpec((half_depth, 8 * size), lambda k, s: (s[0], k)) for size in sizes
                ],
                out_specs=pl.BlockSpec((4, half_depth, whole), lambda k, s: (k, 0, 0)),
            ),
            compiler_params=pltpu.CompilerParams(vmem_limit_bytes=60 << 20),
            cost_estimate=pl.CostEstimate(flops=0, bytes_accessed=0, transcendentals=0),
        )(where, *weights)
        return packed

    def trade(packed):
        got = lax.all_to_all(packed, "fsdp", 0, 0, tiled=True)
        return got.reshape(n * half_depth, got.shape[-1])

    def more(value):
        for place in range(X + 1, bits()):
            low = value.astype(bf16)
            value = low.astype(f32) + swap(low, place).astype(f32)
        return value

    def columns_grad(zs, parts):
        count, size = len(zs), parts[0].shape[-1]

        def body(*refs):
            zs, parts, outs = refs[:count], refs[count : 2 * count], refs[2 * count :]
            for j in (1, 0):
                for t in (1, 0):
                    columns = slice(t * half_width, (t + 1) * half_width)
                    value = sum(dot(z[:, columns], part[j], 0, 0) for z, part in zip(zs, parts))
                    outs[2 * j + t][...] = value.astype(bf16)

        return kernel(
            body, [shape((half_width, size), bf16)] * 4, *zs, *parts, limit=LIMITS[5]
        )

    def sum_cores(own, own_t, other, other_t):
        given = other.astype(f32) + swap(other_t, CORE).astype(f32)
        return own, swap(own_t, CORE), given.astype(bf16)

    def sum_x(own, own_c, got):
        return more(own.astype(f32) + own_c.astype(f32) + got.astype(f32)).astype(bf16)

    def give(grad):
        grad = grad.reshape(n, half_depth, grad.shape[-1])
        return lax.all_to_all(grad, "fsdp", 0, 0, tiled=True)

    def everywhere(own, other):
        return own, swap(own, CORE), other, swap(other, CORE)

    def flat(pieces, sizes):
        whole = sum(sizes) // 2

        def body(s, own, own_c, other, other_c, *outs):
            here = pl.ds(s[0] * half_depth, half_depth)
            there = pl.ds((1 - s[0]) * half_depth, half_depth)
            for h in (0, 1):
                start = 0
                for out, size in zip(outs, sizes):
                    half = size // 2
                    columns = slice(start, start + half)
                    for x, a, b in ((s[1], own, own_c), (1 - s[1], other, other_c)):
                        place = pl.ds(pl.multiple_of(x * half, half) + h * size, half)
                        out[here, place] = a[h, :, columns].astype(f32)
                        out[there, place] = b[h, :, columns].astype(f32)
                    start += half

        return pl.pallas_call(
            body,
            out_shape=[shape((depth, n * size), f32) for size in sizes],
            grid_spec=pltpu.PrefetchScalarGridSpec(
                num_scalar_prefetch=1,
                grid=(n // 2,),
                in_specs=[pl.BlockSpec((2, half_depth, whole), lambda k, s: (k, 0, 0))] * 4,
                out_specs=[pl.BlockSpec((depth, 2 * size), lambda k, s: (0, k)) for size in sizes],
            ),
            compiler_params=pltpu.CompilerParams(vmem_limit_bytes=24 << 20),
            cost_estimate=pl.CostEstimate(flops=0, bytes_accessed=0, transcendentals=0),
        )(where, *pieces)


    def rows_products(s, lefts, right, kept, given):
        size = lefts[0].shape[1] // 4
        for out, c in ((kept, s[0]), (given, 1 - s[0])):
            for i in (0, 1):
                columns = pl.ds(pl.multiple_of((2 * i + c) * size, size), size)
                total, start = 0.0, 0
                for left in lefts:
                    rows_here = slice(start, start + left.shape[0])
                    total = total + dot(left[:, columns], right[rows_here], 0, 0)
                    start += left.shape[0]
                out[i] = total.astype(bf16)

    def rows_grad(lefts, right):
        count = len(lefts)

        def body(s, *refs):
            rows_products(s, refs[:count], *refs[count:])

        return kernel(
            body, [shape((2, lefts[0].shape[1] // 4, right.shape[1]), bf16)] * 2, *lefts, right,
            scalars=where, limit=14,
        )

    def sum_cores_rows(kept, given):
        return (kept.astype(f32) + swap(given, CORE).astype(f32)).astype(bf16)

    def sum_x_rows(mine, got):
        return more(mine.astype(f32) + got[::-1].astype(f32)).astype(bf16)

    def flat_rows(grad):
        size = grad.shape[1]

        def body(s, own, own_c, out):
            for i, x in enumerate((s[1], 1 - s[1])):
                out[pl.ds((2 * x + s[0]) * size, size), :] = own[i].astype(f32)
                out[pl.ds((2 * x + 1 - s[0]) * size, size), :] = own_c[i].astype(f32)

        (out,) = kernel(
            body, [shape((4 * size, grad.shape[2]), f32)], grad, swap(grad, CORE), scalars=where
        )
        return out


    def arranged(s):
        for i in range(2 * n):
            column = ((i % n) * 2 + (s[0] ^ (i // n))) * half_depth
            yield i * half_depth, pl.ds(pl.multiple_of(column, half_depth), half_depth)

    block_f32 = shape((rows, width), f32)
    block_bf16 = shape((rows, width), bf16)
    pair_f32 = shape((2, width), f32)
    room_of_block = [pltpu.VMEM((rows, width), f32)]

    def second_norm(s, *refs):
        sums, (tokens, gains, resid, z, room) = refs[:-5], refs[-5:]
        value = tokens[...].astype(f32) + total(sums)
        resid[...] = value
        normed, _ = normalize(value)
        room[...] = normed * gains[2:3] + gains[3:4]
        for start, columns in arranged(s):
            z[:, start : start + half_depth] = room[:, columns].astype(bf16)

    def norm_back(s, refs, inputs, gain, room, sums=None):
        grad = total(refs)
        for start, columns in arranged(s):
            room[:, columns] = grad[:, start : start + half_depth]
        grad = room[...]
        normed, scale = normalize(inputs)
        if sums is not None:
            sums[0:1] = jnp.sum(grad * normed, axis=0, keepdims=True)
            sums[1:2] = jnp.sum(grad, axis=0, keepdims=True)
        return normalize_back(normed, scale, grad * gain)

    def second_back(s, *refs):
        parts, (resid, cot, gains, grad_resid, sums, out, room) = refs[:3], refs[3:]
        grad = norm_back(s, parts, resid[...], gains[2:3], room, sums)
        grad = grad + cot[...].astype(f32)
        grad_resid[...] = grad
        out[...] = grad.astype(bf16)

    def first_back(s, *refs):
        parts, (tokens, grad_resid, gains, out, room) = refs[:3], refs[3:]
        grad = norm_back(s, parts, tokens[...].astype(f32), gains[0:1], room)
        out[...] = grad_resid[...] + grad

    def last_sum(*refs):
        parts, resid, out = refs[:3], refs[3], refs[4]
        out[...] = (resid[...] + total(parts)).astype(bf16)


    tiles = range(4)
    halves = (slice(0, half_width), slice(half_width, width))

    def rows_of(i):
        return slice(2 * i * rows, 2 * (i + 1) * rows)

    def in_order(x, own, other):
        first = jnp.where(x == 0, own, other)
        second = jnp.where(x == 0, other, own)
        return first, second

    def of_x(ref, x, size):
        return [ref[pl.ds(pl.multiple_of(i * size, size), size), :] for i in (x, 1 - x)]

    def mixer(s, *refs, ready, push):
        pieces, gains, w, (cosine, sine, decay, w_out), refs = (
            refs[:9], refs[9], refs[10:14], refs[14:18], refs[18:]
        )
        z, q, k, v, g, p, retained, mixed, *outs, room = refs
        x = s[1]
        one, half, middle = dk // 2, dv // 2, dk + dv // 2
        for i in tiles:
            normed, _ = normalize(tile(pieces, i).astype(f32))
            room[...] = normed * gains[0:1] + gains[1:2]
            for start, columns in arranged(s):
                z[rows_of(i), start : start + half_depth] = room[:, columns].astype(bf16)
        push(0)
        ready(10, 11, 12, 13, 14, 15)
        for i in tiles:
            here = rows_of(i)
            own, other = (
                dot(z[here, halves[0]], w[j][...]) + dot(z[here, halves[1]], w[2 + j][...])
                for j in (0, 1)
            )
            c, sn = cosine[here], sine[here]
            a, b = in_order(x, own[:, :one], other[:, :one])
            q[here, :one] = (a * c - b * sn).astype(bf16)
            q[here, one:] = (b * c + a * sn).astype(bf16)
            a, b = in_order(x, own[:, one:dk], other[:, one:dk])
            k[here, :one] = ((a * c - b * sn) * dk**-0.5).astype(bf16)
            k[here, one:] = ((b * c + a * sn) * dk**-0.5).astype(bf16)
            v[here, :half] = own[:, dk:middle].astype(bf16)
            v[here, half:] = other[:, dk:middle].astype(bf16)
            g[here, :half] = own[:, middle:]
            g[here, half:] = other[:, middle:]
        for i in (1, 2, 3, 4):
            push(i)
        ready(16, 17)
        for i in tiles:
            here = rows_of(i)
            scores = (dot(q[here], k[...], 1, 1) * decay[here]).astype(bf16)
            p[here] = scores
            value = dot(scores, v[...])
            retained[here] = value
            normed, _ = head_norm(value)
            gate = g[here]
            part = (normed * gate / (1.0 + jnp.exp(-gate))).astype(bf16)
            mixed[here] = part
            own, other = of_x(w_out, x, half)
            put_tile(outs, i, dot(part[:, :half], own) + dot(part[:, half:], other))
        for i in (9, 10, 8, 5, 6, 7):
            push(i)

    def join_tiles(*refs):
        for i in tiles:
            refs[9][rows_of(i)] = tile(refs, i)

    def feed(which, count):
        def body(s, *refs):
            pieces, cots, w_down, w = (
                refs[:count], refs[count : 2 * count], refs[2 * count],
                refs[2 * count + 1 : 2 * count + 5],
            )
            (z, hidden, grad), outs = refs[2 * count + 5 : 2 * count + 8], refs[2 * count + 8 :]
            half = ff // 2
            for i in which:
                here = rows_of(i - which[0])
                part, cot = (
                    tile(p, i) if count > 3 else jnp.concatenate([r[...] for r in p], 0)
                    for p in (pieces, cots)
                )
                z[here] = part
                downs = of_x(w_down, s[1], half)
                for j in (0, 1):
                    ab = dot(part[:, halves[0]], w[j][...]) + dot(part[:, halves[1]], w[2 + j][...])
                    a, b = ab[:, :half], ab[:, half:]
                    below = 0.5 * (1.0 + lax.erf(a * math.sqrt(0.5)))
                    gelu = a * below
                    slope = below + a * jnp.exp(-0.5 * a * a) * (1.0 / math.sqrt(2.0 * math.pi))
                    columns = slice(j * half, (j + 1) * half)
                    hidden[here, columns] = (gelu * b).astype(bf16)
                    d = dot(cot, downs[j], 1, 1).astype(bf16).astype(f32)
                    both = jnp.concatenate([d * b * slope, d * gelu], -1).astype(bf16)
                    grad[j, here] = both
                for t in (0, 1):
                    back = dot(grad[0, here], w[2 * t][...], 1, 1)
                    back = back + dot(grad[1, here], w[2 * t + 1][...], 1, 1)
                    put_tile(outs, i, back, which[0], t)

        return body

    def feed_shapes(which):
        count = 2 * rows * len(which)
        return [
            shape((count, width), bf16), shape((count, ff), bf16), shape((2, count, ff), bf16)
        ] + term_shapes(rows, width, which)

    def down(s, h, last_h, w, *outs):
        half = ff // 2
        for i in tiles:
            here = h[rows_of(i)] if i < 3 else last_h[...]
            own, other = of_x(w, s[1], half)
            put_tile(outs, i, dot(here[:, :half], own) + dot(here[:, half:], other))

    def mixer_back(s, *refs, ready, push):
        pieces, (w_out, r, g, mixed, q, k, v, p, decay, cosine, sine), w, z = (
            refs[:9], refs[9:20], refs[20:24], refs[24]
        )
        kept, given, sums, d_pre, *outs = refs[25:32]
        d_out, d_r, d_k, d_v, room = refs[32:]
        one, half = dk // 2, dv // 2
        cut = dk + half
        x = s[1]
        for i in tiles:
            here = rows_of(i)
            part = tile(pieces, i)
            d_out[here] = part
            own, other = of_x(w_out, x, half)
            d_mixed = jnp.concatenate([dot(part, own, 1, 1), dot(part, other, 1, 1)], -1)
            d_mixed = d_mixed.astype(bf16).astype(f32)
            normed, scale = head_norm(r[here])
            gate = g[here]
            sigmoid = 1.0 / (1.0 + jnp.exp(-gate))
            both = (d_mixed * normed * sigmoid * (1.0 + gate * (1.0 - sigmoid))).astype(bf16)
            d_pre[0, here, cut:], d_pre[1, here, cut:] = both[:, :half], both[:, half:]
            d_r[here] = normalize_back(normed, scale, d_mixed * gate * sigmoid).astype(bf16)
        ready(12)
        rows_products(s, [mixed], d_out, kept, given)
        push(0)
        push(1)
        ready(13, 14, 15, 16, 17, 18, 19)
        for i in tiles:
            here = rows_of(i)
            scores = (dot(d_r[here], v[...], 1, 1) * decay[here]).astype(bf16)
            c, sn = cosine[here], sine[here]
            grad = dot(scores, k[...])
            a, b = grad[:, :one], grad[:, one:]
            own, other = in_order(x, a * c + b * sn, b * c - a * sn)
            d_pre[0, here, :one] = own.astype(bf16)
            d_pre[1, here, :one] = other.astype(bf16)
            more_k, more_v = dot(scores, q[here], 0, 0), dot(p[here], d_r[here], 0, 0)
            if i == 0:
                d_k[...], d_v[...] = more_k, more_v
            else:
                d_k[...] += more_k
                d_v[...] += more_v
        for i in tiles:
            here = rows_of(i)
            c, sn = cosine[here] * dk**-0.5, sine[here] * dk**-0.5
            a, b = d_k[here, :one], d_k[here, one:]
            own, other = in_order(x, a * c + b * sn, b * c - a * sn)
            d_pre[0, here, one:dk] = own.astype(bf16)
            d_pre[1, here, one:dk] = other.astype(bf16)
            d_pre[0, here, dk:cut] = d_v[here, :half].astype(bf16)
            d_pre[1, here, dk:cut] = d_v[here, half:].astype(bf16)
        push(3)
        ready(20, 21, 22, 23, 24)
        for i in tiles:
            here = rows_of(i)
            for t in (0, 1):
                back = dot(d_pre[0, here], w[2 * t][...], 1, 1)
                back = back + dot(d_pre[1, here], w[2 * t + 1][...], 1, 1)
                put_tile(outs, i, back, part=t)
                parts = jnp.concatenate(
                    [
                        jnp.sum(back * z[here, halves[t]].astype(f32), axis=0, keepdims=True),
                        jnp.sum(back, axis=0, keepdims=True),
                    ],
                    0,
                )
                if i == 0:
                    room[:, halves[t]] = parts
                else:
                    room[:, halves[t]] += parts
        for i in (5, 6, 4):
            push(i)
        for start, columns in arranged(s):
            sums[:, columns] = room[:, start : start + half_depth]

    terms = term_shapes(rows, width)


    packed, tokens_late, ffn_gate_late, ffn_up_late, *gains_late = after(
        fetch(w_query, w_key, w_value, w_gate), tokens, w_ffn_gate, w_ffn_up,
        norm1_gain, norm1_bias, norm2_gain, norm2_bias,
    )
    gains_late = jnp.stack(gains_late)
    mix_own = trade(packed)
    ring = Gather(tokens_late)

    head = lax.axis_index("fsdp")
    gamma_log = jnp.log(1.0 - 2.0 ** (-5.0 - head.astype(f32)))
    positions = (owners() * rows)[:, None] + jnp.arange(rows, dtype=jnp.int32)[None, :]
    positions = positions.reshape(-1).astype(f32)
    half = dk // 2
    freqs = jnp.exp(-jnp.arange(half, dtype=f32) * (math.log(10000.0) / half))
    angles = positions[:, None] * freqs[None, :]
    cosine, sine = jnp.cos(angles), jnp.sin(angles)
    differ = positions[:, None] - positions[None, :]
    decay = jnp.where(differ >= 0, jnp.exp(jnp.maximum(differ, 0.0) * gamma_log), 0.0)

    def widen(value, place):
        other = swap(value, place)
        first = bit(place) == 0
        return jnp.concatenate([jnp.where(first, value, other), jnp.where(first, other, value)], 1)

    cosine, sine, decay, ffn_packed, mix_own, gains = ring.step(
        cosine, sine, decay, fetch(ffn_gate_late, ffn_up_late), mix_own, widen(gains_late, 0)
    )
    mix_other = swap(mix_own, X)
    mix_own_c = swap(mix_own, CORE)
    (gains,) = ring.step(widen(gains, 1))
    (gains,) = ring.step(widen(gains, 2))
    gains = gains.astype(f32)

    mix_other, mix_own_c, ffn_packed = ring.step(mix_other, mix_own_c, ffn_packed)
    mix_other_c = swap(mix_other, CORE)
    w_mix = (mix_own, mix_other, mix_own_c, mix_other_c)
    ffn_own = trade(ffn_packed)
    z_first, query, key, value, gate, scores, retained, mixed, *parts = streamed(
        mixer,
        [shape((every, width), bf16)]
        + [shape((every, dk), bf16)] * 2
        + [shape((every, dv), bf16), shape((every, dv), f32), shape((every, every), bf16)]
        + [shape((every, dv), f32), shape((every, dv), bf16)]
        + terms,
        *ring.pieces(), gains, *w_mix, cosine, sine, decay, w_out,
        scalars=where, limit=LIMITS[0], late=range(10, 18), stream=range(11),
        scratch=[pltpu.VMEM((2 * rows, width), f32)],
    )
    *parts, cot_late = after(*parts, cotangent)
    ring = Pair(parts)
    cot_ring = Gather(cot_late)
    ring.step(0)
    ring.a[0], ffn_own = after(ring.a[0], ffn_own)
    ffn_other = swap(ffn_own, X)
    ffn_own_c = swap(ffn_own, CORE)
    ring.step(1)
    for _ in range(3):
        ring.step(0)
        ring.step(1)
        cot_ring.step()
    resid, second = kernel(
        second_norm, [block_f32, block_bf16], *ring.pieces(), tokens, gains,
        scalars=where, scratch=room_of_block, limit=8,
    )

    ring = Gather(second)
    (ffn_other,) = ring.step(ffn_other)
    ffn_other_c = swap(ffn_other, CORE)
    ring.step()
    w_ffn = ring.step(ffn_own, ffn_other, ffn_own_c, ffn_other_c)
    early = (ring.own, *ring.ahead[1:4], *ring.behind[1:3])
    early_cots = (cot_ring.own, *cot_ring.ahead[1:4], *cot_ring.behind[1:3])
    done = kernel(
        feed((0, 1, 2), 6), feed_shapes((0, 1, 2)),
        *early, *early_cots, w_ffn_down, *w_ffn,
        scalars=where, limit=LIMITS[2],
    )
    a, b, *done = after(*cot_ring.peek(), *done)
    cot_ring.put(a, b)
    done = ring.step(*done)
    z_second, hidden, d_ab, terms_early = done
    z_last, hidden_last, d_ab_last, *parts = kernel(
        feed((3,), 3), feed_shapes((3,)),
        ring.behind[3], ring.ahead[4], ring.behind[4],
        cot_ring.behind[3], cot_ring.ahead[4], cot_ring.behind[4], w_ffn_down, *w_ffn,
        scalars=where, limit=18,
    )
    ring = Scatter([terms_early, *parts])
    (cot_all,) = ring.step(
        *kernel(join_tiles, [shape((every, width), bf16)], *cot_ring.pieces(), limit=24)
    )
    grad_ffn = ring.step(*columns_grad([z_second, z_last], [d_ab, d_ab_last]))
    ffn_own, ffn_own_c, ffn_given = sum_cores(*grad_ffn)
    ffn_own, ffn_own_c, ffn_given, down_kept, down_given = ring.step(
        ffn_own, ffn_own_c, ffn_given, *rows_grad([hidden, hidden_last], cot_all)
    )
    ffn_sent = swap(ffn_given, X)
    (down_sum,) = ring.step(sum_cores_rows(down_kept, down_given))
    grad_resid, second_sums, part = kernel(
        second_back, [block_f32, pair_f32, block_bf16],
        *ring.pieces(), resid, cotangent, gains,
        scalars=where, scratch=room_of_block,
    )
    ring = Gather(part)
    ffn_own, ffn_sent, down_sum = ring.step(ffn_own, ffn_sent, down_sum)
    down_got = swap(down_sum, X)
    ffn_sum = sum_x(ffn_own, ffn_own_c, ffn_sent)
    ring.step()
    last = Scatter(kernel(down, terms, hidden, hidden_last, w_ffn_down, scalars=where, limit=20))
    ring.step()
    a, b, down_got, ffn_sum = ring.step(*last.peek(), down_got, ffn_sum)
    last.put(a, b)

    ffn_owned = give(ffn_sum)
    out_kept, out_given, first_sums, d_pre, *parts = streamed(
        mixer_back,
        [shape((2, dv // 4, width), bf16)] * 2
        + [pair_f32, shape((2, every, dk + dv), bf16)]
        + terms,
        *ring.pieces(), w_out, retained, gate, mixed,
        query, key, value, scores, decay, cosine, sine, *w_mix, z_first,
        scalars=where, limit=LIMITS[4], late=range(12, 25), stream=(0, 1, 3, 4, 5, 6),
        scratch=[
            pltpu.VMEM((every, width), bf16),
            pltpu.VMEM((every, dv), bf16),
            pltpu.VMEM((every, dk), f32),
            pltpu.VMEM((every, dv), f32),
            pltpu.VMEM((2, width), f32),
        ],
    )
    out_kept, out_given, first_sums, d_pre, ffn_owned, *parts = after(
        out_kept, out_given, first_sums, d_pre, ffn_owned, *parts
    )
    ring = Scatter(parts)
    stack = jnp.concatenate([first_sums, second_sums])
    mix_own, mix_own_c, mix_given = sum_cores(*columns_grad([z_first], [d_pre]))
    out_sum = sum_cores_rows(out_kept, out_given)
    mix_own, mix_own_c, mix_given, out_sum, stack_c = ring.step(
        mix_own, mix_own_c, mix_given, out_sum, swap(stack, X)
    )
    stack = stack + stack_c
    for place in range(X + 1, bits()):
        stack = stack + swap(stack, place)
    mix_sent = swap(mix_given, X)
    (stack_c,) = ring.step(swap(stack, CORE))
    stack = stack + stack_c
    (stack_c,) = ring.step(swap(stack, 0))
    stack = stack + stack_c
    mix_sent, stack_c, out_sum = ring.step(mix_sent, swap(stack, 1), out_sum)
    stack = stack + stack_c
    mix_owned = give(sum_x(mix_own, mix_own_c, mix_sent))
    out_got, ffn_other = swap(out_sum, X), swap(ffn_owned, X)
    grad_tokens = kernel(
        first_back, [block_f32], *ring.pieces(), tokens, grad_resid, gains,
        scalars=where, scratch=room_of_block,
    )[0]
    grad_down = flat_rows(sum_x_rows(down_sum, down_got))
    a, b, mix_owned, ffn_other, out_got, grad_tokens, grad_down = after(
        *last.peek(), mix_owned, ffn_other, out_got, grad_tokens, grad_down
    )
    last.put(a, b)
    mix_other = swap(mix_owned, X)
    grad_ffn_gate, grad_ffn_up = flat(everywhere(ffn_owned, ffn_other), [ff, ff])
    grad_out = flat_rows(sum_x_rows(out_sum, out_got))
    grad_ffn_gate, grad_ffn_up, grad_out, stack_c = last.step(
        grad_ffn_gate, grad_ffn_up, grad_out, swap(stack, 2)
    )
    stack = lax.dynamic_slice_in_dim(stack + stack_c, head * depth, depth, 1)
    first_gain = (stack[0] - norm1_bias.astype(f32) * stack[1]) / norm1_gain.astype(f32)
    last.step()
    (output,) = kernel(last_sum, [block_bf16], *last.pieces(), resid)
    mix_other, output, first_gain = after(mix_other, output, first_gain)
    grad_query, grad_key, grad_value, grad_gate = flat(
        everywhere(mix_owned, mix_other), [dk, dk, dv, dv]
    )

    return (
        output,
        grad_tokens,
        grad_query,
        grad_key,
        grad_value,
        grad_gate,
        grad_out,
        first_gain,
        stack[1],
        grad_ffn_gate,
        grad_ffn_up,
        grad_down,
        stack[2],
        stack[3],
    )


def solution(mesh):
    tokens = P(("rep", "fsdp"), None)
    matrix = P("fsdp", None)
    vector = P("fsdp")
    in_specs = (tokens,) + (matrix,) * 5 + (vector,) * 2 + (matrix,) * 3 + (vector,) * 2 + (tokens,)
    out_specs = (tokens,) * 2 + (matrix,) * 5 + (vector,) * 2 + (matrix,) * 3 + (vector,) * 2
    return jax.shard_map(
        on_device, mesh=mesh, in_specs=in_specs, out_specs=out_specs, check_vma=False
    )
```

```python
import math

import jax
import jax.numpy as jnp
from jax import lax
from jax.experimental import pallas as pl
from jax.experimental.pallas import tpu as pltpu
from jax.sharding import PartitionSpec as P

HEADS = 8
epsilon = 1e-05
head_epsilon = 1.0
f32 = jnp.float32
bf16 = jnp.bfloat16
BOTH = ("rep", "fsdp")
CORE, X = 3, 4
LIMITS = (52, 30, 38, 30, 56, 24)


def dot(a, b, ca=1, cb=0, kind=f32):
    return lax.dot_general(a, b, (((ca,), (cb,)), ((), ())), preferred_element_type=kind)


def after(*values):
    return lax.optimization_barrier(values)


def shape(dims, kind):
    return jax.ShapeDtypeStruct(tuple(dims), kind)


def block(dims, *index):
    return pl.BlockSpec(dims, lambda *_: index)


def kernel(body, outs, *ins, scalars=None, scratch=(), limit=8):
    whole = pl.BlockSpec(memory_space=pltpu.VMEM)
    grid = (1,) if any(isinstance(i, tuple) for i in ins) else ()
    specs = [i[1] if isinstance(i, tuple) else whole for i in ins]
    ins = [i[0] if isinstance(i, tuple) else i for i in ins]
    if scalars is not None:
        specs = [pl.BlockSpec(memory_space=pltpu.SMEM)] + specs
        ins = [scalars] + ins
    return pl.pallas_call(
        body,
        out_shape=list(outs),
        grid=grid,
        in_specs=specs,
        out_specs=[whole] * len(outs),
        scratch_shapes=list(scratch),
        compiler_params=pltpu.CompilerParams(vmem_limit_bytes=limit << 20),
        cost_estimate=pl.CostEstimate(flops=0, bytes_accessed=0, transcendentals=0),
    )(*ins)


def streamed(body, outs, *ins, scalars=None, scratch=(), limit=8, late=(), stream=()):
    whole = pl.BlockSpec(memory_space=pltpu.VMEM)
    away = pl.BlockSpec(memory_space=pltpu.HBM)
    first = 0 if scalars is None else 1
    n_in, n_out, n_own = len(ins), len(outs), len(scratch)
    late, stream = list(late), list(stream)
    pushes = len(stream)

    def run(*refs):
        given, refs = refs[:first], refs[first:]
        ins, refs = list(refs[:n_in]), refs[n_in:]
        outs, refs = list(refs[:n_out]), refs[n_out:]
        own, refs = refs[:n_own], refs[n_own:]
        rooms, refs = refs[: len(late)], refs[len(late) :]
        stages, refs = refs[: len(stream)], refs[len(stream) :]
        comes, goes = refs
        arrivals, departures = {}, []
        for k, (i, room) in enumerate(zip(late, rooms)):
            arrivals[i] = pltpu.make_async_copy(ins[i], room, comes.at[k])
            arrivals[i].start()
            ins[i] = room
        targets = {}
        for i, stage in zip(stream, stages):
            targets[i], outs[i] = outs[i], stage

        def ready(*numbers):
            for i in numbers:
                arrivals.pop(i).wait()

        def push(i, *index):
            source, target = outs[i], targets[i]
            if index:
                source, target = source.at[index], target.at[index]
            copy = pltpu.make_async_copy(source, target, goes.at[len(departures)])
            copy.start()
            departures.append(copy)

        more = {}
        if late:
            more["ready"] = ready
        if stream:
            more["push"] = push
        body(*given, *ins, *outs, *own, **more)
        for copy in departures:
            copy.wait()

    specs = [away if i in late else whole for i in range(n_in)]
    if scalars is not None:
        specs = [pl.BlockSpec(memory_space=pltpu.SMEM)] + specs
    rooms = [pltpu.VMEM(ins[i].shape, ins[i].dtype) for i in late]
    stages = [pltpu.VMEM(outs[i].shape, outs[i].dtype) for i in stream]
    sems = [pltpu.SemaphoreType.DMA((max(len(late), 1),)), pltpu.SemaphoreType.DMA((pushes,))]
    return pl.pallas_call(
        run,
        out_shape=list(outs),
        in_specs=specs,
        out_specs=[away if i in stream else whole for i in range(n_out)],
        scratch_shapes=[*scratch, *rooms, *stages, *sems],
        compiler_params=pltpu.CompilerParams(vmem_limit_bytes=limit << 20),
        cost_estimate=pl.CostEstimate(flops=0, bytes_accessed=0, transcendentals=0),
    )(*(() if scalars is None else (scalars,)), *ins)


def number():
    return lax.axis_index("rep") * lax.axis_size("fsdp") + lax.axis_index("fsdp")


def bit(place):
    return (number() >> place) & 1


def bits():
    return (lax.axis_size("rep") * lax.axis_size("fsdp")).bit_length() - 1


def swap(value, place):
    count = 1 << bits()
    return lax.ppermute(value, BOTH, [(i, i ^ (1 << place)) for i in range(count)])


RING = (0, 2, 4, 6, 7, 5, 3, 1)
OFFSETS = (0, -1, -2, -3, 1, 2, 3, 4)


def owners():
    place = jnp.array([RING.index(i) for i in range(HEADS)], jnp.int32)[lax.axis_index("fsdp")]
    return jnp.array(RING, jnp.int32)[(place + jnp.array(OFFSETS, jnp.int32)) % HEADS]


def send(value, ahead):
    pairs = [(RING[i], RING[(i + 1) % HEADS]) for i in range(HEADS)]
    return lax.ppermute(value, "fsdp", pairs if ahead else [(b, a) for a, b in pairs])


class Gather:
    def __init__(self, own):
        self.own, self.ahead, self.behind = own, [own], [own]

    def peek(self):
        a, b = self.ahead[-1], self.behind[-1]
        if len(self.ahead) == 4:
            rows = a.shape[0] // 2
            a, b = a[:rows], b[rows:]
        return send(a, True), send(b, False)

    def put(self, a, b):
        self.ahead.append(a)
        self.behind.append(b)

    def step(self, *others):
        a, b, *others = after(*self.peek(), *others)
        self.put(a, b)
        return others

    def hold(self, *others):
        self.ahead[-1], self.behind[-1], *others = after(self.ahead[-1], self.behind[-1], *others)
        return others

    def pieces(self):
        return (self.own, *self.ahead[1:4], *self.behind[1:4], self.ahead[4], self.behind[4])


def tile(refs, i):
    names = ((0, 1), (2, 3), (4, 5), (6, 7, 8))[i]
    return jnp.concatenate([refs[j][...] for j in names], 0)


def term_shapes(rows, width, tiles=(0, 1, 2, 3)):
    full = 2 * len(tiles) - (3 in tiles)
    return [shape((full * rows, width), bf16)] + [shape((rows // 2, width), bf16)] * 2 * (3 in tiles)


def put_tile(refs, i, values, first=0, part=None):
    both, width = values.shape
    rows, start = both // 2, (i - first) * both
    values = values.astype(bf16)
    columns = slice(0, width) if part is None else slice(part * width, (part + 1) * width)
    if i < 3:
        refs[0][start : start + both, columns] = values
    else:
        refs[0][start : start + rows, columns] = values[:rows]
        refs[1][:, columns] = values[rows : rows + rows // 2]
        refs[2][:, columns] = values[rows + rows // 2 :]


def fold(term_a, term_b, a, b):
    rows, width = term_a[1].block_shape
    half = rows // 2

    def body(term_a, term_b, a, b, out_a, out_b):
        if a.shape[0] == rows:
            out_a[...] = (term_a[...].astype(f32) + a[...].astype(f32)).astype(bf16)
            out_b[...] = (term_b[...].astype(f32) + b[...].astype(f32)).astype(bf16)
        else:
            out_a[:half] = (term_a[:half].astype(f32) + a[...].astype(f32)).astype(bf16)
            out_a[half:] = term_a[half:]
            out_b[:half] = term_b[:half]
            out_b[half:] = (term_b[half:].astype(f32) + b[...].astype(f32)).astype(bf16)

    return kernel(body, [shape((rows, width), bf16)] * 2, term_a, term_b, a, b)


class Scatter:
    def __init__(self, terms):
        *self.terms, self.a, self.b = terms
        self.rows = 2 * self.a.shape[0]
        self.steps = 0

    def term(self, offset):
        slot = OFFSETS.index(offset)
        rows, width = self.rows, self.terms[0].shape[1]
        for terms in self.terms:
            if slot < terms.shape[0] // rows:
                return terms, block((rows, width), slot, 0)
            slot -= terms.shape[0] // rows

    def peek(self):
        if self.steps:
            self.fold(4 - self.steps)
        self.steps += 1
        return send(self.a, True), send(self.b, False)

    def put(self, a, b):
        self.a, self.b = a, b

    def step(self, *others):
        a, b, *others = after(*self.peek(), *others)
        self.put(a, b)
        return others

    def hold(self, *others):
        self.a, self.b, *others = after(self.a, self.b, *others)
        return others

    def fold(self, offset):
        self.a, self.b = fold(self.term(offset), self.term(-offset), self.a, self.b)

    def pieces(self):
        return self.term(0), self.a, self.b


class Pair:
    def __init__(self, terms):
        *self.terms, a, b = terms
        self.rows, self.width = 2 * a.shape[0], a.shape[1] // 2
        self.a = [a[:, : self.width], a[:, self.width :]]
        self.b = [b[:, : self.width], b[:, self.width :]]
        self.steps = [0, 0]

    def term(self, offset, c):
        slot = OFFSETS.index(offset)
        for terms in self.terms:
            if slot < terms.shape[0] // self.rows:
                return terms, block((self.rows, self.width), slot, c)
            slot -= terms.shape[0] // self.rows

    def step(self, c):
        if self.steps[c]:
            offset = 4 - self.steps[c]
            self.a[c], self.b[c] = fold(
                self.term(offset, c), self.term(-offset, c), self.a[c], self.b[c]
            )
        self.steps[c] += 1
        self.a[c], self.b[c] = after(send(self.a[c], True), send(self.b[c], False))

    def run(self):
        for _ in range(4):
            for c in (0, 1):
                self.step(c)

    def pieces(self):
        whole = block((self.rows, 2 * self.width), 0, 0)
        return ((self.terms[0], whole), *self.a, *self.b)


def total(refs):
    if len(refs) == 5:
        a, b = (jnp.concatenate([refs[i][...], refs[i + 1][...]], -1) for i in (1, 3))
    else:
        a, b = refs[1][...], refs[2][...]
    return refs[0][...].astype(f32) + a.astype(f32) + b.astype(f32)


def normalize(values):
    center = values - jnp.mean(values, axis=-1, keepdims=True)
    scale = lax.rsqrt(jnp.mean(center * center, axis=-1, keepdims=True) + epsilon)
    return center * scale, scale


def normalize_back(normed, scale, grad):
    return scale * (
        grad
        - jnp.mean(grad, axis=-1, keepdims=True)
        - normed * jnp.mean(grad * normed, axis=-1, keepdims=True)
    )


def head_norm(values):
    center = values - jnp.mean(values, axis=-1, keepdims=True)
    scale = lax.rsqrt(jnp.mean(center * center, axis=-1, keepdims=True) + head_epsilon)
    return center * scale, scale


def on_device(
    tokens,
    w_query,
    w_key,
    w_value,
    w_gate,
    w_out,
    norm1_gain,
    norm1_bias,
    w_ffn_gate,
    w_ffn_up,
    w_ffn_down,
    norm2_gain,
    norm2_bias,
    cotangent,
):
    n = lax.axis_size("fsdp")
    assert n == HEADS
    rows, width = tokens.shape
    depth = w_query.shape[0]
    half_depth = depth // 2
    dk = w_query.shape[1] // n
    dv = w_value.shape[1] // n
    ff = w_ffn_gate.shape[1] // n
    every = n * rows
    half_width = width // 2
    where = jnp.stack([bit(CORE), bit(X)])


    def fetch(*weights):
        sizes = [w.shape[1] // n // 2 for w in weights]
        whole = sum(sizes)

        def body(s, *refs):
            for h in range(4):
                start = 0
                for ref, size in zip(refs, sizes):
                    place = pl.multiple_of((2 * h + s[1]) * size, size)
                    refs[-1][h, :, start : start + size] = ref[:, pl.ds(place, size)]
                    start += size

        packed = pl.pallas_call(
            body,
            out_shape=shape((n, half_depth, whole), bf16),
            grid_spec=pltpu.PrefetchScalarGridSpec(
                num_scalar_prefetch=1,
                grid=(n // 4,),
                in_specs=[
                    pl.BlockSpec((half_depth, 8 * size), lambda k, s: (s[0], k)) for size in sizes
                ],
                out_specs=pl.BlockSpec((4, half_depth, whole), lambda k, s: (k, 0, 0)),
            ),
            compiler_params=pltpu.CompilerParams(vmem_limit_bytes=60 << 20),
            cost_estimate=pl.CostEstimate(flops=0, bytes_accessed=0, transcendentals=0),
        )(where, *weights)
        return packed

    def trade(packed):
        got = lax.all_to_all(packed, "fsdp", 0, 0, tiled=True)
        return got.reshape(n * half_depth, got.shape[-1])

    def more(value):
        for place in range(X + 1, bits()):
            low = value.astype(bf16)
            value = low.astype(f32) + swap(low, place).astype(f32)
        return value

    def columns_grad(zs, parts):
        count, size = len(zs), parts[0].shape[-1]

        def body(*refs):
            zs, parts, outs = refs[:count], refs[count : 2 * count], refs[2 * count :]
            for j in (1, 0):
                for t in (1, 0):
                    columns = slice(t * half_width, (t + 1) * half_width)
                    value = sum(dot(z[:, columns], part[j], 0, 0) for z, part in zip(zs, parts))
                    outs[2 * j + t][...] = value.astype(bf16)

        return kernel(
            body, [shape((half_width, size), bf16)] * 4, *zs, *parts, limit=LIMITS[5]
        )

    def sum_cores(own, own_t, other, other_t):
        given = other.astype(f32) + swap(other_t, CORE).astype(f32)
        return own, swap(own_t, CORE), given.astype(bf16)

    def sum_x(own, own_c, got):
        return more(own.astype(f32) + own_c.astype(f32) + got.astype(f32)).astype(bf16)

    def give(grad):
        grad = grad.reshape(n, half_depth, grad.shape[-1])
        return lax.all_to_all(grad, "fsdp", 0, 0, tiled=True)

    def everywhere(own, other):
        return own, swap(own, CORE), other, swap(other, CORE)

    def flat(pieces, sizes):
        whole = sum(sizes) // 2

        def body(s, own, own_c, other, other_c, *outs):
            here = pl.ds(s[0] * half_depth, half_depth)
            there = pl.ds((1 - s[0]) * half_depth, half_depth)
            for h in (0, 1):
                start = 0
                for out, size in zip(outs, sizes):
                    half = size // 2
                    columns = slice(start, start + half)
                    for x, a, b in ((s[1], own, own_c), (1 - s[1], other, other_c)):
                        place = pl.ds(pl.multiple_of(x * half, half) + h * size, half)
                        out[here, place] = a[h, :, columns].astype(f32)
                        out[there, place] = b[h, :, columns].astype(f32)
                    start += half

        return pl.pallas_call(
            body,
            out_shape=[shape((depth, n * size), f32) for size in sizes],
            grid_spec=pltpu.PrefetchScalarGridSpec(
                num_scalar_prefetch=1,
                grid=(n // 2,),
                in_specs=[pl.BlockSpec((2, half_depth, whole), lambda k, s: (k, 0, 0))] * 4,
                out_specs=[pl.BlockSpec((depth, 2 * size), lambda k, s: (0, k)) for size in sizes],
            ),
            compiler_params=pltpu.CompilerParams(vmem_limit_bytes=24 << 20),
            cost_estimate=pl.CostEstimate(flops=0, bytes_accessed=0, transcendentals=0),
        )(where, *pieces)


    def rows_products(s, lefts, right, kept, given):
        size = lefts[0].shape[1] // 4
        for out, c in ((kept, s[0]), (given, 1 - s[0])):
            for i in (0, 1):
                columns = pl.ds(pl.multiple_of((2 * i + c) * size, size), size)
                total, start = 0.0, 0
                for left in lefts:
                    rows_here = slice(start, start + left.shape[0])
                    total = total + dot(left[:, columns], right[rows_here], 0, 0)
                    start += left.shape[0]
                out[i] = total.astype(bf16)

    def rows_grad(lefts, right):
        count = len(lefts)

        def body(s, *refs):
            rows_products(s, refs[:count], *refs[count:])

        return kernel(
            body, [shape((2, lefts[0].shape[1] // 4, right.shape[1]), bf16)] * 2, *lefts, right,
            scalars=where, limit=14,
        )

    def sum_cores_rows(kept, given):
        return (kept.astype(f32) + swap(given, CORE).astype(f32)).astype(bf16)

    def sum_x_rows(mine, got):
        return more(mine.astype(f32) + got[::-1].astype(f32)).astype(bf16)

    def flat_rows(grad):
        size = grad.shape[1]

        def body(s, own, own_c, out):
            for i, x in enumerate((s[1], 1 - s[1])):
                out[pl.ds((2 * x + s[0]) * size, size), :] = own[i].astype(f32)
                out[pl.ds((2 * x + 1 - s[0]) * size, size), :] = own_c[i].astype(f32)

        (out,) = kernel(
            body, [shape((4 * size, grad.shape[2]), f32)], grad, swap(grad, CORE), scalars=where
        )
        return out


    def arranged(s):
        for i in range(2 * n):
            column = ((i % n) * 2 + (s[0] ^ (i // n))) * half_depth
            yield i * half_depth, pl.ds(pl.multiple_of(column, half_depth), half_depth)

    block_f32 = shape((rows, width), f32)
    block_bf16 = shape((rows, width), bf16)
    pair_f32 = shape((2, width), f32)
    room_of_block = [pltpu.VMEM((rows, width), f32)]

    def second_norm(s, *refs):
        sums, (tokens, gains, resid, z, room) = refs[:-5], refs[-5:]
        value = tokens[...].astype(f32) + total(sums)
        resid[...] = value
        normed, _ = normalize(value)
        room[...] = normed * gains[2:3] + gains[3:4]
        for start, columns in arranged(s):
            z[:, start : start + half_depth] = room[:, columns].astype(bf16)

    def norm_back(s, refs, inputs, gain, room, sums=None):
        grad = total(refs)
        for start, columns in arranged(s):
            room[:, columns] = grad[:, start : start + half_depth]
        grad = room[...]
        normed, scale = normalize(inputs)
        if sums is not None:
            sums[0:1] = jnp.sum(grad * normed, axis=0, keepdims=True)
            sums[1:2] = jnp.sum(grad, axis=0, keepdims=True)
        return normalize_back(normed, scale, grad * gain)

    def second_back(s, *refs):
        parts, (resid, cot, gains, grad_resid, sums, out, room) = refs[:3], refs[3:]
        grad = norm_back(s, parts, resid[...], gains[2:3], room, sums)
        grad = grad + cot[...].astype(f32)
        grad_resid[...] = grad
        out[...] = grad.astype(bf16)

    def first_back(s, *refs):
        parts, (tokens, grad_resid, gains, out, room) = refs[:3], refs[3:]
        grad = norm_back(s, parts, tokens[...].astype(f32), gains[0:1], room)
        out[...] = grad_resid[...] + grad

    def last_sum(*refs):
        parts, resid, out = refs[:3], refs[3], refs[4]
        out[...] = (resid[...] + total(parts)).astype(bf16)


    tiles = range(4)
    halves = (slice(0, half_width), slice(half_width, width))

    def rows_of(i):
        return slice(2 * i * rows, 2 * (i + 1) * rows)

    def in_order(x, own, other):
        first = jnp.where(x == 0, own, other)
        second = jnp.where(x == 0, other, own)
        return first, second

    def of_x(ref, x, size):
        return [ref[pl.ds(pl.multiple_of(i * size, size), size), :] for i in (x, 1 - x)]

    def mixer(s, *refs, ready, push):
        pieces, gains, w, (cosine, sine, decay, w_out), refs = (
            refs[:9], refs[9], refs[10:14], refs[14:18], refs[18:]
        )
        z, q, k, v, g, p, retained, mixed, *outs, room = refs
        x = s[1]
        one, half, middle = dk // 2, dv // 2, dk + dv // 2
        for i in tiles:
            normed, _ = normalize(tile(pieces, i).astype(f32))
            room[...] = normed * gains[0:1] + gains[1:2]
            for start, columns in arranged(s):
                z[rows_of(i), start : start + half_depth] = room[:, columns].astype(bf16)
        push(0)
        ready(10, 11, 12, 13, 14, 15)
        for i in tiles:
            here = rows_of(i)
            own, other = (
                dot(z[here, halves[0]], w[j][...]) + dot(z[here, halves[1]], w[2 + j][...])
                for j in (0, 1)
            )
            c, sn = cosine[here], sine[here]
            a, b = in_order(x, own[:, :one], other[:, :one])
            q[here, :one] = (a * c - b * sn).astype(bf16)
            q[here, one:] = (b * c + a * sn).astype(bf16)
            a, b = in_order(x, own[:, one:dk], other[:, one:dk])
            k[here, :one] = ((a * c - b * sn) * dk**-0.5).astype(bf16)
            k[here, one:] = ((b * c + a * sn) * dk**-0.5).astype(bf16)
            v[here, :half] = own[:, dk:middle].astype(bf16)
            v[here, half:] = other[:, dk:middle].astype(bf16)
            g[here, :half] = own[:, middle:]
            g[here, half:] = other[:, middle:]
        for i in (1, 2, 3, 4):
            push(i)
        ready(16, 17)
        for i in tiles:
            here = rows_of(i)
            scores = (dot(q[here], k[...], 1, 1) * decay[here]).astype(bf16)
            p[here] = scores
            value = dot(scores, v[...])
            retained[here] = value
            normed, _ = head_norm(value)
            gate = g[here]
            part = (normed * gate / (1.0 + jnp.exp(-gate))).astype(bf16)
            mixed[here] = part
            own, other = of_x(w_out, x, half)
            put_tile(outs, i, dot(part[:, :half], own) + dot(part[:, half:], other))
        for i in (9, 10, 8, 5, 6, 7):
            push(i)

    def join_tiles(*refs):
        for i in tiles:
            refs[9][rows_of(i)] = tile(refs, i)

    def feed(which, count):
        def body(s, *refs):
            pieces, cots, w_down, w = (
                refs[:count], refs[count : 2 * count], refs[2 * count],
                refs[2 * count + 1 : 2 * count + 5],
            )
            (z, hidden, grad), outs = refs[2 * count + 5 : 2 * count + 8], refs[2 * count + 8 :]
            half = ff // 2
            for i in which:
                here = rows_of(i - which[0])
                part, cot = (
                    tile(p, i) if count > 3 else jnp.concatenate([r[...] for r in p], 0)
                    for p in (pieces, cots)
                )
                z[here] = part
                downs = of_x(w_down, s[1], half)
                for j in (0, 1):
                    ab = dot(part[:, halves[0]], w[j][...]) + dot(part[:, halves[1]], w[2 + j][...])
                    a, b = ab[:, :half], ab[:, half:]
                    below = 0.5 * (1.0 + lax.erf(a * math.sqrt(0.5)))
                    gelu = a * below
                    slope = below + a * jnp.exp(-0.5 * a * a) * (1.0 / math.sqrt(2.0 * math.pi))
                    columns = slice(j * half, (j + 1) * half)
                    hidden[here, columns] = (gelu * b).astype(bf16)
                    d = dot(cot, downs[j], 1, 1).astype(bf16).astype(f32)
                    both = jnp.concatenate([d * b * slope, d * gelu], -1).astype(bf16)
                    grad[j, here] = both
                for t in (0, 1):
                    back = dot(grad[0, here], w[2 * t][...], 1, 1)
                    back = back + dot(grad[1, here], w[2 * t + 1][...], 1, 1)
                    put_tile(outs, i, back, which[0], t)

        return body

    def feed_shapes(which):
        count = 2 * rows * len(which)
        return [
            shape((count, width), bf16), shape((count, ff), bf16), shape((2, count, ff), bf16)
        ] + term_shapes(rows, width, which)

    def down(s, h, last_h, w, *outs):
        half = ff // 2
        for i in tiles:
            here = h[rows_of(i)] if i < 3 else last_h[...]
            own, other = of_x(w, s[1], half)
            put_tile(outs, i, dot(here[:, :half], own) + dot(here[:, half:], other))

    def mixer_back(s, *refs, ready, push):
        pieces, (w_out, r, g, mixed, q, k, v, p, decay, cosine, sine), w, z = (
            refs[:9], refs[9:20], refs[20:24], refs[24]
        )
        kept, given, sums, d_pre, *outs = refs[25:32]
        d_out, d_r, d_k, d_v, room = refs[32:]
        one, half = dk // 2, dv // 2
        cut = dk + half
        x = s[1]
        for i in tiles:
            here = rows_of(i)
            part = tile(pieces, i)
            d_out[here] = part
            own, other = of_x(w_out, x, half)
            d_mixed = jnp.concatenate([dot(part, own, 1, 1), dot(part, other, 1, 1)], -1)
            d_mixed = d_mixed.astype(bf16).astype(f32)
            normed, scale = head_norm(r[here])
            gate = g[here]
            sigmoid = 1.0 / (1.0 + jnp.exp(-gate))
            both = (d_mixed * normed * sigmoid * (1.0 + gate * (1.0 - sigmoid))).astype(bf16)
            d_pre[0, here, cut:], d_pre[1, here, cut:] = both[:, :half], both[:, half:]
            d_r[here] = normalize_back(normed, scale, d_mixed * gate * sigmoid).astype(bf16)
        ready(12)
        rows_products(s, [mixed], d_out, kept, given)
        push(0)
        push(1)
        ready(13, 14, 15, 16, 17, 18, 19)
        for i in tiles:
            here = rows_of(i)
            scores = (dot(d_r[here], v[...], 1, 1) * decay[here]).astype(bf16)
            c, sn = cosine[here], sine[here]
            grad = dot(scores, k[...])
            a, b = grad[:, :one], grad[:, one:]
            own, other = in_order(x, a * c + b * sn, b * c - a * sn)
            d_pre[0, here, :one] = own.astype(bf16)
            d_pre[1, here, :one] = other.astype(bf16)
            more_k, more_v = dot(scores, q[here], 0, 0), dot(p[here], d_r[here], 0, 0)
            if i == 0:
                d_k[...], d_v[...] = more_k, more_v
            else:
                d_k[...] += more_k
                d_v[...] += more_v
        for i in tiles:
            here = rows_of(i)
            c, sn = cosine[here] * dk**-0.5, sine[here] * dk**-0.5
            a, b = d_k[here, :one], d_k[here, one:]
            own, other = in_order(x, a * c + b * sn, b * c - a * sn)
            d_pre[0, here, one:dk] = own.astype(bf16)
            d_pre[1, here, one:dk] = other.astype(bf16)
            d_pre[0, here, dk:cut] = d_v[here, :half].astype(bf16)
            d_pre[1, here, dk:cut] = d_v[here, half:].astype(bf16)
        push(3)
        ready(20, 21, 22, 23, 24)
        for i in tiles:
            here = rows_of(i)
            for t in (0, 1):
                back = dot(d_pre[0, here], w[2 * t][...], 1, 1)
                back = back + dot(d_pre[1, here], w[2 * t + 1][...], 1, 1)
                put_tile(outs, i, back, part=t)
                parts = jnp.concatenate(
                    [
                        jnp.sum(back * z[here, halves[t]].astype(f32), axis=0, keepdims=True),
                        jnp.sum(back, axis=0, keepdims=True),
                    ],
                    0,
                )
                if i == 0:
                    room[:, halves[t]] = parts
                else:
                    room[:, halves[t]] += parts
        for i in (5, 6, 4):
            push(i)
        for start, columns in arranged(s):
            sums[:, columns] = room[:, start : start + half_depth]

    terms = term_shapes(rows, width)


    packed, tokens_late, ffn_gate_late, ffn_up_late, *gains_late = after(
        fetch(w_query, w_key, w_value, w_gate), tokens, w_ffn_gate, w_ffn_up,
        norm1_gain, norm1_bias, norm2_gain, norm2_bias,
    )
    gains_late = jnp.stack(gains_late)
    mix_own = trade(packed)
    ring = Gather(tokens_late)

    head = lax.axis_index("fsdp")
    gamma_log = jnp.log(1.0 - 2.0 ** (-5.0 - head.astype(f32)))
    positions = (owners() * rows)[:, None] + jnp.arange(rows, dtype=jnp.int32)[None, :]
    positions = positions.reshape(-1).astype(f32)
    half = dk // 2
    freqs = jnp.exp(-jnp.arange(half, dtype=f32) * (math.log(10000.0) / half))
    angles = positions[:, None] * freqs[None, :]
    cosine, sine = jnp.cos(angles), jnp.sin(angles)
    differ = positions[:, None] - positions[None, :]
    decay = jnp.where(differ >= 0, jnp.exp(jnp.maximum(differ, 0.0) * gamma_log), 0.0)

    def widen(value, place):
        other = swap(value, place)
        first = bit(place) == 0
        return jnp.concatenate([jnp.where(first, value, other), jnp.where(first, other, value)], 1)

    cosine, sine, decay, ffn_packed, mix_own, gains = ring.step(
        cosine, sine, decay, fetch(ffn_gate_late, ffn_up_late), mix_own, widen(gains_late, 0)
    )
    mix_other = swap(mix_own, X)
    mix_own_c = swap(mix_own, CORE)
    (gains,) = ring.step(widen(gains, 1))
    (gains,) = ring.step(widen(gains, 2))
    gains = gains.astype(f32)

    mix_other, mix_own_c, ffn_packed = ring.step(mix_other, mix_own_c, ffn_packed)
    mix_other_c = swap(mix_other, CORE)
    w_mix = (mix_own, mix_other, mix_own_c, mix_other_c)
    ffn_own = trade(ffn_packed)
    z_first, query, key, value, gate, scores, retained, mixed, *parts = streamed(
        mixer,
        [shape((every, width), bf16)]
        + [shape((every, dk), bf16)] * 2
        + [shape((every, dv), bf16), shape((every, dv), f32), shape((every, every), bf16)]
        + [shape((every, dv), f32), shape((every, dv), bf16)]
        + terms,
        *ring.pieces(), gains, *w_mix, cosine, sine, decay, w_out,
        scalars=where, limit=LIMITS[0], late=range(10, 18), stream=range(11),
        scratch=[pltpu.VMEM((2 * rows, width), f32)],
    )
    *parts, cot_late = after(*parts, cotangent)
    ring = Pair(parts)
    cot_ring = Gather(cot_late)
    ring.step(0)
    ring.a[0], ffn_own = after(ring.a[0], ffn_own)
    ffn_other = swap(ffn_own, X)
    ffn_own_c = swap(ffn_own, CORE)
    ring.step(1)
    for _ in range(3):
        ring.step(0)
        ring.step(1)
        cot_ring.step()
    resid, second = kernel(
        second_norm, [block_f32, block_bf16], *ring.pieces(), tokens, gains,
        scalars=where, scratch=room_of_block, limit=8,
    )

    ring = Gather(second)
    (ffn_other,) = ring.step(ffn_other)
    ffn_other_c = swap(ffn_other, CORE)
    ring.step()
    w_ffn = ring.step(ffn_own, ffn_other, ffn_own_c, ffn_other_c)
    early = (ring.own, *ring.ahead[1:4], *ring.behind[1:3])
    early_cots = (cot_ring.own, *cot_ring.ahead[1:4], *cot_ring.behind[1:3])
    done = kernel(
        feed((0, 1, 2), 6), feed_shapes((0, 1, 2)),
        *early, *early_cots, w_ffn_down, *w_ffn,
        scalars=where, limit=LIMITS[2],
    )
    a, b, *done = after(*cot_ring.peek(), *done)
    cot_ring.put(a, b)
    done = ring.step(*done)
    z_second, hidden, d_ab, terms_early = done
    z_last, hidden_last, d_ab_last, *parts = kernel(
        feed((3,), 3), feed_shapes((3,)),
        ring.behind[3], ring.ahead[4], ring.behind[4],
        cot_ring.behind[3], cot_ring.ahead[4], cot_ring.behind[4], w_ffn_down, *w_ffn,
        scalars=where, limit=18,
    )
    ring = Scatter([terms_early, *parts])
    (cot_all,) = ring.step(
        *kernel(join_tiles, [shape((every, width), bf16)], *cot_ring.pieces(), limit=24)
    )
    grad_ffn = ring.step(*columns_grad([z_second, z_last], [d_ab, d_ab_last]))
    ffn_own, ffn_own_c, ffn_given = sum_cores(*grad_ffn)
    ffn_own, ffn_own_c, ffn_given, down_kept, down_given = ring.step(
        ffn_own, ffn_own_c, ffn_given, *rows_grad([hidden, hidden_last], cot_all)
    )
    ffn_sent = swap(ffn_given, X)
    (down_sum,) = ring.step(sum_cores_rows(down_kept, down_given))
    grad_resid, second_sums, part = kernel(
        second_back, [block_f32, pair_f32, block_bf16],
        *ring.pieces(), resid, cotangent, gains,
        scalars=where, scratch=room_of_block,
    )
    ring = Gather(part)
    ffn_own, ffn_sent, down_sum = ring.step(ffn_own, ffn_sent, down_sum)
    down_got = swap(down_sum, X)
    ffn_sum = sum_x(ffn_own, ffn_own_c, ffn_sent)
    ring.step()
    last = Scatter(kernel(down, terms, hidden, hidden_last, w_ffn_down, scalars=where, limit=20))
    ring.step()
    a, b, down_got, ffn_sum = ring.step(*last.peek(), down_got, ffn_sum)
    last.put(a, b)

    ffn_owned = give(ffn_sum)
    out_kept, out_given, first_sums, d_pre, *parts = streamed(
        mixer_back,
        [shape((2, dv // 4, width), bf16)] * 2
        + [pair_f32, shape((2, every, dk + dv), bf16)]
        + terms,
        *ring.pieces(), w_out, retained, gate, mixed,
        query, key, value, scores, decay, cosine, sine, *w_mix, z_first,
        scalars=where, limit=LIMITS[4], late=range(12, 25), stream=(0, 1, 3, 4, 5, 6),
        scratch=[
            pltpu.VMEM((every, width), bf16),
            pltpu.VMEM((every, dv), bf16),
            pltpu.VMEM((every, dk), f32),
            pltpu.VMEM((every, dv), f32),
            pltpu.VMEM((2, width), f32),
        ],
    )
    out_kept, out_given, first_sums, d_pre, ffn_owned, *parts = after(
        out_kept, out_given, first_sums, d_pre, ffn_owned, *parts
    )
    ring = Scatter(parts)
    stack = jnp.concatenate([first_sums, second_sums])
    mix_own, mix_own_c, mix_given = sum_cores(*columns_grad([z_first], [d_pre]))
    out_sum = sum_cores_rows(out_kept, out_given)
    mix_own, mix_own_c, mix_given, out_sum, stack_c = ring.step(
        mix_own, mix_own_c, mix_given, out_sum, swap(stack, X)
    )
    stack = stack + stack_c
    for place in range(X + 1, bits()):
        stack = stack + swap(stack, place)
    mix_sent = swap(mix_given, X)
    (stack_c,) = ring.step(swap(stack, CORE))
    stack = stack + stack_c
    (stack_c,) = ring.step(swap(stack, 0))
    stack = stack + stack_c
    mix_sent, stack_c, out_sum = ring.step(mix_sent, swap(stack, 1), out_sum)
    stack = stack + stack_c
    mix_owned = give(sum_x(mix_own, mix_own_c, mix_sent))
    out_got, ffn_other = swap(out_sum, X), swap(ffn_owned, X)
    grad_tokens = kernel(
        first_back, [block_f32], *ring.pieces(), tokens, grad_resid, gains,
        scalars=where, scratch=room_of_block,
    )[0]
    grad_down = flat_rows(sum_x_rows(down_sum, down_got))
    a, b, mix_owned, ffn_other, out_got, grad_tokens, grad_down = after(
        *last.peek(), mix_owned, ffn_other, out_got, grad_tokens, grad_down
    )
    last.put(a, b)
    mix_other = swap(mix_owned, X)
    grad_ffn_gate, grad_ffn_up = flat(everywhere(ffn_owned, ffn_other), [ff, ff])
    grad_out = flat_rows(sum_x_rows(out_sum, out_got))
    grad_ffn_gate, grad_ffn_up, grad_out, stack_c = last.step(
        grad_ffn_gate, grad_ffn_up, grad_out, swap(stack, 2)
    )
    stack = lax.dynamic_slice_in_dim(stack + stack_c, head * depth, depth, 1)
    first_gain = (stack[0] - norm1_bias.astype(f32) * stack[1]) / norm1_gain.astype(f32)
    last.step()
    (output,) = kernel(last_sum, [block_bf16], *last.pieces(), resid)
    mix_other, first_gain = after(mix_other, first_gain)
    grad_query, grad_key, grad_value, grad_gate = flat(
        everywhere(mix_owned, mix_other), [dk, dk, dv, dv]
    )

    return (
        output,
        grad_tokens,
        grad_query,
        grad_key,
        grad_value,
        grad_gate,
        grad_out,
        first_gain,
        stack[1],
        grad_ffn_gate,
        grad_ffn_up,
        grad_down,
        stack[2],
        stack[3],
    )


def solution(mesh):
    tokens = P(("rep", "fsdp"), None)
    matrix = P("fsdp", None)
    vector = P("fsdp")
    in_specs = (tokens,) + (matrix,) * 5 + (vector,) * 2 + (matrix,) * 3 + (vector,) * 2 + (tokens,)
    out_specs = (tokens,) * 2 + (matrix,) * 5 + (vector,) * 2 + (matrix,) * 3 + (vector,) * 2
    return jax.shard_map(
        on_device, mesh=mesh, in_specs=in_specs, out_specs=out_specs, check_vma=False
    )
```
